32 devices in a mesh: group: 2 (over y), tensor: 16 (over z, x, core).
Axes of the slice: x: 2, y: 2, z: 4, core: 2. Of those that a mesh axis runs over, the one named last changes fastest.
Arguments:
- tokens: bfloat16 [64, 8192], P(('group', 'tensor')), parts along dimension 0, may hold values from -6 to 6
- gate_weight: bfloat16 [8192, 28672], P(None, 'tensor'), may hold values from -0.0625 to 0.0625
- up_weight: bfloat16 [8192, 28672], P(None, 'tensor'), may hold values from -0.0625 to 0.0625
- a_gate: float32 [16384, 1024], P(('group', 'tensor')), parts along dimension 0, may hold values from -0.0625 to 0.0625
- a_up: float32 [16384, 1024], P(('group', 'tensor')), parts along dimension 0, may hold values from -0.0625 to 0.0625
- b_gate: float32 [2048, 28672], P('group', 'tensor'), parts along dimension 0, may hold values from -0.75 to 0.75
- b_up: float32 [2048, 28672], P('group', 'tensor'), parts along dimension 0, may hold values from -0.75 to 0.75
- agent: int32 [64], P('group'), parts along dimension 0, may hold values from 0 to 15
- d_hidden: bfloat16 [64, 28672], P('group', 'tensor'), parts along dimension 0, may hold values from -6 to 6
Outputs:
- token_gradient: bfloat16 [64, 8192], P(('group', 'tensor')), parts along dimension 0
- gate_down_gradient: float32 [16384, 1024], P(('group', 'tensor')), parts along dimension 0
- up_down_gradient: float32 [16384, 1024], P(('group', 'tensor')), parts along dimension 0
- gate_lift_gradient: float32 [2048, 28672], P('group', 'tensor'), parts along dimension 0
- up_lift_gradient: float32 [2048, 28672], P('group', 'tensor'), parts along dimension 0
The draws below stay inside these ranges and needn't reach their ends.
There are 2 independent parts, one for each index of `group`. The reference program is written for one: setup_inputs(seed, part) draws one part's arguments, and reference() takes and returns one part's arrays. A program takes and returns all parts, laid end to end along the dimension named above; an argument that names none is the same for every part. Nothing has to cross between parts.
All inputs are finite; a program needn't handle non-finite values.
Results may differ from the reference program's by a relative error of at most 0.009.
Values may be sent and summed in bfloat16 or wider, within the bound.
No kernel may reach another device: no remote copies, remote signals or barrier semaphores. Data moves between devices by JAX's collectives and lax.ppermute only.
A program may use at most 192 MiB of HBM per device.

```python
import jax
import jax.numpy as jnp

D = 8192
FF = 28672
R = 64
AG = 16
TOKENS = 32


def touch_ends(values, rng, low, largest):
    longest = values.shape.index(max(values.shape))
    spots = []
    for shift in (0, 1):
        where = [jax.random.randint(jax.random.fold_in(rng, axis), (), 0, length) for axis, length in enumerate(values.shape)]
        where[longest] = (where[longest] + shift) % values.shape[longest]
        spots.append(tuple(where))
    return values.at[spots[0]].set(low).at[spots[1]].set(largest)


def level_of(key, extent, shards, low, high):
    def one(position, blocks):
        steps = jax.random.uniform(jax.random.fold_in(jax.random.fold_in(key, 6), position), (blocks,), jnp.float32, low / len(shards), high / len(shards))
        return jnp.repeat(jnp.exp(steps), extent[position] // blocks).reshape((-1,) + (1,) * (len(extent) - position - 1))

    gain = one(*shards[0])
    for cut in shards[1:]:
        gain = gain * one(*cut)
    return gain


def scatter_about(key, shape, spread, reach, shards=(), kind=jnp.bfloat16):
    factor_of = level_of(key, shape, shards, -0.22, 0.18) if shards else 1.0
    drawn = jax.random.normal(key, shape, jnp.float32) * spread * factor_of
    return jnp.minimum(jnp.maximum(drawn, -reach), reach).astype(kind)


def setup_inputs(seed: int = 0, part: int = 0) -> dict:
    key_list = jax.random.split(jax.random.key(seed), 10)
    part_splits = jax.random.split(jax.random.fold_in(key_list[9], part), 10)
    tokens = scatter_about(part_splits[0], (TOKENS, D), 1.0, 6.0, ((0, 16),))
    gate_weight = scatter_about(key_list[1], (D, FF), D ** -0.5, 0.0625, ((1, 16),))
    up_weight = scatter_about(key_list[2], (D, FF), D ** -0.5, 0.0625, ((1, 16),))
    a_gate = scatter_about(part_splits[3], (D, AG * R), D ** -0.5, 0.0625, ((0, 16),), jnp.float32)
    a_up = scatter_about(part_splits[4], (D, AG * R), D ** -0.5, 0.0625, ((0, 16),), jnp.float32)
    b_gate = scatter_about(part_splits[5], (AG * R, FF), R ** -0.5, 0.75, ((1, 16),), jnp.float32)
    b_up = scatter_about(part_splits[6], (AG * R, FF), R ** -0.5, 0.75, ((1, 16),), jnp.float32)
    agent = touch_ends(jax.random.randint(part_splits[7], (TOKENS,), 0, AG), jax.random.fold_in(part_splits[7], 1), 0, AG - 1).astype(jnp.int32)
    d_hidden = scatter_about(part_splits[8], (TOKENS, FF), 1.0, 6.0, ((1, 16),))
    return {"tokens": tokens, "gate_weight": gate_weight, "up_weight": up_weight, "a_gate": a_gate, "a_up": a_up, "b_gate": b_gate, "b_up": b_up, "agent": agent, "d_hidden": d_hidden}


adapter_scale = 2.0


def agent_mask(agent):
    onehot = (agent[:, None] == jnp.arange(AG, dtype=jnp.int32)[None, :]).astype(jnp.float32)
    return onehot


def select_rank(values, onehot):
    shaped = values.reshape(values.shape[0], AG, R)
    return jnp.sum(shaped * onehot[:, :, None], axis=1)


def spread_rank(small, onehot):
    wide = onehot[:, :, None] * small.astype(jnp.float32)[:, None, :]
    return wide.reshape(small.shape[0], AG * R).astype(jnp.bfloat16)


def reference(tokens, gate_weight, up_weight, a_gate, a_up, b_gate, b_up, agent, d_hidden):
    onehot = agent_mask(agent)
    agent_gate_down = a_gate.astype(jnp.bfloat16)
    agent_up_down = a_up.astype(jnp.bfloat16)
    agent_gate_lift = b_gate.astype(jnp.bfloat16)
    agent_up_lift = b_up.astype(jnp.bfloat16)
    u_gate = select_rank(jnp.dot(tokens, agent_gate_down, preferred_element_type=jnp.float32), onehot)
    u_up = select_rank(jnp.dot(tokens, agent_up_down, preferred_element_type=jnp.float32), onehot)
    up_factor_gate = spread_rank(u_gate.astype(jnp.bfloat16), onehot)
    up_factor_up = spread_rank(u_up.astype(jnp.bfloat16), onehot)
    gate_values = jnp.dot(tokens, gate_weight, preferred_element_type=jnp.float32) + adapter_scale * jnp.dot(up_factor_gate, agent_gate_lift, preferred_element_type=jnp.float32)
    up_values = jnp.dot(tokens, up_weight, preferred_element_type=jnp.float32) + adapter_scale * jnp.dot(up_factor_up, agent_up_lift, preferred_element_type=jnp.float32)
    sig = jax.nn.sigmoid(gate_values)
    dh = d_hidden.astype(jnp.float32)
    gate_gradient = (dh * up_values * sig * (1.0 + gate_values * (1.0 - sig))).astype(jnp.bfloat16)
    up_gradient = (dh * gate_values * sig).astype(jnp.bfloat16)
    g_gate = select_rank(jnp.dot(gate_gradient, agent_gate_lift.T, preferred_element_type=jnp.float32), onehot)
    g_up = select_rank(jnp.dot(up_gradient, agent_up_lift.T, preferred_element_type=jnp.float32), onehot)
    gate_factor_gate = spread_rank(g_gate.astype(jnp.bfloat16), onehot)
    gate_factor_up = spread_rank(g_up.astype(jnp.bfloat16), onehot)
    token_gradient = jnp.dot(gate_gradient, gate_weight.T, preferred_element_type=jnp.float32) + jnp.dot(up_gradient, up_weight.T, preferred_element_type=jnp.float32)
    token_gradient = token_gradient + adapter_scale * (jnp.dot(gate_factor_gate, agent_gate_down.T, preferred_element_type=jnp.float32) + jnp.dot(gate_factor_up, agent_up_down.T, preferred_element_type=jnp.float32))
    gate_down_gradient = adapter_scale * jnp.dot(tokens.T, gate_factor_gate, preferred_element_type=jnp.float32)
    up_down_gradient = adapter_scale * jnp.dot(tokens.T, gate_factor_up, preferred_element_type=jnp.float32)
    gate_lift_gradient = adapter_scale * jnp.dot(up_factor_gate.T, gate_gradient, preferred_element_type=jnp.float32)
    up_lift_gradient = adapter_scale * jnp.dot(up_factor_up.T, up_gradient, preferred_element_type=jnp.float32)
    return token_gradient.astype(jnp.bfloat16), gate_down_gradient, up_down_gradient, gate_lift_gradient, up_lift_gradient
```

```python
import jax
import jax.numpy as jnp
from jax import lax
from jax.experimental import pallas as pl
from jax.experimental.pallas import tpu as pltpu
from jax.sharding import PartitionSpec as P

R = 64
AG = 16

adapter_scale = 2.0
BF16 = jnp.bfloat16
F32 = jnp.float32


def agent_mask(agent):
    return (agent[:, None] == jnp.arange(AG, dtype=jnp.int32)[None, :]).astype(jnp.float32)


def select_rank(values, onehot):
    shaped = values.reshape(values.shape[0], AG, R)
    return jnp.sum(shaped * onehot[:, :, None], axis=1)


def spread_rank(small, onehot):
    wide = onehot[:, :, None] * small.astype(jnp.float32)[:, None, :]
    return wide.reshape(small.shape[0], AG * R).astype(jnp.bfloat16)


def flipped_product(left, weight):
    return lax.dot_general(
        left, weight, (((1,), (1,)), ((), ())), preferred_element_type=jnp.float32
    )


def rows_product(left, right):
    return lax.dot_general(
        left, right, (((0,), (0,)), ((), ())), preferred_element_type=jnp.float32
    )


def plain_device(tokens, gate_weight, up_weight, a_gate, a_up, b_gate, b_up, agent, d_hidden):
    onehot = agent_mask(agent)
    feat_rows = a_gate.shape[0]
    feat_start = lax.axis_index("tensor") * feat_rows
    agent_gate_down = a_gate.astype(jnp.bfloat16)
    agent_up_down = a_up.astype(jnp.bfloat16)
    agent_gate_lift = b_gate.astype(jnp.bfloat16)
    agent_up_lift = b_up.astype(jnp.bfloat16)
    complete_result = lax.all_gather(tokens, "tensor", axis=0, tiled=True)
    own_cols = lax.dynamic_slice_in_dim(complete_result, feat_start, feat_rows, 1)
    part_gate = select_rank(
        jnp.dot(own_cols, agent_gate_down, preferred_element_type=jnp.float32), onehot
    )
    part_up = select_rank(
        jnp.dot(own_cols, agent_up_down, preferred_element_type=jnp.float32), onehot
    )
    u_gate, u_up = lax.psum((part_gate, part_up), "tensor")
    up_factor_gate = spread_rank(u_gate.astype(jnp.bfloat16), onehot)
    up_factor_up = spread_rank(u_up.astype(jnp.bfloat16), onehot)
    gate_values = jnp.dot(
        complete_result, gate_weight, preferred_element_type=jnp.float32
    ) + adapter_scale * jnp.dot(up_factor_gate, agent_gate_lift, preferred_element_type=jnp.float32)
    up_values = jnp.dot(
        complete_result, up_weight, preferred_element_type=jnp.float32
    ) + adapter_scale * jnp.dot(up_factor_up, agent_up_lift, preferred_element_type=jnp.float32)
    sig = jax.nn.sigmoid(gate_values)
    hidden_grad = d_hidden.astype(jnp.float32)
    gate_gradient = (hidden_grad * up_values * sig * (1.0 + gate_values * (1.0 - sig))).astype(
        jnp.bfloat16
    )
    up_gradient = (hidden_grad * gate_values * sig).astype(jnp.bfloat16)
    pg_gate = select_rank(flipped_product(gate_gradient, agent_gate_lift), onehot)
    pg_up = select_rank(flipped_product(up_gradient, agent_up_lift), onehot)
    g_gate, g_up = lax.psum((pg_gate, pg_up), "tensor")
    gate_factor_gate = spread_rank(g_gate.astype(jnp.bfloat16), onehot)
    gate_factor_up = spread_rank(g_up.astype(jnp.bfloat16), onehot)
    adapter_contribution = adapter_scale * (
        flipped_product(gate_factor_gate, agent_gate_down)
        + flipped_product(gate_factor_up, agent_up_down)
    )
    base_rows = flipped_product(gate_gradient, gate_weight) + flipped_product(
        up_gradient, up_weight
    )
    joined = lax.dynamic_slice_in_dim(base_rows, feat_start, feat_rows, 1) + adapter_contribution
    token_gradient = lax.psum_scatter(
        lax.dynamic_update_slice_in_dim(base_rows, joined, feat_start, 1),
        "tensor",
        scatter_dimension=0,
        tiled=True,
    ).astype(jnp.bfloat16)
    gate_down_gradient = adapter_scale * rows_product(own_cols, gate_factor_gate)
    up_down_gradient = adapter_scale * rows_product(own_cols, gate_factor_up)
    gate_lift_gradient = adapter_scale * rows_product(up_factor_gate, gate_gradient)
    up_lift_gradient = adapter_scale * rows_product(up_factor_up, up_gradient)
    return (
        token_gradient,
        gate_down_gradient,
        up_down_gradient,
        gate_lift_gradient,
        up_lift_gradient,
    )


def forward_kernel(side_ref, x_ref, wg_ref, wu_ref, g_ref, u_ref):
    @pl.when(pl.program_id(0) == 0)
    def _():
        g_ref[...] = jnp.zeros_like(g_ref)
        u_ref[...] = jnp.zeros_like(u_ref)

    x = x_ref[...]
    g_ref[...] += jnp.dot(x, wg_ref[...], preferred_element_type=F32)
    u_ref[...] += jnp.dot(x, wu_ref[...], preferred_element_type=F32)


def forward_products(side, x, gate_weight, up_weight, half, depth=1024):
    rows, d = x.shape
    weight_block = pl.BlockSpec((depth, half), lambda k, s: (k, s[0]))
    out_block = pl.BlockSpec((rows, half), lambda k, s: (0, 0))
    return pl.pallas_call(
        forward_kernel,
        grid_spec=pltpu.PrefetchScalarGridSpec(
            num_scalar_prefetch=1,
            grid=(d // depth,),
            in_specs=[pl.BlockSpec((rows, depth), lambda k, s: (0, k)), weight_block, weight_block],
            out_specs=[out_block, out_block],
        ),
        out_shape=[jax.ShapeDtypeStruct((rows, half), F32)] * 2,
        compiler_params=pltpu.CompilerParams(vmem_limit_bytes=20 << 20),
        cost_estimate=pl.CostEstimate(
            flops=4 * rows * d * half, bytes_accessed=4 * d * half, transcendentals=0
        ),
        name="forward_products",
    )(side, x, gate_weight, up_weight)


def backward_kernel(side_ref, dg_ref, du_ref, wg_ref, wu_ref, out_ref):
    total = flipped_product(dg_ref[...], wg_ref[...]) + flipped_product(du_ref[...], wu_ref[...])
    out_ref[...] = total.astype(out_ref.dtype)


def backward_products(side, dg, du, gate_weight, up_weight, first, count, depth=1024):
    rows, half = dg.shape
    start = first // depth
    weight_block = pl.BlockSpec((depth, half), lambda k, s: (k + start, s[0]))
    left_block = pl.BlockSpec((rows, half), lambda k, s: (0, 0))
    return pl.pallas_call(
        backward_kernel,
        grid_spec=pltpu.PrefetchScalarGridSpec(
            num_scalar_prefetch=1,
            grid=(count // depth,),
            in_specs=[left_block, left_block, weight_block, weight_block],
            out_specs=pl.BlockSpec((rows, depth), lambda k, s: (0, k)),
        ),
        out_shape=jax.ShapeDtypeStruct((rows, count), F32),
        compiler_params=pltpu.CompilerParams(vmem_limit_bytes=24 << 20),
        cost_estimate=pl.CostEstimate(
            flops=4 * rows * count * half, bytes_accessed=4 * count * half, transcendentals=0
        ),
        name="backward_products",
    )(side, dg, du, gate_weight, up_weight)


N = 16


def along_tensor(value, mask):
    return lax.ppermute(value, "tensor", [(i, i ^ mask) for i in range(N)])


def across_groups(value):
    return lax.ppermute(value, "group", [(0, 1), (1, 0)])


def sum_over_tensor(value):
    shape = value.shape
    v = value.reshape(2, 2, 4, 2, shape[1])
    v = v + along_tensor(v, 1)[::-1]
    v = v + along_tensor(v, 2)[:, ::-1]
    parts = [along_tensor(v, 4 * m) for m in (1, 2, 3)]
    total = v
    for m, part in zip((1, 2, 3), parts):
        total = total + jnp.stack([part[:, :, q ^ m] for q in range(4)], axis=2)
    return total.reshape(shape)


def split_device(tokens, gate_weight, up_weight, a_gate, a_up, b_gate, b_up, agent, d_hidden):
    group = lax.axis_index("group")
    t = lax.axis_index("tensor")
    side = group.astype(jnp.int32).reshape(1)
    d = tokens.shape[1]
    ff = b_gate.shape[1]
    half = ff // 2
    feat_rows = a_gate.shape[0]
    feat_start = t * feat_rows
    mine = group * half
    other = half - mine

    line = jnp.concatenate([tokens] + [along_tensor(tokens, 4 * m) for m in (1, 2, 3)], axis=0)
    both = jnp.stack([line, across_groups(line)])
    both = jnp.concatenate([both, along_tensor(both, 2)], axis=1)
    both = jnp.concatenate([both, along_tensor(both, 1)], axis=1)
    rows = both.shape[1]
    x = both.reshape(2 * rows, d)

    place = jnp.arange(rows, dtype=jnp.int32)
    block = ((place >> 1) & 3) * 4 + ((place >> 3) & 1) * 2 + (place >> 4)
    token_of = ((t ^ block) << 1) + (place & 1)
    shuffle = token_of[:, None] == jnp.arange(rows, dtype=jnp.int32)[None, :]
    agent_here = jnp.sum(jnp.where(shuffle, agent[None, :], 0), axis=1)
    onehot = agent_mask(agent_here)

    hidden_other = across_groups(lax.dynamic_slice_in_dim(d_hidden, other, half, 1))
    hidden_mine = lax.dynamic_slice_in_dim(d_hidden, mine, half, 1)
    hidden = jnp.dot(
        shuffle.astype(BF16),
        jnp.concatenate([hidden_mine, hidden_other], axis=1),
        preferred_element_type=F32,
    )
    hidden_grad = jnp.concatenate([hidden[:, :half], hidden[:, half:]], axis=0)

    agent_gate_down = a_gate.astype(BF16)
    agent_up_down = a_up.astype(BF16)
    agent_gate_lift = b_gate.astype(BF16)
    agent_up_lift = b_up.astype(BF16)

    own_cols = lax.dynamic_slice_in_dim(x[:rows], feat_start, feat_rows, 1)
    part_gate = select_rank(jnp.dot(own_cols, agent_gate_down, preferred_element_type=F32), onehot)
    part_up = select_rank(jnp.dot(own_cols, agent_up_down, preferred_element_type=F32), onehot)
    u = sum_over_tensor(jnp.concatenate([part_gate, part_up], axis=1)).astype(BF16)
    up_factor_gate = spread_rank(u[:, :R], onehot)
    up_factor_up = spread_rank(u[:, R:], onehot)

    base_gate, base_up = forward_products(side, x, gate_weight, up_weight, half)

    lifted = jnp.stack(
        [
            adapter_scale * jnp.dot(up_factor_gate, agent_gate_lift, preferred_element_type=F32),
            adapter_scale * jnp.dot(up_factor_up, agent_up_lift, preferred_element_type=F32),
        ]
    )
    lifted_other = across_groups(lax.dynamic_slice_in_dim(lifted, other, half, 2).astype(BF16))
    lifted_mine = lax.dynamic_slice_in_dim(lifted, mine, half, 2)
    gate_values = base_gate + jnp.concatenate([lifted_mine[0], lifted_other[0].astype(F32)], axis=0)
    up_values = base_up + jnp.concatenate([lifted_mine[1], lifted_other[1].astype(F32)], axis=0)

    sig = jax.nn.sigmoid(gate_values)
    gate_gradient = (hidden_grad * up_values * sig * (1.0 + gate_values * (1.0 - sig))).astype(BF16)
    up_gradient = (hidden_grad * gate_values * sig).astype(BF16)

    swapped = across_groups(jnp.stack([gate_gradient[rows:], up_gradient[rows:]]))
    own = jnp.stack([gate_gradient[:rows], up_gradient[:rows]])
    first = group == 0
    whole = jnp.concatenate(
        [jnp.where(first, own, swapped), jnp.where(first, swapped, own)], axis=2
    )

    def core_first(v):
        q = rows // 2
        return jnp.concatenate([v[:q], v[rows : rows + q], v[q:rows], v[rows + q :]], axis=0)

    dg, du = core_first(gate_gradient), core_first(up_gradient)
    chunks = 2
    count = d // chunks
    pieces = []
    for c in range(chunks):
        grad = backward_products(side, dg, du, gate_weight, up_weight, c * count, count)
        grad = grad[:rows] + along_tensor(grad[rows:].astype(BF16), 1).astype(F32)
        grad = grad[: rows // 2] + across_groups(grad[rows // 2 :].astype(BF16)).astype(F32)
        grad = grad[: rows // 4] + along_tensor(grad[rows // 4 :].astype(BF16), 2).astype(F32)
        total = grad[:2]
        for m in (1, 2, 3):
            total = total + along_tensor(grad[2 * m : 2 * m + 2].astype(BF16), 4 * m).astype(F32)
        pieces.append(total)

    pg_gate = select_rank(flipped_product(whole[0], agent_gate_lift), onehot)
    pg_up = select_rank(flipped_product(whole[1], agent_up_lift), onehot)
    g = sum_over_tensor(jnp.concatenate([pg_gate, pg_up], axis=1)).astype(BF16)
    gate_factor_gate = spread_rank(g[:, :R], onehot)
    gate_factor_up = spread_rank(g[:, R:], onehot)
    adapter_contribution = adapter_scale * (
        flipped_product(gate_factor_gate, agent_gate_down)
        + flipped_product(gate_factor_up, agent_up_down)
    )
    move = adapter_contribution.astype(BF16).reshape(2, 2, 4, 2, feat_rows)
    move = jnp.stack([move[0], along_tensor(move[1], 1)])
    move = jnp.stack([move[:, 0], along_tensor(move[:, 1], 2)])
    move = jnp.stack([move[:, :, 0]] + [along_tensor(move[:, :, m], 4 * m) for m in (1, 2, 3)])
    move = move.reshape(N, 2 * feat_rows)
    source = jnp.arange(N, dtype=jnp.int32)
    sort = (source[:, None] == (t ^ source)[None, :]).astype(BF16)
    sorted_rows = jnp.dot(sort, move, preferred_element_type=F32).reshape(N, 2, feat_rows)
    contribution = sorted_rows.transpose(1, 0, 2).reshape(2, d)
    token_gradient = (jnp.concatenate(pieces, axis=1) + contribution).astype(BF16)

    gate_down_gradient = adapter_scale * rows_product(own_cols, gate_factor_gate)
    up_down_gradient = adapter_scale * rows_product(own_cols, gate_factor_up)
    gate_lift_gradient = adapter_scale * rows_product(up_factor_gate, whole[0])
    up_lift_gradient = adapter_scale * rows_product(up_factor_up, whole[1])
    return (
        token_gradient,
        gate_down_gradient,
        up_down_gradient,
        gate_lift_gradient,
        up_lift_gradient,
    )


def solution(mesh):
    sizes = dict(mesh.shape)

    def per_device(*args):
        tokens, b_gate = args[0], args[5]
        fits = (
            sizes["group"] == 2
            and sizes["tensor"] == N
            and tokens.shape[0] == 2
            and b_gate.shape[1] % 256 == 0
            and tokens.shape[1] % 2048 == 0
        )
        return (split_device if fits else plain_device)(*args)

    in_specs = (
        P(("group", "tensor"), None),
        P(None, "tensor"),
        P(None, "tensor"),
        P(("group", "tensor"), None),
        P(("group", "tensor"), None),
        P("group", "tensor"),
        P("group", "tensor"),
        P("group"),
        P("group", "tensor"),
    )
    out_specs = (
        P(("group", "tensor"), None),
        P(("group", "tensor"), None),
        P(("group", "tensor"), None),
        P("group", "tensor"),
        P("group", "tensor"),
    )
    return jax.shard_map(
        per_device, mesh=mesh, in_specs=in_specs, out_specs=out_specs, check_vma=False
    )
```

```python
import jax
import jax.numpy as jnp
from jax import lax
from jax.experimental import pallas as pl
from jax.experimental.pallas import tpu as pltpu
from jax.sharding import PartitionSpec as P

R = 64
AG = 16

adapter_scale = 2.0
BF16 = jnp.bfloat16
F32 = jnp.float32


def agent_mask(agent):
    return (agent[:, None] == jnp.arange(AG, dtype=jnp.int32)[None, :]).astype(jnp.float32)


def select_rank(values, onehot):
    shaped = values.reshape(values.shape[0], AG, R)
    return jnp.sum(shaped * onehot[:, :, None], axis=1)


def spread_rank(small, onehot):
    wide = onehot[:, :, None] * small.astype(jnp.float32)[:, None, :]
    return wide.reshape(small.shape[0], AG * R).astype(jnp.bfloat16)


def flipped_product(left, weight):
    return lax.dot_general(
        left, weight, (((1,), (1,)), ((), ())), preferred_element_type=jnp.float32
    )


def rows_product(left, right):
    return lax.dot_general(
        left, right, (((0,), (0,)), ((), ())), preferred_element_type=jnp.float32
    )


def plain_device(tokens, gate_weight, up_weight, a_gate, a_up, b_gate, b_up, agent, d_hidden):
    onehot = agent_mask(agent)
    feat_rows = a_gate.shape[0]
    feat_start = lax.axis_index("tensor") * feat_rows
    agent_gate_down = a_gate.astype(jnp.bfloat16)
    agent_up_down = a_up.astype(jnp.bfloat16)
    agent_gate_lift = b_gate.astype(jnp.bfloat16)
    agent_up_lift = b_up.astype(jnp.bfloat16)
    complete_result = lax.all_gather(tokens, "tensor", axis=0, tiled=True)
    own_cols = lax.dynamic_slice_in_dim(complete_result, feat_start, feat_rows, 1)
    part_gate = select_rank(
        jnp.dot(own_cols, agent_gate_down, preferred_element_type=jnp.float32), onehot
    )
    part_up = select_rank(
        jnp.dot(own_cols, agent_up_down, preferred_element_type=jnp.float32), onehot
    )
    u_gate, u_up = lax.psum((part_gate, part_up), "tensor")
    up_factor_gate = spread_rank(u_gate.astype(jnp.bfloat16), onehot)
    up_factor_up = spread_rank(u_up.astype(jnp.bfloat16), onehot)
    gate_values = jnp.dot(
        complete_result, gate_weight, preferred_element_type=jnp.float32
    ) + adapter_scale * jnp.dot(up_factor_gate, agent_gate_lift, preferred_element_type=jnp.float32)
    up_values = jnp.dot(
        complete_result, up_weight, preferred_element_type=jnp.float32
    ) + adapter_scale * jnp.dot(up_factor_up, agent_up_lift, preferred_element_type=jnp.float32)
    sig = jax.nn.sigmoid(gate_values)
    hidden_grad = d_hidden.astype(jnp.float32)
    gate_gradient = (hidden_grad * up_values * sig * (1.0 + gate_values * (1.0 - sig))).astype(
        jnp.bfloat16
    )
    up_gradient = (hidden_grad * gate_values * sig).astype(jnp.bfloat16)
    pg_gate = select_rank(flipped_product(gate_gradient, agent_gate_lift), onehot)
    pg_up = select_rank(flipped_product(up_gradient, agent_up_lift), onehot)
    g_gate, g_up = lax.psum((pg_gate, pg_up), "tensor")
    gate_factor_gate = spread_rank(g_gate.astype(jnp.bfloat16), onehot)
    gate_factor_up = spread_rank(g_up.astype(jnp.bfloat16), onehot)
    adapter_contribution = adapter_scale * (
        flipped_product(gate_factor_gate, agent_gate_down)
        + flipped_product(gate_factor_up, agent_up_down)
    )
    base_rows = flipped_product(gate_gradient, gate_weight) + flipped_product(
        up_gradient, up_weight
    )
    joined = lax.dynamic_slice_in_dim(base_rows, feat_start, feat_rows, 1) + adapter_contribution
    token_gradient = lax.psum_scatter(
        lax.dynamic_update_slice_in_dim(base_rows, joined, feat_start, 1),
        "tensor",
        scatter_dimension=0,
        tiled=True,
    ).astype(jnp.bfloat16)
    gate_down_gradient = adapter_scale * rows_product(own_cols, gate_factor_gate)
    up_down_gradient = adapter_scale * rows_product(own_cols, gate_factor_up)
    gate_lift_gradient = adapter_scale * rows_product(up_factor_gate, gate_gradient)
    up_lift_gradient = adapter_scale * rows_product(up_factor_up, up_gradient)
    return (
        token_gradient,
        gate_down_gradient,
        up_down_gradient,
        gate_lift_gradient,
        up_lift_gradient,
    )


def forward_kernel(x_ref, wg_ref, wu_ref, g0_ref, u0_ref, g_ref, u_ref):
    @pl.when(pl.program_id(0) == 0)
    def _():
        g_ref[...] = g0_ref[...]
        u_ref[...] = u0_ref[...]

    x = x_ref[...]
    g_ref[...] += jnp.dot(x, wg_ref[...], preferred_element_type=F32)
    u_ref[...] += jnp.dot(x, wu_ref[...], preferred_element_type=F32)


def forward_products(x, gate_weight, up_weight, so_far, first, count, depth=512):
    rows = x.shape[0]
    ff = gate_weight.shape[1]
    start = first // depth
    weight_block = pl.BlockSpec((depth, ff), lambda k: (k + start, 0))
    out_block = pl.BlockSpec((rows, ff), lambda k: (0, 0))
    return pl.pallas_call(
        forward_kernel,
        grid=(count // depth,),
        in_specs=[
            pl.BlockSpec((rows, depth), lambda k: (0, k + start)),
            weight_block,
            weight_block,
            out_block,
            out_block,
        ],
        out_specs=[out_block, out_block],
        out_shape=[jax.ShapeDtypeStruct((rows, ff), F32)] * 2,
        compiler_params=pltpu.CompilerParams(vmem_limit_bytes=40 << 20),
        cost_estimate=pl.CostEstimate(
            flops=4 * rows * count * ff, bytes_accessed=4 * count * ff, transcendentals=0
        ),
        name="forward_products",
    )(x, gate_weight, up_weight, *so_far)


def backward_kernel(dgt_ref, dut_ref, wg_ref, wu_ref, keep_ref, send_ref):
    total = jnp.dot(wg_ref[...], dgt_ref[...], preferred_element_type=F32)
    total += jnp.dot(wu_ref[...], dut_ref[...], preferred_element_type=F32)
    flat = total.T
    half = keep_ref.shape[0]
    keep_ref[...] = flat[:half]
    send_ref[...] = flat[half:].astype(send_ref.dtype)


def backward_products(dgt, dut, gate_weight, up_weight, first, count, depth=256):
    ff, rows = dgt.shape
    start = first // depth
    weight_block = pl.BlockSpec((depth, ff), lambda k: (k + start, 0))
    right_block = pl.BlockSpec((ff, rows), lambda k: (0, 0))
    out_block = pl.BlockSpec((rows // 2, depth), lambda k: (0, k))
    return pl.pallas_call(
        backward_kernel,
        grid=(count // depth,),
        in_specs=[right_block, right_block, weight_block, weight_block],
        out_specs=[out_block, out_block],
        out_shape=[
            jax.ShapeDtypeStruct((rows // 2, count), F32),
            jax.ShapeDtypeStruct((rows // 2, count), BF16),
        ],
        compiler_params=pltpu.CompilerParams(vmem_limit_bytes=40 << 20),
        cost_estimate=pl.CostEstimate(
            flops=4 * rows * count * ff, bytes_accessed=4 * count * ff, transcendentals=0
        ),
        name="backward_products",
    )(dgt, dut, gate_weight, up_weight)


N = 16


def along_tensor(value, mask):
    return lax.ppermute(value, "tensor", [(i, i ^ mask) for i in range(N)])


SLOTS = 4


def summed(value, recv, slot):
    shape = value.shape
    v, r = (w.reshape(2, 2, 2, 2, 2, shape[1]) for w in (value, recv))
    r = (r[::-1], r[:, ::-1], r[:, :, :, ::-1], r[:, :, ::-1])[slot]
    return (v + r).reshape(shape)


def in_order(*values):
    return lax.optimization_barrier(values)


def staged_device(tokens, gate_weight, up_weight, a_gate, a_up, b_gate, b_up, agent, d_hidden):
    t = lax.axis_index("tensor")
    d = tokens.shape[1]
    feat_rows = a_gate.shape[0]
    feat_start = t * feat_rows

    x = jnp.concatenate([tokens] + [along_tensor(tokens, 4 * m) for m in (1, 2, 3)], axis=0)
    x = jnp.concatenate([x, along_tensor(x, 2)], axis=0)
    x = jnp.concatenate([x, along_tensor(x, 1)], axis=0)
    rows = x.shape[0]

    place = jnp.arange(rows, dtype=jnp.int32)
    block = ((place >> 1) & 3) * 4 + ((place >> 3) & 1) * 2 + (place >> 4)
    token_of = ((t ^ block) << 1) + (place & 1)
    shuffle = token_of[:, None] == jnp.arange(rows, dtype=jnp.int32)[None, :]
    agent_here = jnp.sum(jnp.where(shuffle, agent[None, :], 0), axis=1)
    onehot = agent_mask(agent_here)
    hidden_grad = jnp.dot(shuffle.astype(BF16), d_hidden, preferred_element_type=F32)

    agent_gate_down = a_gate.astype(BF16)
    agent_up_down = a_up.astype(BF16)
    agent_gate_lift = b_gate.astype(BF16)
    agent_up_lift = b_up.astype(BF16)

    own_cols = lax.dynamic_slice_in_dim(x, feat_start, feat_rows, 1)
    part_gate = select_rank(jnp.dot(own_cols, agent_gate_down, preferred_element_type=F32), onehot)
    part_up = select_rank(jnp.dot(own_cols, agent_up_down, preferred_element_type=F32), onehot)
    part = jnp.concatenate([part_gate, part_up], axis=1)
    base = [jnp.zeros((rows, gate_weight.shape[1]), F32)] * 2
    count = d // SLOTS
    for slot in range(SLOTS):
        recv = along_tensor(part, 1 << slot)
        base = forward_products(x, gate_weight, up_weight, base, slot * count, count)
        recv, part, *base = in_order(recv, part, *base)
        part = summed(part, recv, slot)
    u = part.astype(BF16)
    up_factor_gate = spread_rank(u[:, :R], onehot)
    up_factor_up = spread_rank(u[:, R:], onehot)

    gate_values = base[0] + adapter_scale * jnp.dot(
        up_factor_gate, agent_gate_lift, preferred_element_type=F32
    )
    up_values = base[1] + adapter_scale * jnp.dot(
        up_factor_up, agent_up_lift, preferred_element_type=F32
    )
    sig = jax.nn.sigmoid(gate_values)
    gate_gradient = (hidden_grad * up_values * sig * (1.0 + gate_values * (1.0 - sig))).astype(BF16)
    up_gradient = (hidden_grad * gate_values * sig).astype(BF16)

    pg_gate = select_rank(flipped_product(gate_gradient, agent_gate_lift), onehot)
    pg_up = select_rank(flipped_product(up_gradient, agent_up_lift), onehot)
    part = jnp.concatenate([pg_gate, pg_up], axis=1)
    dgt, dut = gate_gradient.T, up_gradient.T
    kept, leave = [], []
    first_half = None
    for slot in range(SLOTS):
        recv = along_tensor(part, 1 << slot)
        if slot == 2:
            first_half = along_tensor(jnp.concatenate(leave, axis=1), 1)
        if slot == 3:
            first_half = jnp.concatenate(kept[:2], axis=1) + first_half.astype(F32)
            travel = along_tensor(first_half[rows // 4 :].astype(BF16), 2)
        keep, out = backward_products(dgt, dut, gate_weight, up_weight, slot * count, count)
        kept.append(keep)
        leave.append(out)
        if slot == 2:
            recv, part, dgt, dut, keep, first_half = in_order(recv, part, dgt, dut, keep, first_half)
        elif slot == 3:
            recv, part, travel = in_order(recv, part, travel)
        else:
            recv, part, dgt, dut = in_order(recv, part, dgt, dut)
        part = summed(part, recv, slot)
    first_half = first_half[: rows // 4] + travel.astype(F32)
    g = part.astype(BF16)
    gate_factor_gate = spread_rank(g[:, :R], onehot)
    gate_factor_up = spread_rank(g[:, R:], onehot)
    adapter_contribution = (
        adapter_scale
        * (
            flipped_product(gate_factor_gate, agent_gate_down)
            + flipped_product(gate_factor_up, agent_up_down)
        )
    ).astype(BF16)

    width = 2 * count
    sums = jnp.concatenate(kept[2:], axis=1)
    q = rows // 2
    recv = along_tensor(
        jnp.concatenate([*leave[2:], adapter_contribution[q:]], axis=1), 1
    )
    z_parts = [along_tensor(first_half[2 * m : 2 * m + 2].astype(BF16), 4 * m) for m in (1, 2, 3)]
    gate_lift_gradient = adapter_scale * rows_product(up_factor_gate, gate_gradient)
    recv, gate_lift_gradient, *z_parts = in_order(recv, gate_lift_gradient, *z_parts)
    first_half = first_half[:2] + sum(p.astype(F32) for p in z_parts)
    sums = sums + recv[:, :width].astype(F32)
    moved = jnp.concatenate([adapter_contribution[:q], recv[:, width:]], axis=1)

    q = rows // 4
    recv = along_tensor(jnp.concatenate([sums[q:].astype(BF16), moved[q:]], axis=1), 2)
    up_lift_gradient = adapter_scale * rows_product(up_factor_up, up_gradient)
    recv, up_lift_gradient = in_order(recv, up_lift_gradient)
    sums = sums[:q] + recv[:, :width].astype(F32)
    moved = jnp.concatenate([moved[:q], recv[:, width:]], axis=1)

    last = jnp.concatenate([sums.astype(BF16), moved], axis=1)
    z_parts = [along_tensor(last[2 * m : 2 * m + 2], 4 * m) for m in (1, 2, 3)]
    gate_down_gradient = adapter_scale * rows_product(own_cols, gate_factor_gate)
    up_down_gradient = adapter_scale * rows_product(own_cols, gate_factor_up)
    gate_down_gradient, up_down_gradient, *z_parts = in_order(
        gate_down_gradient, up_down_gradient, *z_parts
    )
    sums = sums[:2] + sum(p[:, :width].astype(F32) for p in z_parts)
    moved = jnp.stack([moved[:2]] + [p[:, width:] for p in z_parts])
    moved = moved.reshape(4, 2, 2, 2, feat_rows).transpose(0, 2, 3, 1, 4).reshape(N, 2 * feat_rows)
    source = jnp.arange(N, dtype=jnp.int32)
    sort = (source[:, None] == (t ^ source)[None, :]).astype(BF16)
    sorted_rows = jnp.dot(sort, moved, preferred_element_type=F32).reshape(N, 2, feat_rows)
    contribution = sorted_rows.transpose(1, 0, 2).reshape(2, d)
    token_gradient = (jnp.concatenate([first_half, sums], axis=1) + contribution).astype(BF16)
    return (
        token_gradient,
        gate_down_gradient,
        up_down_gradient,
        gate_lift_gradient,
        up_lift_gradient,
    )


def solution(mesh):
    sizes = dict(mesh.shape)

    def per_device(*args):
        tokens, b_gate = args[0], args[5]
        fits = (
            sizes["tensor"] == N
            and tokens.shape[0] == 2
            and b_gate.shape[1] % 128 == 0
            and tokens.shape[1] % 2048 == 0
        )
        return (staged_device if fits else plain_device)(*args)

    in_specs = (
        P(("group", "tensor"), None),
        P(None, "tensor"),
        P(None, "tensor"),
        P(("group", "tensor"), None),
        P(("group", "tensor"), None),
        P("group", "tensor"),
        P("group", "tensor"),
        P("group"),
        P("group", "tensor"),
    )
    out_specs = (
        P(("group", "tensor"), None),
        P(("group", "tensor"), None),
        P(("group", "tensor"), None),
        P("group", "tensor"),
        P("group", "tensor"),
    )
    return jax.shard_map(
        per_device, mesh=mesh, in_specs=in_specs, out_specs=out_specs, check_vma=False
    )
```

```python
import jax
import jax.numpy as jnp
from jax import lax
from jax.experimental import pallas as pl
from jax.experimental.pallas import tpu as pltpu
from jax.sharding import PartitionSpec as P

R = 64
AG = 16

adapter_scale = 2.0
BF16 = jnp.bfloat16
F32 = jnp.float32


def agent_mask(agent):
    return (agent[:, None] == jnp.arange(AG, dtype=jnp.int32)[None, :]).astype(jnp.float32)


def select_rank(values, onehot):
    shaped = values.reshape(values.shape[0], AG, R)
    return jnp.sum(shaped * onehot[:, :, None], axis=1)


def spread_rank(small, onehot):
    wide = onehot[:, :, None] * small.astype(jnp.float32)[:, None, :]
    return wide.reshape(small.shape[0], AG * R).astype(jnp.bfloat16)


def flipped_product(left, weight):
    return lax.dot_general(
        left, weight, (((1,), (1,)), ((), ())), preferred_element_type=jnp.float32
    )


def rows_product(left, right):
    return lax.dot_general(
        left, right, (((0,), (0,)), ((), ())), preferred_element_type=jnp.float32
    )


def plain_device(tokens, gate_weight, up_weight, a_gate, a_up, b_gate, b_up, agent, d_hidden):
    onehot = agent_mask(agent)
    feat_rows = a_gate.shape[0]
    feat_start = lax.axis_index("tensor") * feat_rows
    agent_gate_down = a_gate.astype(jnp.bfloat16)
    agent_up_down = a_up.astype(jnp.bfloat16)
    agent_gate_lift = b_gate.astype(jnp.bfloat16)
    agent_up_lift = b_up.astype(jnp.bfloat16)
    complete_result = lax.all_gather(tokens, "tensor", axis=0, tiled=True)
    own_cols = lax.dynamic_slice_in_dim(complete_result, feat_start, feat_rows, 1)
    part_gate = select_rank(
        jnp.dot(own_cols, agent_gate_down, preferred_element_type=jnp.float32), onehot
    )
    part_up = select_rank(
        jnp.dot(own_cols, agent_up_down, preferred_element_type=jnp.float32), onehot
    )
    u_gate, u_up = lax.psum((part_gate, part_up), "tensor")
    up_factor_gate = spread_rank(u_gate.astype(jnp.bfloat16), onehot)
    up_factor_up = spread_rank(u_up.astype(jnp.bfloat16), onehot)
    gate_values = jnp.dot(
        complete_result, gate_weight, preferred_element_type=jnp.float32
    ) + adapter_scale * jnp.dot(up_factor_gate, agent_gate_lift, preferred_element_type=jnp.float32)
    up_values = jnp.dot(
        complete_result, up_weight, preferred_element_type=jnp.float32
    ) + adapter_scale * jnp.dot(up_factor_up, agent_up_lift, preferred_element_type=jnp.float32)
    sig = jax.nn.sigmoid(gate_values)
    hidden_grad = d_hidden.astype(jnp.float32)
    gate_gradient = (hidden_grad * up_values * sig * (1.0 + gate_values * (1.0 - sig))).astype(
        jnp.bfloat16
    )
    up_gradient = (hidden_grad * gate_values * sig).astype(jnp.bfloat16)
    pg_gate = select_rank(flipped_product(gate_gradient, agent_gate_lift), onehot)
    pg_up = select_rank(flipped_product(up_gradient, agent_up_lift), onehot)
    g_gate, g_up = lax.psum((pg_gate, pg_up), "tensor")
    gate_factor_gate = spread_rank(g_gate.astype(jnp.bfloat16), onehot)
    gate_factor_up = spread_rank(g_up.astype(jnp.bfloat16), onehot)
    adapter_contribution = adapter_scale * (
        flipped_product(gate_factor_gate, agent_gate_down)
        + flipped_product(gate_factor_up, agent_up_down)
    )
    base_rows = flipped_product(gate_gradient, gate_weight) + flipped_product(
        up_gradient, up_weight
    )
    joined = lax.dynamic_slice_in_dim(base_rows, feat_start, feat_rows, 1) + adapter_contribution
    token_gradient = lax.psum_scatter(
        lax.dynamic_update_slice_in_dim(base_rows, joined, feat_start, 1),
        "tensor",
        scatter_dimension=0,
        tiled=True,
    ).astype(jnp.bfloat16)
    gate_down_gradient = adapter_scale * rows_product(own_cols, gate_factor_gate)
    up_down_gradient = adapter_scale * rows_product(own_cols, gate_factor_up)
    gate_lift_gradient = adapter_scale * rows_product(up_factor_gate, gate_gradient)
    up_lift_gradient = adapter_scale * rows_product(up_factor_up, up_gradient)
    return (
        token_gradient,
        gate_down_gradient,
        up_down_gradient,
        gate_lift_gradient,
        up_lift_gradient,
    )


def forward_kernel(side_ref, x_ref, w_ref, *refs):
    before_ref, out_refs, total = refs[0], refs[-3:-1], refs[-1]
    step = pl.program_id(0)

    @pl.when(step == 0)
    def _():
        total[...] = before_ref[...] if len(refs) == 4 else jnp.zeros_like(total)

    total[...] += jnp.dot(x_ref[...], w_ref[...], preferred_element_type=F32)

    @pl.when(step == pl.num_programs(0) - 1)
    def _():
        half = out_refs[0].shape[0]
        out_refs[0][...] = total[:half].astype(out_refs[0].dtype)
        out_refs[1][...] = total[half:].astype(out_refs[1].dtype)


def forward_products(side, x, weight, before, first, count, send, depth=512):
    rows, features = x.shape
    ff = weight.shape[1]
    start = first // depth
    per_side = features // depth
    whole = pl.BlockSpec((rows, ff), lambda k, s: (0, 0))
    half = pl.BlockSpec((rows // 2, ff), lambda k, s: (0, 0))
    extra = () if before is None else (jnp.concatenate(before, axis=0),)
    return pl.pallas_call(
        forward_kernel,
        grid_spec=pltpu.PrefetchScalarGridSpec(
            num_scalar_prefetch=1,
            grid=(count // depth,),
            in_specs=[
                pl.BlockSpec((rows, depth), lambda k, s: (0, k + start)),
                pl.BlockSpec((depth, ff), lambda k, s: (s[0] * per_side + k + start, 0)),
            ]
            + [whole] * len(extra),
            out_specs=[half, half],
            scratch_shapes=[pltpu.VMEM((rows, ff), F32)],
        ),
        out_shape=[
            jax.ShapeDtypeStruct((rows // 2, ff), F32),
            jax.ShapeDtypeStruct((rows // 2, ff), send),
        ],
        compiler_params=pltpu.CompilerParams(vmem_limit_bytes=40 << 20),
        cost_estimate=pl.CostEstimate(
            flops=2 * rows * count * ff, bytes_accessed=2 * count * ff, transcendentals=0
        ),
        name="forward_products",
    )(side, x, weight, *extra)


def hidden_kernel(
    eug_ref, euu_ref, bg_ref, bu_ref, g0_ref, g1_ref, u0_ref, u1_ref, dh_ref, dg_ref, du_ref, pg_ref, pu_ref
):
    @pl.when(pl.program_id(0) == 0)
    def _():
        pg_ref[...] = jnp.zeros_like(pg_ref)
        pu_ref[...] = jnp.zeros_like(pu_ref)

    bg = bg_ref[...].astype(BF16)
    bu = bu_ref[...].astype(BF16)
    gate = (
        g0_ref[...]
        + g1_ref[...].astype(F32)
        + adapter_scale * jnp.dot(eug_ref[...], bg, preferred_element_type=F32)
    )
    up = (
        u0_ref[...]
        + u1_ref[...].astype(F32)
        + adapter_scale * jnp.dot(euu_ref[...], bu, preferred_element_type=F32)
    )
    sig = jax.nn.sigmoid(gate)
    hidden_grad = dh_ref[...]
    dg = (hidden_grad * up * sig * (1.0 + gate * (1.0 - sig))).astype(BF16)
    du = (hidden_grad * gate * sig).astype(BF16)
    dg_ref[...] = dg
    du_ref[...] = du
    pg_ref[...] += flipped_product(dg, bg)
    pu_ref[...] += flipped_product(du, bu)


def hidden_gradients(eug, euu, b_gate, b_up, gate, up, hidden_grad, width=256):
    rows, wide = eug.shape
    ff = b_gate.shape[1]
    fixed = pl.BlockSpec((rows, wide), lambda k: (0, 0))
    b_block = pl.BlockSpec((wide, width), lambda k: (0, k))
    block = pl.BlockSpec((rows, width), lambda k: (0, k))
    return pl.pallas_call(
        hidden_kernel,
        grid=(ff // width,),
        in_specs=[fixed, fixed, b_block, b_block, block, block, block, block, block],
        out_specs=[block, block, fixed, fixed],
        out_shape=[jax.ShapeDtypeStruct((rows, ff), BF16)] * 2
        + [jax.ShapeDtypeStruct((rows, wide), F32)] * 2,
        compiler_params=pltpu.CompilerParams(vmem_limit_bytes=40 << 20),
        cost_estimate=pl.CostEstimate(
            flops=8 * rows * wide * ff, bytes_accessed=8 * wide * ff, transcendentals=rows * ff
        ),
        name="hidden_gradients",
    )(eug, euu, b_gate, b_up, *gate, *up, hidden_grad)


def backward_kernel(side_ref, dg_ref, du_ref, wg_ref, wu_ref, keep_ref, send_ref):
    total = flipped_product(dg_ref[...], wg_ref[...]) + flipped_product(du_ref[...], wu_ref[...])
    q = total.shape[0] // 4
    keep_ref[:q] = total[:q]
    keep_ref[q:] = total[2 * q : 3 * q]
    send_ref[:q] = total[q : 2 * q].astype(send_ref.dtype)
    send_ref[q:] = total[3 * q :].astype(send_ref.dtype)


def backward_products(side, dg, du, gate_weight, up_weight, first, count, depth=512):
    rows, ff = dg.shape
    start = first // depth
    per_side = gate_weight.shape[0] // 2 // depth
    weight_block = pl.BlockSpec((depth, ff), lambda k, s: (s[0] * per_side + k + start, 0))
    left_block = pl.BlockSpec((rows, ff), lambda k, s: (0, 0))
    out_block = pl.BlockSpec((rows // 2, depth), lambda k, s: (0, k))
    return pl.pallas_call(
        backward_kernel,
        grid_spec=pltpu.PrefetchScalarGridSpec(
            num_scalar_prefetch=1,
            grid=(count // depth,),
            in_specs=[left_block, left_block, weight_block, weight_block],
            out_specs=[out_block, out_block],
        ),
        out_shape=[
            jax.ShapeDtypeStruct((rows // 2, count), F32),
            jax.ShapeDtypeStruct((rows // 2, count), BF16),
        ],
        compiler_params=pltpu.CompilerParams(vmem_limit_bytes=40 << 20),
        cost_estimate=pl.CostEstimate(
            flops=4 * rows * count * ff, bytes_accessed=4 * count * ff, transcendentals=0
        ),
        name="backward_products",
    )(side, dg, du, gate_weight, up_weight)


N = 16
SLOTS = 4


def along_tensor(value, mask):
    return lax.ppermute(value, "tensor", [(i, i ^ mask) for i in range(N)])


def across_groups(value):
    return lax.ppermute(value, "group", [(0, 1), (1, 0)])


def summed(value, recv, slot):
    shape = value.shape
    v, r = (w.reshape(2, 2, 2, 2, 2, shape[1]) for w in (value, recv))
    r = (r[::-1], r[:, ::-1], r[:, :, :, ::-1], r[:, :, ::-1])[slot]
    return (v + r).reshape(shape)


def in_order(*values):
    return lax.optimization_barrier(values)


def from_far_z(value):
    return [along_tensor(v, 4 * m) for m, v in zip((1, 2, 3), value)]


def shared_device(tokens, gate_weight, up_weight, a_gate, a_up, b_gate, b_up, agent, d_hidden):
    group = lax.axis_index("group")
    t = lax.axis_index("tensor")
    side = group.astype(jnp.int32).reshape(1)
    d = tokens.shape[1]
    half = d // 2
    feat_rows = a_gate.shape[0]
    per_half = half // feat_rows

    x = jnp.stack(
        [
            lax.dynamic_slice_in_dim(tokens, group * half, half, 1),
            across_groups(lax.dynamic_slice_in_dim(tokens, half - group * half, half, 1)),
        ]
    )
    x = jnp.concatenate([x] + from_far_z([x] * 3), axis=1)
    x = jnp.concatenate([x, along_tensor(x, 2)], axis=1)
    x = jnp.concatenate([x, along_tensor(x, 1)], axis=1)
    rows = x.shape[1]
    x = x.reshape(2 * rows, half)

    place = jnp.arange(rows, dtype=jnp.int32)
    block = ((place >> 1) & 3) * 4 + ((place >> 3) & 1) * 2 + (place >> 4)
    token_of = ((t ^ block) << 1) + (place & 1)
    shuffle = token_of[:, None] == jnp.arange(rows, dtype=jnp.int32)[None, :]
    agent_here = jnp.sum(jnp.where(shuffle, agent[None, :], 0), axis=1)
    onehot = agent_mask(agent_here)
    hidden_grad = jnp.dot(shuffle.astype(BF16), d_hidden, preferred_element_type=F32)

    blocks = lax.dynamic_slice_in_dim(x, (t % per_half) * feat_rows, feat_rows, 1)
    swapped = across_groups(blocks[rows:])
    count = half // 2
    gate = forward_products(side, x, gate_weight, None, 0, count, F32)
    swapped, *gate = in_order(swapped, *gate)
    own_cols = jnp.where(t // per_half == group, blocks[:rows], swapped)

    part_gate = select_rank(
        jnp.dot(own_cols, a_gate.astype(BF16), preferred_element_type=F32), onehot
    )
    part_up = select_rank(jnp.dot(own_cols, a_up.astype(BF16), preferred_element_type=F32), onehot)
    part = jnp.concatenate([part_gate, part_up], axis=1)

    part, *gate = in_order(part, *gate)
    recv = along_tensor(part, 1)
    gate = forward_products(side, x, gate_weight, gate, count, count, BF16)
    recv, x, *gate = in_order(recv, x, *gate)
    part = summed(part, recv, 0)

    recv, far = along_tensor(part, 2), across_groups(gate[1])
    up = forward_products(side, x, up_weight, None, 0, count, F32)
    recv, far, x, *up = in_order(recv, far, x, *up)
    gate = gate[0], far
    part = summed(part, recv, 1)

    recv = along_tensor(part, 4)
    up = forward_products(side, x, up_weight, up, count, count, BF16)
    recv, *up = in_order(recv, *up)
    up = up[0], across_groups(up[1])
    part = summed(part, recv, 2)
    part = summed(part, along_tensor(part, 8), 3)
    u = part.astype(BF16)
    up_factor_gate = spread_rank(u[:, :R], onehot)
    up_factor_up = spread_rank(u[:, R:], onehot)

    gate_gradient, up_gradient, pg_gate, pg_up = hidden_gradients(
        up_factor_gate, up_factor_up, b_gate, b_up, gate, up, hidden_grad
    )

    far = across_groups(jnp.stack([gate_gradient, up_gradient]))
    part = jnp.concatenate([select_rank(pg_gate, onehot), select_rank(pg_up, onehot)], axis=1)
    recv = along_tensor(part, 1)
    gate_lift_gradient = adapter_scale * rows_product(up_factor_gate, gate_gradient)
    far, recv, gate_lift_gradient = in_order(far, recv, gate_lift_gradient)
    part = summed(part, recv, 0)
    dg = jnp.concatenate([gate_gradient, far[0]], axis=0)
    du = jnp.concatenate([up_gradient, far[1]], axis=0)

    count = half // SLOTS

    def backward(slot):
        return backward_products(side, dg, du, gate_weight, up_weight, slot * count, count)

    recv = along_tensor(part, 2)
    keep_0, send_0 = backward(0)
    recv, dg, du, keep_0, send_0 = in_order(recv, dg, du, keep_0, send_0)
    part = summed(part, recv, 1)

    recv = along_tensor(part, 4)
    keep_1, send_1 = backward(1)
    recv, dg, du, keep_1, send_1 = in_order(recv, dg, du, keep_1, send_1)
    part = summed(part, recv, 2)

    recv = along_tensor(part, 8)
    far = along_tensor(jnp.concatenate([send_0, send_1], axis=1), 1)
    keep_2, send_2 = backward(2)
    recv, far, dg, du, keep_2, send_2 = in_order(recv, far, dg, du, keep_2, send_2)
    part = summed(part, recv, 3)
    g = part.astype(BF16)
    gate_factor_gate = spread_rank(g[:, :R], onehot)
    gate_factor_up = spread_rank(g[:, R:], onehot)

    early = (jnp.concatenate([keep_0, keep_1], axis=1) + far.astype(F32)).reshape(2, 16, -1)
    far = along_tensor(early[:, 8:].astype(BF16), 2)
    keep_3, send_3 = backward(3)
    far, keep_3, send_3 = in_order(far, keep_3, send_3)
    early = early[:, :8] + far.astype(F32)
    contribution = (
        adapter_scale
        * (
            flipped_product(gate_factor_gate, a_gate.astype(BF16))
            + flipped_product(gate_factor_up, a_up.astype(BF16))
        )
    ).astype(BF16)

    def beside(sums, columns):
        other = jnp.zeros_like(columns)
        return jnp.concatenate([sums.astype(BF16), jnp.stack([columns, other])], axis=2)

    width = 2 * count
    sums = jnp.concatenate([keep_2, keep_3], axis=1).reshape(2, 16, -1)
    send = jnp.concatenate([send_2, send_3], axis=1).reshape(2, 16, -1)
    far = along_tensor(beside(send, contribution[16:]), 1)
    parts = from_far_z([early[:, 2 * m : 2 * m + 2].astype(BF16) for m in (1, 2, 3)])
    gate_down_gradient = adapter_scale * rows_product(own_cols, gate_factor_gate)
    far, gate_down_gradient, *parts = in_order(far, gate_down_gradient, *parts)
    early = early[:, :2] + sum(p.astype(F32) for p in parts)
    sums = sums + far[:, :, :width].astype(F32)
    moved = jnp.concatenate([contribution[:16], far[0, :, width:]], axis=1)

    far = along_tensor(beside(sums[:, 8:], moved[8:]), 2)
    up_down_gradient = adapter_scale * rows_product(own_cols, gate_factor_up)
    far, up_down_gradient = in_order(far, up_down_gradient)
    sums = sums[:, :8] + far[:, :, :width].astype(F32)
    moved = jnp.concatenate([moved[:8], far[0, :, width:]], axis=1)

    last = beside(sums, moved)
    parts = from_far_z([last[:, 2 * m : 2 * m + 2] for m in (1, 2, 3)])
    up_lift_gradient = adapter_scale * rows_product(up_factor_up, up_gradient)
    up_lift_gradient, *parts = in_order(up_lift_gradient, *parts)
    sums = sums[:, :2] + sum(p[:, :, :width].astype(F32) for p in parts)
    sums = jnp.concatenate([early, sums], axis=2)
    far = across_groups(sums[1].astype(BF16))

    moved = jnp.stack([moved[:2]] + [p[0, :, width:] for p in parts])
    moved = moved.reshape(4, 2, 2, 2, feat_rows).transpose(0, 2, 3, 1, 4).reshape(N, 2 * feat_rows)
    source = jnp.arange(N, dtype=jnp.int32)
    sort = (source[:, None] == (t ^ source)[None, :]).astype(BF16)
    sorted_rows = jnp.dot(sort, moved, preferred_element_type=F32).reshape(N, 2, feat_rows)
    contribution = sorted_rows.transpose(1, 0, 2).reshape(2, d)
    far = far.astype(F32)
    token_gradient = (
        jnp.where(
            group == 0,
            jnp.concatenate([sums[0], far], axis=1),
            jnp.concatenate([far, sums[0]], axis=1),
        )
        + contribution
    ).astype(BF16)
    return (
        token_gradient,
        gate_down_gradient,
        up_down_gradient,
        gate_lift_gradient,
        up_lift_gradient,
    )


def solution(mesh):
    sizes = dict(mesh.shape)

    def per_device(*args):
        tokens, b_gate = args[0], args[5]
        fits = (
            sizes["group"] == 2
            and sizes["tensor"] == N
            and tokens.shape[0] == 2
            and b_gate.shape[1] % 256 == 0
            and tokens.shape[1] % 4096 == 0
        )
        return (shared_device if fits else plain_device)(*args)

    in_specs = (
        P(("group", "tensor"), None),
        P(None, "tensor"),
        P(None, "tensor"),
        P(("group", "tensor"), None),
        P(("group", "tensor"), None),
        P("group", "tensor"),
        P("group", "tensor"),
        P("group"),
        P("group", "tensor"),
    )
    out_specs = (
        P(("group", "tensor"), None),
        P(("group", "tensor"), None),
        P(("group", "tensor"), None),
        P("group", "tensor"),
        P("group", "tensor"),
    )
    return jax.shard_map(
        per_device, mesh=mesh, in_specs=in_specs, out_specs=out_specs, check_vma=False
    )
```

```python
import functools

import jax
import jax.numpy as jnp
from jax import lax
from jax.experimental import pallas as pl
from jax.experimental.pallas import tpu as pltpu
from jax.sharding import PartitionSpec as P

R = 64
AG = 16

adapter_scale = 2.0
BF16 = jnp.bfloat16
F32 = jnp.float32


def agent_mask(agent):
    return (agent[:, None] == jnp.arange(AG, dtype=jnp.int32)[None, :]).astype(jnp.float32)


def select_rank(values, onehot):
    shaped = values.reshape(values.shape[0], AG, R)
    return jnp.sum(shaped * onehot[:, :, None], axis=1)


def spread_rank(small, onehot):
    wide = onehot[:, :, None] * small.astype(jnp.float32)[:, None, :]
    return wide.reshape(small.shape[0], AG * R).astype(jnp.bfloat16)


def flipped_product(left, weight):
    return lax.dot_general(
        left, weight, (((1,), (1,)), ((), ())), preferred_element_type=jnp.float32
    )


def rows_product(left, right):
    return lax.dot_general(
        left, right, (((0,), (0,)), ((), ())), preferred_element_type=jnp.float32
    )


def plain_device(tokens, gate_weight, up_weight, a_gate, a_up, b_gate, b_up, agent, d_hidden):
    onehot = agent_mask(agent)
    feat_rows = a_gate.shape[0]
    feat_start = lax.axis_index("tensor") * feat_rows
    agent_gate_down = a_gate.astype(jnp.bfloat16)
    agent_up_down = a_up.astype(jnp.bfloat16)
    agent_gate_lift = b_gate.astype(jnp.bfloat16)
    agent_up_lift = b_up.astype(jnp.bfloat16)
    complete_result = lax.all_gather(tokens, "tensor", axis=0, tiled=True)
    own_cols = lax.dynamic_slice_in_dim(complete_result, feat_start, feat_rows, 1)
    part_gate = select_rank(
        jnp.dot(own_cols, agent_gate_down, preferred_element_type=jnp.float32), onehot
    )
    part_up = select_rank(
        jnp.dot(own_cols, agent_up_down, preferred_element_type=jnp.float32), onehot
    )
    u_gate, u_up = lax.psum((part_gate, part_up), "tensor")
    up_factor_gate = spread_rank(u_gate.astype(jnp.bfloat16), onehot)
    up_factor_up = spread_rank(u_up.astype(jnp.bfloat16), onehot)
    gate_values = jnp.dot(
        complete_result, gate_weight, preferred_element_type=jnp.float32
    ) + adapter_scale * jnp.dot(up_factor_gate, agent_gate_lift, preferred_element_type=jnp.float32)
    up_values = jnp.dot(
        complete_result, up_weight, preferred_element_type=jnp.float32
    ) + adapter_scale * jnp.dot(up_factor_up, agent_up_lift, preferred_element_type=jnp.float32)
    sig = jax.nn.sigmoid(gate_values)
    hidden_grad = d_hidden.astype(jnp.float32)
    gate_gradient = (hidden_grad * up_values * sig * (1.0 + gate_values * (1.0 - sig))).astype(
        jnp.bfloat16
    )
    up_gradient = (hidden_grad * gate_values * sig).astype(jnp.bfloat16)
    pg_gate = select_rank(flipped_product(gate_gradient, agent_gate_lift), onehot)
    pg_up = select_rank(flipped_product(up_gradient, agent_up_lift), onehot)
    g_gate, g_up = lax.psum((pg_gate, pg_up), "tensor")
    gate_factor_gate = spread_rank(g_gate.astype(jnp.bfloat16), onehot)
    gate_factor_up = spread_rank(g_up.astype(jnp.bfloat16), onehot)
    adapter_contribution = adapter_scale * (
        flipped_product(gate_factor_gate, agent_gate_down)
        + flipped_product(gate_factor_up, agent_up_down)
    )
    base_rows = flipped_product(gate_gradient, gate_weight) + flipped_product(
        up_gradient, up_weight
    )
    joined = lax.dynamic_slice_in_dim(base_rows, feat_start, feat_rows, 1) + adapter_contribution
    token_gradient = lax.psum_scatter(
        lax.dynamic_update_slice_in_dim(base_rows, joined, feat_start, 1),
        "tensor",
        scatter_dimension=0,
        tiled=True,
    ).astype(jnp.bfloat16)
    gate_down_gradient = adapter_scale * rows_product(own_cols, gate_factor_gate)
    up_down_gradient = adapter_scale * rows_product(own_cols, gate_factor_up)
    gate_lift_gradient = adapter_scale * rows_product(up_factor_gate, gate_gradient)
    up_lift_gradient = adapter_scale * rows_product(up_factor_up, up_gradient)
    return (
        token_gradient,
        gate_down_gradient,
        up_down_gradient,
        gate_lift_gradient,
        up_lift_gradient,
    )


def forward_kernel(first, side_ref, x_ref, wg_ref, wu_ref, keep_ref, send_ref, piece, sem):
    pieces, depth, count = piece.shape[1:]
    half = keep_ref.shape[1]
    base = side_ref[0] * (pieces * depth)
    copies = []
    for i, w_ref in enumerate((wg_ref, wu_ref)):
        for k in range(pieces):
            source = pl.ds(pl.multiple_of(base + k * depth, depth), depth)
            copy = pltpu.make_async_copy(
                w_ref.at[source, pl.ds(first, count)], piece.at[i, k], sem.at[i, k]
            )
            copy.start()
            copies.append(copy)
    for i in range(2):
        total = None
        for k in range(pieces):
            copies[i * pieces + k].wait()
            term = jnp.dot(
                x_ref[:, k * depth : (k + 1) * depth], piece[i, k], preferred_element_type=F32
            )
            total = term if total is None else total + term
        keep_ref[i] = total[:half]
        send_ref[i] = total[half:].astype(send_ref.dtype)


def forward_products(side, x, gate_weight, up_weight, first, count, pieces=4):
    rows, depth = x.shape
    vmem = pl.BlockSpec(memory_space=pltpu.VMEM)
    hbm = pl.BlockSpec(memory_space=pltpu.HBM)
    return pl.pallas_call(
        functools.partial(forward_kernel, first),
        in_specs=[pl.BlockSpec(memory_space=pltpu.SMEM), vmem, hbm, hbm],
        out_specs=[vmem] * 2,
        out_shape=[
            jax.ShapeDtypeStruct((2, rows // 2, count), F32),
            jax.ShapeDtypeStruct((2, rows // 2, count), BF16),
        ],
        scratch_shapes=[
            pltpu.VMEM((2, pieces, depth // pieces, count), BF16),
            pltpu.SemaphoreType.DMA((2, pieces)),
        ],
        compiler_params=pltpu.CompilerParams(vmem_limit_bytes=20 << 20),
        cost_estimate=pl.CostEstimate(
            flops=4 * rows * count * depth, bytes_accessed=6 * count * depth, transcendentals=0
        ),
        name="forward_products",
    )(
        side,
        x,
        pltpu.with_memory_space_constraint(gate_weight, pltpu.HBM),
        pltpu.with_memory_space_constraint(up_weight, pltpu.HBM),
    )


def hidden_kernel(
    eug_ref, euu_ref, bg_ref, bu_ref, keep_ref, far_ref, dh_ref, d_ref, pg_ref, pu_ref
):
    @pl.when(pl.program_id(0) == 0)
    def _():
        pg_ref[...] = jnp.zeros_like(pg_ref)
        pu_ref[...] = jnp.zeros_like(pu_ref)

    bg = bg_ref[...].astype(BF16)
    bu = bu_ref[...].astype(BF16)
    gate = (
        keep_ref[0]
        + far_ref[0].astype(F32)
        + adapter_scale * jnp.dot(eug_ref[...], bg, preferred_element_type=F32)
    )
    up = (
        keep_ref[1]
        + far_ref[1].astype(F32)
        + adapter_scale * jnp.dot(euu_ref[...], bu, preferred_element_type=F32)
    )
    sig = jax.nn.sigmoid(gate)
    hidden_grad = dh_ref[...]
    dg = (hidden_grad * up * sig * (1.0 + gate * (1.0 - sig))).astype(BF16)
    du = (hidden_grad * gate * sig).astype(BF16)
    d_ref[0] = dg
    d_ref[1] = du
    pg_ref[...] += flipped_product(dg, bg)
    pu_ref[...] += flipped_product(du, bu)


def hidden_gradients(eug, euu, b_gate, b_up, keep, far, hidden_grad, first, width=256):
    rows, wide = eug.shape
    count = keep.shape[2]
    start = first // width
    fixed = pl.BlockSpec((rows, wide), lambda k: (0, 0))
    b_block = pl.BlockSpec((wide, width), lambda k: (0, k + start))
    block = pl.BlockSpec((2, rows, width), lambda k: (0, 0, k))
    return pl.pallas_call(
        hidden_kernel,
        grid=(count // width,),
        in_specs=[
            fixed,
            fixed,
            b_block,
            b_block,
            block,
            block,
            pl.BlockSpec((rows, width), lambda k: (0, k + start)),
        ],
        out_specs=[block, fixed, fixed],
        out_shape=[jax.ShapeDtypeStruct((2, rows, count), BF16)]
        + [jax.ShapeDtypeStruct((rows, wide), F32)] * 2,
        compiler_params=pltpu.CompilerParams(vmem_limit_bytes=20 << 20),
        cost_estimate=pl.CostEstimate(
            flops=8 * rows * wide * count, bytes_accessed=16 * wide * count, transcendentals=0
        ),
        name="hidden_gradients",
    )(
        eug,
        euu,
        pltpu.with_memory_space_constraint(b_gate, pltpu.HBM),
        pltpu.with_memory_space_constraint(b_up, pltpu.HBM),
        keep,
        far,
        hidden_grad,
    )


def backward_kernel(first, side_ref, dg_ref, du_ref, wg_ref, wu_ref, keep_ref, send_ref, piece, sem):
    pieces, depth = piece.shape[1:3]
    base = side_ref[0] * (wg_ref.shape[0] // 2) + first
    copies = []
    for k in range(pieces):
        for i, w_ref in enumerate((wg_ref, wu_ref)):
            source = pl.ds(pl.multiple_of(base + k * depth, depth), depth)
            copy = pltpu.make_async_copy(w_ref.at[source], piece.at[i, k], sem.at[i, k])
            copy.start()
            copies.append(copy)
    q = dg_ref.shape[0] // 4
    for k in range(pieces):
        copies[2 * k].wait()
        total = flipped_product(dg_ref[...], piece[0, k])
        copies[2 * k + 1].wait()
        total += flipped_product(du_ref[...], piece[1, k])
        out = pl.ds(k * depth, depth)
        keep_ref[:q, out] = total[:q]
        keep_ref[q:, out] = total[2 * q : 3 * q]
        send_ref[:q, out] = total[q : 2 * q].astype(send_ref.dtype)
        send_ref[q:, out] = total[3 * q :].astype(send_ref.dtype)


def backward_products(side, dg, du, gate_weight, up_weight, first, count, pieces=4):
    rows, ff = dg.shape
    vmem = pl.BlockSpec(memory_space=pltpu.VMEM)
    hbm = pl.BlockSpec(memory_space=pltpu.HBM)
    return pl.pallas_call(
        functools.partial(backward_kernel, first),
        in_specs=[pl.BlockSpec(memory_space=pltpu.SMEM), vmem, vmem, hbm, hbm],
        out_specs=[vmem] * 2,
        out_shape=[
            jax.ShapeDtypeStruct((rows // 2, count), F32),
            jax.ShapeDtypeStruct((rows // 2, count), BF16),
        ],
        scratch_shapes=[
            pltpu.VMEM((2, pieces, count // pieces, ff), BF16),
            pltpu.SemaphoreType.DMA((2, pieces)),
        ],
        compiler_params=pltpu.CompilerParams(vmem_limit_bytes=20 << 20),
        cost_estimate=pl.CostEstimate(
            flops=4 * rows * count * ff, bytes_accessed=6 * count * ff, transcendentals=0
        ),
        name="backward_products",
    )(
        side,
        dg,
        du,
        pltpu.with_memory_space_constraint(gate_weight, pltpu.HBM),
        pltpu.with_memory_space_constraint(up_weight, pltpu.HBM),
    )


N = 16
CORE, X = 1, 2


def along_tensor(value, mask):
    return lax.ppermute(value, "tensor", [(i, i ^ mask) for i in range(N)])


def across_groups(value, mask=0):
    both = ("group", "tensor")
    return lax.ppermute(value, both, [(i, i ^ (N | mask)) for i in range(2 * N)])


def from_far_z(values):
    return [along_tensor(v, 4 * m) for m, v in zip((1, 2, 3), values)]


def in_order(*values):
    return lax.optimization_barrier(values)


def add_core(value, recv):
    half = value.shape[0] // 2
    return value + jnp.concatenate([recv[half:], recv[:half]], axis=0)


def add_x(value, recv):
    q = value.shape[0] // 4
    order = (1, 0, 3, 2)
    return value + jnp.concatenate([recv[o * q : (o + 1) * q] for o in order], axis=0)


def add_far_z(value, parts):
    shape = value.shape
    total = value.reshape(4, 4, 2, shape[1])
    for m, part in zip((1, 2, 3), parts):
        part = part.reshape(total.shape)
        total = total + jnp.stack([part[:, q ^ m] for q in range(4)], axis=1)
    return total.reshape(shape)


def shared_device(tokens, gate_weight, up_weight, a_gate, a_up, b_gate, b_up, agent, d_hidden):
    group = lax.axis_index("group")
    t = lax.axis_index("tensor")
    side = group.astype(jnp.int32).reshape(1)
    d = tokens.shape[1]
    half = d // 2
    feat_rows = a_gate.shape[0]
    per_half = half // feat_rows
    rows = 2 * N
    ff = b_gate.shape[1]

    parts = from_far_z([tokens] * 3)
    line = jnp.concatenate([tokens, *parts], axis=0)
    mine = lax.dynamic_slice_in_dim(line, group * half, half, 1)
    other = lax.dynamic_slice_in_dim(line, half - group * half, half, 1)
    parts = [along_tensor(mine, X), across_groups(other), across_groups(other, X)]
    x = jnp.stack(
        [jnp.concatenate([mine, parts[0]], axis=0), jnp.concatenate([parts[1], parts[2]], axis=0)]
    )
    x = jnp.concatenate([x, along_tensor(x, CORE)], axis=1).reshape(2 * rows, half)

    place = jnp.arange(rows, dtype=jnp.int32)
    block = ((place >> 1) & 3) * 4 + ((place >> 3) & 1) * 2 + (place >> 4)
    token_of = ((t ^ block) << 1) + (place & 1)
    shuffle = token_of[:, None] == jnp.arange(rows, dtype=jnp.int32)[None, :]
    agent_here = jnp.sum(jnp.where(shuffle, agent[None, :], 0), axis=1)
    chosen = agent_here[:, None] == (jnp.arange(AG * R, dtype=jnp.int32) // R)[None, :]
    hidden_grad = jnp.dot(shuffle.astype(BF16), d_hidden, preferred_element_type=F32)

    def select(values):
        kept = jnp.where(chosen, values, 0.0)
        pair = sum(kept[:, c : c + 2 * R] for c in range(0, AG * R, 2 * R))
        return pair[:, :R] + pair[:, R:]

    def spread(small):
        wide = jnp.concatenate([small] * AG, axis=1)
        return jnp.where(chosen, wide, 0.0).astype(BF16)

    blocks = lax.dynamic_slice_in_dim(x, (t % per_half) * feat_rows, feat_rows, 1)
    swapped = across_groups(blocks[rows:])
    cuts = [ff * c // 7 for c in (0, 2, 4, 5, 7)]

    def forward(c):
        return forward_products(
            side, x, gate_weight, up_weight, cuts[c], cuts[c + 1] - cuts[c]
        )

    keep_0, send_0 = forward(0)
    swapped, x, keep_0, send_0 = in_order(swapped, x, keep_0, send_0)
    own_cols = jnp.where(t // per_half == group, blocks[:rows], swapped)
    part = jnp.concatenate(
        [
            select(jnp.dot(own_cols, a_gate.astype(BF16), preferred_element_type=F32)),
            select(jnp.dot(own_cols, a_up.astype(BF16), preferred_element_type=F32)),
        ],
        axis=1,
    )

    part, x = in_order(part, x)
    recv = along_tensor(part, CORE)
    keep_1, send_1 = forward(1)
    recv, x, keep_1, send_1 = in_order(recv, x, keep_1, send_1)
    part = add_core(part, recv)

    recv = along_tensor(part, X)
    far_a = across_groups(jnp.concatenate([send_0, send_1], axis=2))
    keep_2, send_2 = forward(2)
    recv, x, keep_2, send_2 = in_order(recv, x, keep_2, send_2)
    part = add_x(part, recv)

    parts = from_far_z([part] * 3)
    keep_3, send_3 = forward(3)
    far_a, keep_3, send_3, *parts = in_order(far_a, keep_3, send_3, *parts)
    part = add_far_z(part, parts)
    u = part.astype(BF16).astype(F32)
    up_factor_gate = spread(u[:, :R])
    up_factor_up = spread(u[:, R:])

    far_b = across_groups(jnp.concatenate([send_2, send_3], axis=2))
    d_a, pg_a, pu_a = hidden_gradients(
        up_factor_gate,
        up_factor_up,
        b_gate,
        b_up,
        jnp.concatenate([keep_0, keep_1], axis=2),
        far_a,
        hidden_grad,
        0,
    )
    far_b, d_a, pg_a, pu_a = in_order(far_b, d_a, pg_a, pu_a)
    far_a = across_groups(d_a)
    d_b, pg_b, pu_b = hidden_gradients(
        up_factor_gate,
        up_factor_up,
        b_gate,
        b_up,
        jnp.concatenate([keep_2, keep_3], axis=2),
        far_b,
        hidden_grad,
        cuts[2],
    )
    far_a, d_b, pg_b, pu_b = in_order(far_a, d_b, pg_b, pu_b)
    far_b = across_groups(d_b)
    part = jnp.concatenate([select(pg_a + pg_b), select(pu_a + pu_b)], axis=1)
    recv = along_tensor(part, CORE)
    own = jnp.concatenate([d_a, d_b], axis=2)
    gate_lift_gradient = adapter_scale * rows_product(up_factor_gate, own[0])
    far_b, recv, gate_lift_gradient = in_order(far_b, recv, gate_lift_gradient)
    part = add_core(part, recv)
    both = jnp.concatenate([own, jnp.concatenate([far_a, far_b], axis=2)], axis=1)
    dg, du = both[0], both[1]

    count = half // 4

    def backward(c):
        return backward_products(side, dg, du, gate_weight, up_weight, c * count, count)

    recv = along_tensor(part, X)
    keep_0, send_0 = backward(0)
    recv, dg, du, keep_0, send_0 = in_order(recv, dg, du, keep_0, send_0)
    part = add_x(part, recv)

    parts = from_far_z([part] * 3)
    keep_1, send_1 = backward(1)
    dg, du, keep_1, send_1, *parts = in_order(dg, du, keep_1, send_1, *parts)
    part = add_far_z(part, parts)
    g = part.astype(BF16).astype(F32)
    gate_factor_gate = spread(g[:, :R])
    gate_factor_up = spread(g[:, R:])
    moved = (
        adapter_scale
        * (
            flipped_product(gate_factor_gate, a_gate.astype(BF16))
            + flipped_product(gate_factor_up, a_up.astype(BF16))
        )
    ).astype(BF16)
    moved, dg, du = in_order(moved, dg, du)

    width = 2 * count
    far = along_tensor(jnp.concatenate([send_0, send_1], axis=1), CORE)
    far_moved = along_tensor(moved[16:], CORE)
    keep_2, send_2 = backward(2)
    far, far_moved, dg, du, keep_2, send_2 = in_order(far, far_moved, dg, du, keep_2, send_2)
    early = jnp.concatenate([keep_0, keep_1], axis=1) + far.astype(F32)
    moved = jnp.concatenate([moved[:16], far_moved], axis=1)

    def out_of(sums, *extra):
        low = sums.astype(BF16)
        return [
            along_tensor(jnp.concatenate([low[8:16], *extra], axis=1), X),
            across_groups(low[16:24]),
            across_groups(low[24:], X),
        ]

    def joined(sums, parts):
        near = sums[:8] + parts[0][:, :width].astype(F32)
        return jnp.concatenate([near, parts[1].astype(F32) + parts[2].astype(F32)], axis=1)

    parts = out_of(early, moved[8:])
    keep_3, send_3 = backward(3)
    keep_3, send_3, *parts = in_order(keep_3, send_3, *parts)
    early = joined(early, parts)
    moved = jnp.concatenate([moved[:8], parts[0][:, width:]], axis=1)

    far = along_tensor(jnp.concatenate([send_2, send_3], axis=1), CORE)
    low = jnp.concatenate([early.astype(BF16), moved], axis=1)
    parts = from_far_z([low[2 * m : 2 * m + 2] for m in (1, 2, 3)])
    gate_down_gradient = adapter_scale * rows_product(own_cols, gate_factor_gate)
    far, gate_down_gradient, *parts = in_order(far, gate_down_gradient, *parts)
    early = early[:2] + sum(p[:, : 2 * width].astype(F32) for p in parts)
    moved = jnp.stack([moved[:2]] + [p[:, 2 * width :] for p in parts])
    late = jnp.concatenate([keep_2, keep_3], axis=1) + far.astype(F32)

    parts = out_of(late)
    own_cols, gate_factor_up, late = in_order(own_cols, gate_factor_up, late)
    up_down_gradient = adapter_scale * rows_product(own_cols, gate_factor_up)
    up_down_gradient, own, *parts = in_order(up_down_gradient, own, *parts)
    late = joined(late, parts)

    low = late.astype(BF16)
    parts = from_far_z([low[2 * m : 2 * m + 2] for m in (1, 2, 3)])
    up_lift_gradient = adapter_scale * rows_product(up_factor_up, own[1])
    moved = moved.reshape(4, 2, 2, 2, feat_rows).transpose(0, 2, 3, 1, 4).reshape(N, 2 * feat_rows)
    source = jnp.arange(N, dtype=jnp.int32)
    sort = (source[:, None] == (t ^ source)[None, :]).astype(BF16)
    sorted_rows = jnp.dot(sort, moved, preferred_element_type=F32).reshape(N, 2, feat_rows)
    contribution = sorted_rows.transpose(1, 0, 2).reshape(2, d)
    up_lift_gradient, contribution, *parts = in_order(up_lift_gradient, contribution, *parts)
    late = late[:2] + sum(p.astype(F32) for p in parts)
    near = jnp.concatenate([early[:, :width], late[:, :width]], axis=1)
    far = jnp.concatenate([early[:, width:], late[:, width:]], axis=1)
    sums = jnp.where(
        group == 0, jnp.concatenate([near, far], axis=1), jnp.concatenate([far, near], axis=1)
    )
    token_gradient = (sums + contribution).astype(BF16)
    return (
        token_gradient,
        gate_down_gradient,
        up_down_gradient,
        gate_lift_gradient,
        up_lift_gradient,
    )


def solution(mesh):
    sizes = dict(mesh.shape)

    def per_device(*args):
        tokens, b_gate = args[0], args[5]
        fits = (
            sizes["group"] == 2
            and sizes["tensor"] == N
            and tokens.shape[0] == 2
            and b_gate.shape[1] % 1792 == 0
            and tokens.shape[1] % 4096 == 0
        )
        return (shared_device if fits else plain_device)(*args)

    in_specs = (
        P(("group", "tensor"), None),
        P(None, "tensor"),
        P(None, "tensor"),
        P(("group", "tensor"), None),
        P(("group", "tensor"), None),
        P("group", "tensor"),
        P("group", "tensor"),
        P("group"),
        P("group", "tensor"),
    )
    out_specs = (
        P(("group", "tensor"), None),
        P(("group", "tensor"), None),
        P(("group", "tensor"), None),
        P("group", "tensor"),
        P("group", "tensor"),
    )
    return jax.shard_map(
        per_device, mesh=mesh, in_specs=in_specs, out_specs=out_specs, check_vma=False
    )
```

```python
import functools

import jax
import jax.numpy as jnp
from jax import lax
from jax.experimental import pallas as pl
from jax.experimental.pallas import tpu as pltpu
from jax.sharding import PartitionSpec as P

R = 64
AG = 16

adapter_scale = 2.0
BF16 = jnp.bfloat16
F32 = jnp.float32


def agent_mask(agent):
    return (agent[:, None] == jnp.arange(AG, dtype=jnp.int32)[None, :]).astype(jnp.float32)


def select_rank(values, onehot):
    shaped = values.reshape(values.shape[0], AG, R)
    return jnp.sum(shaped * onehot[:, :, None], axis=1)


def spread_rank(small, onehot):
    wide = onehot[:, :, None] * small.astype(jnp.float32)[:, None, :]
    return wide.reshape(small.shape[0], AG * R).astype(jnp.bfloat16)


def flipped_product(left, weight):
    return lax.dot_general(
        left, weight, (((1,), (1,)), ((), ())), preferred_element_type=jnp.float32
    )


def rows_product(left, right):
    return lax.dot_general(
        left, right, (((0,), (0,)), ((), ())), preferred_element_type=jnp.float32
    )


def plain_device(tokens, gate_weight, up_weight, a_gate, a_up, b_gate, b_up, agent, d_hidden):
    onehot = agent_mask(agent)
    feat_rows = a_gate.shape[0]
    feat_start = lax.axis_index("tensor") * feat_rows
    agent_gate_down = a_gate.astype(jnp.bfloat16)
    agent_up_down = a_up.astype(jnp.bfloat16)
    agent_gate_lift = b_gate.astype(jnp.bfloat16)
    agent_up_lift = b_up.astype(jnp.bfloat16)
    complete_result = lax.all_gather(tokens, "tensor", axis=0, tiled=True)
    own_cols = lax.dynamic_slice_in_dim(complete_result, feat_start, feat_rows, 1)
    part_gate = select_rank(
        jnp.dot(own_cols, agent_gate_down, preferred_element_type=jnp.float32), onehot
    )
    part_up = select_rank(
        jnp.dot(own_cols, agent_up_down, preferred_element_type=jnp.float32), onehot
    )
    u_gate, u_up = lax.psum((part_gate, part_up), "tensor")
    up_factor_gate = spread_rank(u_gate.astype(jnp.bfloat16), onehot)
    up_factor_up = spread_rank(u_up.astype(jnp.bfloat16), onehot)
    gate_values = jnp.dot(
        complete_result, gate_weight, preferred_element_type=jnp.float32
    ) + adapter_scale * jnp.dot(up_factor_gate, agent_gate_lift, preferred_element_type=jnp.float32)
    up_values = jnp.dot(
        complete_result, up_weight, preferred_element_type=jnp.float32
    ) + adapter_scale * jnp.dot(up_factor_up, agent_up_lift, preferred_element_type=jnp.float32)
    sig = jax.nn.sigmoid(gate_values)
    hidden_grad = d_hidden.astype(jnp.float32)
    gate_gradient = (hidden_grad * up_values * sig * (1.0 + gate_values * (1.0 - sig))).astype(
        jnp.bfloat16
    )
    up_gradient = (hidden_grad * gate_values * sig).astype(jnp.bfloat16)
    pg_gate = select_rank(flipped_product(gate_gradient, agent_gate_lift), onehot)
    pg_up = select_rank(flipped_product(up_gradient, agent_up_lift), onehot)
    g_gate, g_up = lax.psum((pg_gate, pg_up), "tensor")
    gate_factor_gate = spread_rank(g_gate.astype(jnp.bfloat16), onehot)
    gate_factor_up = spread_rank(g_up.astype(jnp.bfloat16), onehot)
    adapter_contribution = adapter_scale * (
        flipped_product(gate_factor_gate, agent_gate_down)
        + flipped_product(gate_factor_up, agent_up_down)
    )
    base_rows = flipped_product(gate_gradient, gate_weight) + flipped_product(
        up_gradient, up_weight
    )
    joined = lax.dynamic_slice_in_dim(base_rows, feat_start, feat_rows, 1) + adapter_contribution
    token_gradient = lax.psum_scatter(
        lax.dynamic_update_slice_in_dim(base_rows, joined, feat_start, 1),
        "tensor",
        scatter_dimension=0,
        tiled=True,
    ).astype(jnp.bfloat16)
    gate_down_gradient = adapter_scale * rows_product(own_cols, gate_factor_gate)
    up_down_gradient = adapter_scale * rows_product(own_cols, gate_factor_up)
    gate_lift_gradient = adapter_scale * rows_product(up_factor_gate, gate_gradient)
    up_lift_gradient = adapter_scale * rows_product(up_factor_up, up_gradient)
    return (
        token_gradient,
        gate_down_gradient,
        up_down_gradient,
        gate_lift_gradient,
        up_lift_gradient,
    )


def forward_kernel(first, side_ref, x_ref, wg_ref, wu_ref, keep_ref, send_ref, piece, sem):
    pieces, depth, count = piece.shape[1:]
    half = keep_ref.shape[1]
    base = side_ref[0] * (pieces * depth)
    copies = []
    for i, w_ref in enumerate((wg_ref, wu_ref)):
        for k in range(pieces):
            source = pl.ds(pl.multiple_of(base + k * depth, depth), depth)
            copy = pltpu.make_async_copy(
                w_ref.at[source, pl.ds(first, count)], piece.at[i, k], sem.at[i, k]
            )
            copy.start()
            copies.append(copy)
    for i in range(2):
        total = None
        for k in range(pieces):
            copies[i * pieces + k].wait()
            term = jnp.dot(
                x_ref[:, k * depth : (k + 1) * depth], piece[i, k], preferred_element_type=F32
            )
            total = term if total is None else total + term
        keep_ref[i] = total[:half]
        send_ref[i] = total[half:].astype(send_ref.dtype)


def forward_products(side, x, gate_weight, up_weight, first, count, pieces=4):
    rows, depth = x.shape
    vmem = pl.BlockSpec(memory_space=pltpu.VMEM)
    hbm = pl.BlockSpec(memory_space=pltpu.HBM)
    return pl.pallas_call(
        functools.partial(forward_kernel, first),
        in_specs=[pl.BlockSpec(memory_space=pltpu.SMEM), vmem, hbm, hbm],
        out_specs=[vmem] * 2,
        out_shape=[
            jax.ShapeDtypeStruct((2, rows // 2, count), F32),
            jax.ShapeDtypeStruct((2, rows // 2, count), BF16),
        ],
        scratch_shapes=[
            pltpu.VMEM((2, pieces, depth // pieces, count), BF16),
            pltpu.SemaphoreType.DMA((2, pieces)),
        ],
        compiler_params=pltpu.CompilerParams(vmem_limit_bytes=20 << 20),
        cost_estimate=pl.CostEstimate(
            flops=4 * rows * count * depth, bytes_accessed=6 * count * depth, transcendentals=0
        ),
        name="forward_products",
    )(
        side,
        x,
        pltpu.with_memory_space_constraint(gate_weight, pltpu.HBM),
        pltpu.with_memory_space_constraint(up_weight, pltpu.HBM),
    )


def hidden_kernel(
    eug_ref, euu_ref, bg_ref, bu_ref, keep_ref, far_ref, dh_ref, d_ref, pg_ref, pu_ref
):
    @pl.when(pl.program_id(0) == 0)
    def _():
        pg_ref[...] = jnp.zeros_like(pg_ref)
        pu_ref[...] = jnp.zeros_like(pu_ref)

    bg = bg_ref[...].astype(BF16)
    bu = bu_ref[...].astype(BF16)
    gate = (
        keep_ref[0]
        + far_ref[0].astype(F32)
        + adapter_scale * jnp.dot(eug_ref[...], bg, preferred_element_type=F32)
    )
    up = (
        keep_ref[1]
        + far_ref[1].astype(F32)
        + adapter_scale * jnp.dot(euu_ref[...], bu, preferred_element_type=F32)
    )
    sig = jax.nn.sigmoid(gate)
    hidden_grad = dh_ref[...]
    dg = (hidden_grad * up * sig * (1.0 + gate * (1.0 - sig))).astype(BF16)
    du = (hidden_grad * gate * sig).astype(BF16)
    d_ref[0] = dg
    d_ref[1] = du
    pg_ref[...] += flipped_product(dg, bg)
    pu_ref[...] += flipped_product(du, bu)


def hidden_gradients(eug, euu, b_gate, b_up, keep, far, hidden_grad, width=256):
    rows, wide = eug.shape
    count = keep.shape[2]
    fixed = pl.BlockSpec((rows, wide), lambda k: (0, 0))
    b_block = pl.BlockSpec((wide, width), lambda k: (0, k))
    block = pl.BlockSpec((2, rows, width), lambda k: (0, 0, k))
    return pl.pallas_call(
        hidden_kernel,
        grid=(count // width,),
        in_specs=[
            fixed,
            fixed,
            b_block,
            b_block,
            block,
            block,
            pl.BlockSpec((rows, width), lambda k: (0, k)),
        ],
        out_specs=[block, fixed, fixed],
        out_shape=[jax.ShapeDtypeStruct((2, rows, count), BF16)]
        + [jax.ShapeDtypeStruct((rows, wide), F32)] * 2,
        compiler_params=pltpu.CompilerParams(vmem_limit_bytes=20 << 20),
        cost_estimate=pl.CostEstimate(
            flops=8 * rows * wide * count, bytes_accessed=16 * wide * count, transcendentals=0
        ),
        name="hidden_gradients",
    )(
        eug,
        euu,
        pltpu.with_memory_space_constraint(b_gate, pltpu.HBM),
        pltpu.with_memory_space_constraint(b_up, pltpu.HBM),
        keep,
        far,
        hidden_grad,
    )


def backward_kernel(first, side_ref, dg_ref, du_ref, wg_ref, wu_ref, keep_ref, send_ref, rows_ref, sem):
    pieces = sem.shape[1]
    total_rows = rows_ref.shape[1]
    depth = total_rows // pieces
    base = side_ref[0] * (wg_ref.shape[0] // 2) + first
    copies = []
    for k in range(pieces):
        for i, w_ref in enumerate((wg_ref, wu_ref)):
            source = pl.ds(pl.multiple_of(base + k * depth, depth), depth)
            copy = pltpu.make_async_copy(
                w_ref.at[source], rows_ref.at[i, pl.ds(k * depth, depth)], sem.at[i, k]
            )
            copy.start()
            copies.append(copy)
    q = dg_ref.shape[0] // 4
    step = 2 * depth
    for k in range(0, total_rows, step):
        at = 2 * (k // depth)
        for copy in (copies[at], copies[at + 2]):
            copy.wait()
        total = flipped_product(dg_ref[...], rows_ref[0, k : k + step])
        for copy in (copies[at + 1], copies[at + 3]):
            copy.wait()
        total += flipped_product(du_ref[...], rows_ref[1, k : k + step])
        out = pl.ds(k, step)
        keep_ref[:q, out] = total[:q]
        keep_ref[q:, out] = total[2 * q : 3 * q]
        send_ref[:q, out] = total[q : 2 * q].astype(send_ref.dtype)
        send_ref[q:, out] = total[3 * q :].astype(send_ref.dtype)


def backward_products(side, dg, du, gate_weight, up_weight, first, count, depth=256):
    rows, ff = dg.shape
    vmem = pl.BlockSpec(memory_space=pltpu.VMEM)
    hbm = pl.BlockSpec(memory_space=pltpu.HBM)
    return pl.pallas_call(
        functools.partial(backward_kernel, first),
        in_specs=[pl.BlockSpec(memory_space=pltpu.SMEM), vmem, vmem, hbm, hbm],
        out_specs=[vmem] * 2,
        out_shape=[
            jax.ShapeDtypeStruct((rows // 2, count), F32),
            jax.ShapeDtypeStruct((rows // 2, count), BF16),
        ],
        scratch_shapes=[
            pltpu.VMEM((2, count, ff), BF16),
            pltpu.SemaphoreType.DMA((2, count // depth)),
        ],
        compiler_params=pltpu.CompilerParams(vmem_limit_bytes=28 << 20),
        cost_estimate=pl.CostEstimate(
            flops=4 * rows * count * ff, bytes_accessed=6 * count * ff, transcendentals=0
        ),
        name="backward_products",
    )(
        side,
        dg,
        du,
        pltpu.with_memory_space_constraint(gate_weight, pltpu.HBM),
        pltpu.with_memory_space_constraint(up_weight, pltpu.HBM),
    )


N = 16
CORE, X = 1, 2


def along_tensor(value, mask):
    return lax.ppermute(value, "tensor", [(i, i ^ mask) for i in range(N)])


def across_groups(value, mask=0):
    both = ("group", "tensor")
    return lax.ppermute(value, both, [(i, i ^ (N | mask)) for i in range(2 * N)])


def from_far_z(values):
    return [along_tensor(v, 4 * m) for m, v in zip((1, 2, 3), values)]


def in_order(*values):
    return lax.optimization_barrier(values)


def add_core(value, recv):
    half = value.shape[0] // 2
    return value + jnp.concatenate([recv[half:], recv[:half]], axis=0)


def add_x(value, recv):
    q = value.shape[0] // 4
    order = (1, 0, 3, 2)
    return value + jnp.concatenate([recv[o * q : (o + 1) * q] for o in order], axis=0)


def add_z(value, recv, mask):
    shape = value.shape
    v, r = (w.reshape(4, 4, 2, shape[1]) for w in (value, recv))
    return (v + jnp.stack([r[:, q ^ mask] for q in range(4)], axis=1)).reshape(shape)


def shared_device(tokens, gate_weight, up_weight, a_gate, a_up, b_gate, b_up, agent, d_hidden):
    group = lax.axis_index("group")
    t = lax.axis_index("tensor")
    side = group.astype(jnp.int32).reshape(1)
    d = tokens.shape[1]
    half = d // 2
    feat_rows = a_gate.shape[0]
    per_half = half // feat_rows
    rows = 2 * N
    ff = b_gate.shape[1]

    parts = from_far_z([tokens] * 3)
    line = jnp.concatenate([tokens, *parts], axis=0)
    mine = lax.dynamic_slice_in_dim(line, group * half, half, 1)
    other = lax.dynamic_slice_in_dim(line, half - group * half, half, 1)
    parts = [along_tensor(mine, X), across_groups(other), across_groups(other, X)]
    x = jnp.stack(
        [jnp.concatenate([mine, parts[0]], axis=0), jnp.concatenate([parts[1], parts[2]], axis=0)]
    )
    x = jnp.concatenate([x, along_tensor(x, CORE)], axis=1).reshape(2 * rows, half)

    place = jnp.arange(rows, dtype=jnp.int32)
    block = ((place >> 1) & 3) * 4 + ((place >> 3) & 1) * 2 + (place >> 4)
    token_of = ((t ^ block) << 1) + (place & 1)
    shuffle = token_of[:, None] == jnp.arange(rows, dtype=jnp.int32)[None, :]
    agent_here = jnp.sum(jnp.where(shuffle, agent[None, :], 0), axis=1)
    chosen = agent_here[:, None] == (jnp.arange(AG * R, dtype=jnp.int32) // R)[None, :]
    hidden_grad = jnp.dot(shuffle.astype(BF16), d_hidden, preferred_element_type=F32)

    def select(values):
        kept = jnp.where(chosen, values, 0.0)
        pair = sum(kept[:, c : c + 2 * R] for c in range(0, AG * R, 2 * R))
        return pair[:, :R] + pair[:, R:]

    def spread(small):
        wide = jnp.concatenate([small] * AG, axis=1)
        return jnp.where(chosen, wide, 0.0).astype(BF16)

    blocks = lax.dynamic_slice_in_dim(x, (t % per_half) * feat_rows, feat_rows, 1)
    swapped = across_groups(blocks[rows:])
    cuts = [ff * c // 7 for c in (0, 1, 3, 5, 7)]

    def forward(c):
        return forward_products(
            side, x, gate_weight, up_weight, cuts[c], cuts[c + 1] - cuts[c]
        )

    keep_0, send_0 = forward(0)
    swapped, x, keep_0, send_0 = in_order(swapped, x, keep_0, send_0)
    own_cols = jnp.where(t // per_half == group, blocks[:rows], swapped)
    part = jnp.concatenate(
        [
            select(jnp.dot(own_cols, a_gate.astype(BF16), preferred_element_type=F32)),
            select(jnp.dot(own_cols, a_up.astype(BF16), preferred_element_type=F32)),
        ],
        axis=1,
    )

    part = add_core(part, along_tensor(part, CORE))
    part, x = in_order(part, x)
    recv = along_tensor(part, X)
    keep_1, send_1 = forward(1)
    recv, x, keep_1, send_1 = in_order(recv, x, keep_1, send_1)
    part = add_x(part, recv)

    recv = along_tensor(part, 4)
    keep_2, send_2 = forward(2)
    recv, x, keep_2, send_2 = in_order(recv, x, keep_2, send_2)
    part = add_z(part, recv, 1)

    recv = along_tensor(part, 8)
    far_a = across_groups(jnp.concatenate([send_0, send_1, send_2], axis=2))
    keep_3, send_3 = forward(3)
    far_a, recv, keep_3, send_3 = in_order(far_a, recv, keep_3, send_3)
    far_b = across_groups(send_3)
    part = add_z(part, recv, 2)
    u = part.astype(BF16).astype(F32)
    up_factor_gate = spread(u[:, :R])
    up_factor_up = spread(u[:, R:])

    own, pg, pu = hidden_gradients(
        up_factor_gate,
        up_factor_up,
        b_gate,
        b_up,
        jnp.concatenate([keep_0, keep_1, keep_2, keep_3], axis=2),
        jnp.concatenate([far_a, far_b], axis=2),
        hidden_grad,
    )
    far = across_groups(own)
    part = jnp.concatenate([select(pg), select(pu)], axis=1)
    recv = along_tensor(part, CORE)
    gate_lift_gradient = adapter_scale * rows_product(up_factor_gate, own[0])
    far, recv, gate_lift_gradient = in_order(far, recv, gate_lift_gradient)
    part = add_core(part, recv)
    both = jnp.concatenate([own, far], axis=1)
    dg, du = both[0], both[1]

    count = half // 4

    def backward(c, n):
        return backward_products(side, dg, du, gate_weight, up_weight, c * count, n * count)

    recv = along_tensor(part, X)
    keep_0, send_0 = backward(0, 1)
    recv, dg, du, keep_0, send_0 = in_order(recv, dg, du, keep_0, send_0)
    part = add_x(part, recv)

    recv = along_tensor(part, 4)
    keep_1, send_1 = backward(1, 1)
    recv, dg, du, keep_1, send_1 = in_order(recv, dg, du, keep_1, send_1)
    part = add_z(part, recv, 1)

    recv = along_tensor(part, 8)
    keep_2, send_2 = backward(2, 2)
    recv, keep_2, send_2, own, own_cols = in_order(recv, keep_2, send_2, own, own_cols)
    part = add_z(part, recv, 2)
    far = along_tensor(jnp.concatenate([send_0, send_1, send_2], axis=1), CORE)
    g = part.astype(BF16).astype(F32)
    gate_factor_gate = spread(g[:, :R])
    gate_factor_up = spread(g[:, R:])
    moved = (
        adapter_scale
        * (
            flipped_product(gate_factor_gate, a_gate.astype(BF16))
            + flipped_product(gate_factor_up, a_up.astype(BF16))
        )
    ).astype(BF16)

    far_moved = along_tensor(moved[16:], CORE)
    far, far_moved, own_cols = in_order(far, far_moved, own_cols)
    sums = jnp.concatenate([keep_0, keep_1, keep_2], axis=1) + far.astype(F32)
    moved = jnp.concatenate([moved[:16], far_moved], axis=1)

    low = sums.astype(BF16)
    parts = [
        along_tensor(jnp.concatenate([low[8:16], moved[8:]], axis=1), X),
        across_groups(low[16:24]),
        across_groups(low[24:], X),
    ]
    gate_down_gradient = adapter_scale * rows_product(own_cols, gate_factor_gate)
    up_down_gradient = adapter_scale * rows_product(own_cols, gate_factor_up)
    gate_down_gradient, up_down_gradient, own, *parts = in_order(
        gate_down_gradient, up_down_gradient, own, *parts
    )
    near = sums[:8] + parts[0][:, :half].astype(F32)
    sums = jnp.concatenate([near, parts[1].astype(F32) + parts[2].astype(F32)], axis=1)
    moved = jnp.concatenate([moved[:8], parts[0][:, half:]], axis=1)

    low = jnp.concatenate([sums.astype(BF16), moved], axis=1)
    parts = from_far_z([low[2 * m : 2 * m + 2] for m in (1, 2, 3)])
    up_lift_gradient = adapter_scale * rows_product(up_factor_up, own[1])
    up_lift_gradient, *parts = in_order(up_lift_gradient, *parts)
    sums = sums[:2] + sum(p[:, :d].astype(F32) for p in parts)
    moved = jnp.stack([moved[:2]] + [p[:, d:] for p in parts])
    moved = moved.reshape(4, 2, 2, 2, feat_rows).transpose(0, 2, 3, 1, 4).reshape(N, 2 * feat_rows)
    source = jnp.arange(N, dtype=jnp.int32)
    sort = (source[:, None] == (t ^ source)[None, :]).astype(BF16)
    sorted_rows = jnp.dot(sort, moved, preferred_element_type=F32).reshape(N, 2, feat_rows)
    contribution = sorted_rows.transpose(1, 0, 2).reshape(2, d)
    near, far = sums[:, :half], sums[:, half:]
    sums = jnp.where(
        group == 0, jnp.concatenate([near, far], axis=1), jnp.concatenate([far, near], axis=1)
    )
    token_gradient = (sums + contribution).astype(BF16)
    return (
        token_gradient,
        gate_down_gradient,
        up_down_gradient,
        gate_lift_gradient,
        up_lift_gradient,
    )


def solution(mesh):
    sizes = dict(mesh.shape)

    def per_device(*args):
        tokens, b_gate = args[0], args[5]
        fits = (
            sizes["group"] == 2
            and sizes["tensor"] == N
            and tokens.shape[0] == 2
            and b_gate.shape[1] % 1792 == 0
            and tokens.shape[1] % 4096 == 0
        )
        return (shared_device if fits else plain_device)(*args)

    in_specs = (
        P(("group", "tensor"), None),
        P(None, "tensor"),
        P(None, "tensor"),
        P(("group", "tensor"), None),
        P(("group", "tensor"), None),
        P("group", "tensor"),
        P("group", "tensor"),
        P("group"),
        P("group", "tensor"),
    )
    out_specs = (
        P(("group", "tensor"), None),
        P(("group", "tensor"), None),
        P(("group", "tensor"), None),
        P("group", "tensor"),
        P("group", "tensor"),
    )
    return jax.shard_map(
        per_device, mesh=mesh, in_specs=in_specs, out_specs=out_specs, check_vma=False
    )
```

```python
import functools

import jax
import jax.numpy as jnp
from jax import lax
from jax.experimental import pallas as pl
from jax.experimental.pallas import tpu as pltpu
from jax.sharding import PartitionSpec as P

R = 64
AG = 16

adapter_scale = 2.0
BF16 = jnp.bfloat16
F32 = jnp.float32


def agent_mask(agent):
    return (agent[:, None] == jnp.arange(AG, dtype=jnp.int32)[None, :]).astype(jnp.float32)


def select_rank(values, onehot):
    shaped = values.reshape(values.shape[0], AG, R)
    return jnp.sum(shaped * onehot[:, :, None], axis=1)


def spread_rank(small, onehot):
    wide = onehot[:, :, None] * small.astype(jnp.float32)[:, None, :]
    return wide.reshape(small.shape[0], AG * R).astype(jnp.bfloat16)


def flipped_product(left, weight):
    return lax.dot_general(
        left, weight, (((1,), (1,)), ((), ())), preferred_element_type=jnp.float32
    )


def rows_product(left, right):
    return lax.dot_general(
        left, right, (((0,), (0,)), ((), ())), preferred_element_type=jnp.float32
    )


def plain_device(tokens, gate_weight, up_weight, a_gate, a_up, b_gate, b_up, agent, d_hidden):
    onehot = agent_mask(agent)
    feat_rows = a_gate.shape[0]
    feat_start = lax.axis_index("tensor") * feat_rows
    agent_gate_down = a_gate.astype(jnp.bfloat16)
    agent_up_down = a_up.astype(jnp.bfloat16)
    agent_gate_lift = b_gate.astype(jnp.bfloat16)
    agent_up_lift = b_up.astype(jnp.bfloat16)
    complete_result = lax.all_gather(tokens, "tensor", axis=0, tiled=True)
    own_cols = lax.dynamic_slice_in_dim(complete_result, feat_start, feat_rows, 1)
    part_gate = select_rank(
        jnp.dot(own_cols, agent_gate_down, preferred_element_type=jnp.float32), onehot
    )
    part_up = select_rank(
        jnp.dot(own_cols, agent_up_down, preferred_element_type=jnp.float32), onehot
    )
    u_gate, u_up = lax.psum((part_gate, part_up), "tensor")
    up_factor_gate = spread_rank(u_gate.astype(jnp.bfloat16), onehot)
    up_factor_up = spread_rank(u_up.astype(jnp.bfloat16), onehot)
    gate_values = jnp.dot(
        complete_result, gate_weight, preferred_element_type=jnp.float32
    ) + adapter_scale * jnp.dot(up_factor_gate, agent_gate_lift, preferred_element_type=jnp.float32)
    up_values = jnp.dot(
        complete_result, up_weight, preferred_element_type=jnp.float32
    ) + adapter_scale * jnp.dot(up_factor_up, agent_up_lift, preferred_element_type=jnp.float32)
    sig = jax.nn.sigmoid(gate_values)
    hidden_grad = d_hidden.astype(jnp.float32)
    gate_gradient = (hidden_grad * up_values * sig * (1.0 + gate_values * (1.0 - sig))).astype(
        jnp.bfloat16
    )
    up_gradient = (hidden_grad * gate_values * sig).astype(jnp.bfloat16)
    pg_gate = select_rank(flipped_product(gate_gradient, agent_gate_lift), onehot)
    pg_up = select_rank(flipped_product(up_gradient, agent_up_lift), onehot)
    g_gate, g_up = lax.psum((pg_gate, pg_up), "tensor")
    gate_factor_gate = spread_rank(g_gate.astype(jnp.bfloat16), onehot)
    gate_factor_up = spread_rank(g_up.astype(jnp.bfloat16), onehot)
    adapter_contribution = adapter_scale * (
        flipped_product(gate_factor_gate, agent_gate_down)
        + flipped_product(gate_factor_up, agent_up_down)
    )
    base_rows = flipped_product(gate_gradient, gate_weight) + flipped_product(
        up_gradient, up_weight
    )
    joined = lax.dynamic_slice_in_dim(base_rows, feat_start, feat_rows, 1) + adapter_contribution
    token_gradient = lax.psum_scatter(
        lax.dynamic_update_slice_in_dim(base_rows, joined, feat_start, 1),
        "tensor",
        scatter_dimension=0,
        tiled=True,
    ).astype(jnp.bfloat16)
    gate_down_gradient = adapter_scale * rows_product(own_cols, gate_factor_gate)
    up_down_gradient = adapter_scale * rows_product(own_cols, gate_factor_up)
    gate_lift_gradient = adapter_scale * rows_product(up_factor_gate, gate_gradient)
    up_lift_gradient = adapter_scale * rows_product(up_factor_up, up_gradient)
    return (
        token_gradient,
        gate_down_gradient,
        up_down_gradient,
        gate_lift_gradient,
        up_lift_gradient,
    )


def forward_kernel(first, side_ref, x_ref, wg_ref, wu_ref, keep_ref, send_ref, piece, sem):
    pieces, depth, count = piece.shape[1:]
    half = keep_ref.shape[1]
    base = side_ref[0] * (pieces * depth)
    copies = []
    for i, w_ref in enumerate((wg_ref, wu_ref)):
        for k in range(pieces):
            source = pl.ds(pl.multiple_of(base + k * depth, depth), depth)
            copy = pltpu.make_async_copy(
                w_ref.at[source, pl.ds(first, count)], piece.at[i, k], sem.at[i, k]
            )
            copy.start()
            copies.append(copy)
    for i in range(2):
        total = None
        for k in range(pieces):
            copies[i * pieces + k].wait()
            term = jnp.dot(
                x_ref[:, k * depth : (k + 1) * depth], piece[i, k], preferred_element_type=F32
            )
            total = term if total is None else total + term
        keep_ref[i] = total[:half]
        send_ref[i] = total[half:].astype(send_ref.dtype)


def forward_products(side, x, gate_weight, up_weight, first, count, pieces=4):
    rows, depth = x.shape
    vmem = pl.BlockSpec(memory_space=pltpu.VMEM)
    hbm = pl.BlockSpec(memory_space=pltpu.HBM)
    return pl.pallas_call(
        functools.partial(forward_kernel, first),
        in_specs=[pl.BlockSpec(memory_space=pltpu.SMEM), vmem, hbm, hbm],
        out_specs=[vmem] * 2,
        out_shape=[
            jax.ShapeDtypeStruct((2, rows // 2, count), F32),
            jax.ShapeDtypeStruct((2, rows // 2, count), BF16),
        ],
        scratch_shapes=[
            pltpu.VMEM((2, pieces, depth // pieces, count), BF16),
            pltpu.SemaphoreType.DMA((2, pieces)),
        ],
        compiler_params=pltpu.CompilerParams(vmem_limit_bytes=20 << 20),
        cost_estimate=pl.CostEstimate(
            flops=4 * rows * count * depth, bytes_accessed=6 * count * depth, transcendentals=0
        ),
        name="forward_products",
    )(
        side,
        x,
        pltpu.with_memory_space_constraint(gate_weight, pltpu.HBM),
        pltpu.with_memory_space_constraint(up_weight, pltpu.HBM),
    )


def hidden_kernel(
    eug_ref, euu_ref, bg_ref, bu_ref, keep_ref, far_ref, dh_ref, d_ref, pg_ref, pu_ref
):
    @pl.when(pl.program_id(0) == 0)
    def _():
        pg_ref[...] = jnp.zeros_like(pg_ref)
        pu_ref[...] = jnp.zeros_like(pu_ref)

    bg = bg_ref[...].astype(BF16)
    bu = bu_ref[...].astype(BF16)
    gate = (
        keep_ref[0]
        + far_ref[0].astype(F32)
        + adapter_scale * jnp.dot(eug_ref[...], bg, preferred_element_type=F32)
    )
    up = (
        keep_ref[1]
        + far_ref[1].astype(F32)
        + adapter_scale * jnp.dot(euu_ref[...], bu, preferred_element_type=F32)
    )
    sig = jax.nn.sigmoid(gate)
    hidden_grad = dh_ref[...]
    dg = (hidden_grad * up * sig * (1.0 + gate * (1.0 - sig))).astype(BF16)
    du = (hidden_grad * gate * sig).astype(BF16)
    d_ref[0] = dg
    d_ref[1] = du
    pg_ref[...] += flipped_product(dg, bg)
    pu_ref[...] += flipped_product(du, bu)


def hidden_gradients(eug, euu, b_gate, b_up, keep, far, hidden_grad, first, width):
    rows, wide = eug.shape
    count = keep.shape[2]
    start = first // width
    fixed = pl.BlockSpec((rows, wide), lambda k: (0, 0))
    b_block = pl.BlockSpec((wide, width), lambda k: (0, k + start))
    block = pl.BlockSpec((2, rows, width), lambda k: (0, 0, k))
    return pl.pallas_call(
        hidden_kernel,
        grid=(count // width,),
        in_specs=[
            fixed,
            fixed,
            b_block,
            b_block,
            block,
            block,
            pl.BlockSpec((rows, width), lambda k: (0, k + start)),
        ],
        out_specs=[block, fixed, fixed],
        out_shape=[jax.ShapeDtypeStruct((2, rows, count), BF16)]
        + [jax.ShapeDtypeStruct((rows, wide), F32)] * 2,
        compiler_params=pltpu.CompilerParams(vmem_limit_bytes=20 << 20),
        cost_estimate=pl.CostEstimate(
            flops=8 * rows * wide * count, bytes_accessed=16 * wide * count, transcendentals=0
        ),
        name="hidden_gradients",
    )(
        eug,
        euu,
        pltpu.with_memory_space_constraint(b_gate, pltpu.HBM),
        pltpu.with_memory_space_constraint(b_up, pltpu.HBM),
        keep,
        far,
        hidden_grad,
    )


def backward_kernel(first, side_ref, dg_ref, du_ref, wg_ref, wu_ref, keep_ref, send_ref, rows_ref, sem):
    pieces = sem.shape[1]
    total_rows = rows_ref.shape[1]
    depth = total_rows // pieces
    base = side_ref[0] * (wg_ref.shape[0] // 2) + first
    copies = {}
    for k in range(0, pieces, 2):
        for i, w_ref in enumerate((wg_ref, wu_ref)):
            for j in (k, k + 1):
                source = pl.ds(pl.multiple_of(base + j * depth, depth), depth)
                copies[i, j] = pltpu.make_async_copy(
                    w_ref.at[source], rows_ref.at[i, pl.ds(j * depth, depth)], sem.at[i, j]
                )
                copies[i, j].start()
    q = dg_ref.shape[0] // 4
    step = 2 * depth
    for k in range(0, total_rows, step):
        j = k // depth
        copies[0, j].wait()
        copies[0, j + 1].wait()
        total = flipped_product(dg_ref[...], rows_ref[0, k : k + step])
        copies[1, j].wait()
        copies[1, j + 1].wait()
        total += flipped_product(du_ref[...], rows_ref[1, k : k + step])
        out = pl.ds(k, step)
        keep_ref[:q, out] = total[:q]
        keep_ref[q:, out] = total[2 * q : 3 * q]
        send_ref[:q, out] = total[q : 2 * q].astype(send_ref.dtype)
        send_ref[q:, out] = total[3 * q :].astype(send_ref.dtype)


def backward_products(side, dg, du, gate_weight, up_weight, first, count, depth=256):
    rows, ff = dg.shape
    vmem = pl.BlockSpec(memory_space=pltpu.VMEM)
    hbm = pl.BlockSpec(memory_space=pltpu.HBM)
    return pl.pallas_call(
        functools.partial(backward_kernel, first),
        in_specs=[pl.BlockSpec(memory_space=pltpu.SMEM), vmem, vmem, hbm, hbm],
        out_specs=[vmem] * 2,
        out_shape=[
            jax.ShapeDtypeStruct((rows // 2, count), F32),
            jax.ShapeDtypeStruct((rows // 2, count), BF16),
        ],
        scratch_shapes=[
            pltpu.VMEM((2, count, ff), BF16),
            pltpu.SemaphoreType.DMA((2, count // depth)),
        ],
        compiler_params=pltpu.CompilerParams(vmem_limit_bytes=28 << 20),
        cost_estimate=pl.CostEstimate(
            flops=4 * rows * count * ff, bytes_accessed=6 * count * ff, transcendentals=0
        ),
        name="backward_products",
    )(
        side,
        dg,
        du,
        pltpu.with_memory_space_constraint(gate_weight, pltpu.HBM),
        pltpu.with_memory_space_constraint(up_weight, pltpu.HBM),
    )


N = 16
CORE, X = 1, 2


def along_tensor(value, mask):
    return lax.ppermute(value, "tensor", [(i, i ^ mask) for i in range(N)])


def across_groups(value, mask=0):
    both = ("group", "tensor")
    return lax.ppermute(value, both, [(i, i ^ (N | mask)) for i in range(2 * N)])


def from_far_z(values):
    return [along_tensor(v, 4 * m) for m, v in zip((1, 2, 3), values)]


def in_order(*values):
    return lax.optimization_barrier(values)


def add_core(value, recv):
    half = value.shape[0] // 2
    return value + jnp.concatenate([recv[half:], recv[:half]], axis=0)


def add_x(value, recv):
    q = value.shape[0] // 4
    order = (1, 0, 3, 2)
    return value + jnp.concatenate([recv[o * q : (o + 1) * q] for o in order], axis=0)


def add_z(value, recv, mask):
    shape = value.shape
    v, r = (w.reshape(4, 4, 2, shape[1]) for w in (value, recv))
    return (v + jnp.stack([r[:, q ^ mask] for q in range(4)], axis=1)).reshape(shape)


def shared_device(tokens, gate_weight, up_weight, a_gate, a_up, b_gate, b_up, agent, d_hidden):
    group = lax.axis_index("group")
    t = lax.axis_index("tensor")
    side = group.astype(jnp.int32).reshape(1)
    d = tokens.shape[1]
    half = d // 2
    feat_rows = a_gate.shape[0]
    per_half = half // feat_rows
    rows = 2 * N
    ff = b_gate.shape[1]

    line = jnp.concatenate([tokens, along_tensor(tokens, 4)], axis=0)
    line = jnp.concatenate([line, along_tensor(line, 8)], axis=0)
    mine = lax.dynamic_slice_in_dim(line, group * half, half, 1)
    other = lax.dynamic_slice_in_dim(line, half - group * half, half, 1)
    parts = [along_tensor(mine, X), across_groups(other), across_groups(other, X)]
    x = jnp.stack(
        [jnp.concatenate([mine, parts[0]], axis=0), jnp.concatenate([parts[1], parts[2]], axis=0)]
    )
    x = jnp.concatenate([x, along_tensor(x, CORE)], axis=1).reshape(2 * rows, half)

    place = jnp.arange(rows, dtype=jnp.int32)
    block = ((place >> 1) & 3) * 4 + ((place >> 3) & 1) * 2 + (place >> 4)
    token_of = ((t ^ block) << 1) + (place & 1)
    shuffle = token_of[:, None] == jnp.arange(rows, dtype=jnp.int32)[None, :]
    agent_here = jnp.sum(jnp.where(shuffle, agent[None, :], 0), axis=1)
    chosen = agent_here[:, None] == (jnp.arange(AG * R, dtype=jnp.int32) // R)[None, :]
    hidden_grad = jnp.dot(shuffle.astype(BF16), d_hidden, preferred_element_type=F32)

    def select(values):
        kept = jnp.where(chosen, values, 0.0)
        pair = sum(kept[:, c : c + 2 * R] for c in range(0, AG * R, 2 * R))
        return pair[:, :R] + pair[:, R:]

    def spread(small):
        wide = jnp.concatenate([small] * AG, axis=1)
        return jnp.where(chosen, wide, 0.0).astype(BF16)

    blocks = lax.dynamic_slice_in_dim(x, (t % per_half) * feat_rows, feat_rows, 1)
    swapped = across_groups(blocks[rows:])
    cuts = [ff * c // 7 for c in (0, 2, 4, 6, 7)]

    def forward(c):
        return forward_products(
            side, x, gate_weight, up_weight, cuts[c], cuts[c + 1] - cuts[c]
        )

    keep_0, send_0 = forward(0)
    swapped, x, keep_0, send_0 = in_order(swapped, x, keep_0, send_0)
    own_cols = jnp.where(t // per_half == group, blocks[:rows], swapped)
    part = jnp.concatenate(
        [
            select(jnp.dot(own_cols, a_gate.astype(BF16), preferred_element_type=F32)),
            select(jnp.dot(own_cols, a_up.astype(BF16), preferred_element_type=F32)),
        ],
        axis=1,
    )

    part = add_core(part, along_tensor(part, CORE))
    part, x = in_order(part, x)
    recv = along_tensor(part, X)
    keep_1, send_1 = forward(1)
    recv, x, keep_1, send_1 = in_order(recv, x, keep_1, send_1)
    part = add_x(part, recv)

    recv = along_tensor(part, 4)
    keep_2, send_2 = forward(2)
    recv, x, keep_2, send_2 = in_order(recv, x, keep_2, send_2)
    part = add_z(part, recv, 1)

    recv = along_tensor(part, 8)
    far_a = across_groups(jnp.concatenate([send_0, send_1, send_2], axis=2))
    keep_3, send_3 = forward(3)
    far_a, recv, keep_3, send_3 = in_order(far_a, recv, keep_3, send_3)
    far_b = across_groups(send_3)
    part = add_z(part, recv, 2)
    u = part.astype(BF16).astype(F32)
    up_factor_gate = spread(u[:, :R])
    up_factor_up = spread(u[:, R:])

    def hidden(keep, far, first, width):
        return hidden_gradients(
            up_factor_gate, up_factor_up, b_gate, b_up, keep, far, hidden_grad, first, width
        )

    keep = jnp.concatenate([keep_0, keep_1, keep_2], axis=2)
    own_a, pg_a, pu_a = hidden(keep, far_a, 0, 512)
    far_b, own_a = in_order(far_b, own_a)
    own_b, pg_b, pu_b = hidden(keep_3, far_b, cuts[3], 256)
    own = jnp.concatenate([own_a, own_b], axis=2)
    far = across_groups(own)
    part = jnp.concatenate([select(pg_a + pg_b), select(pu_a + pu_b)], axis=1)
    part, own = in_order(part, own)
    recv = along_tensor(part, CORE)
    gate_lift_gradient = adapter_scale * rows_product(up_factor_gate, own[0])
    far, recv, gate_lift_gradient = in_order(far, recv, gate_lift_gradient)
    part = add_core(part, recv)
    both = jnp.concatenate([own, far], axis=1)
    dg, du = both[0], both[1]

    count = half // 4

    def backward(c, n):
        return backward_products(side, dg, du, gate_weight, up_weight, c * count, n * count)

    recv = along_tensor(part, X)
    keep_0, send_0 = backward(0, 1)
    recv, dg, du, keep_0, send_0 = in_order(recv, dg, du, keep_0, send_0)
    part = add_x(part, recv)

    recv = along_tensor(part, 4)
    keep_1, send_1 = backward(1, 1)
    recv, dg, du, keep_1, send_1 = in_order(recv, dg, du, keep_1, send_1)
    part = add_z(part, recv, 1)

    recv = along_tensor(part, 8)
    keep_2, send_2 = backward(2, 2)
    recv, keep_2, send_2, own, own_cols = in_order(recv, keep_2, send_2, own, own_cols)
    part = add_z(part, recv, 2)
    far = along_tensor(jnp.concatenate([send_0, send_1, send_2], axis=1), CORE)
    g = part.astype(BF16).astype(F32)
    gate_factor_gate = spread(g[:, :R])
    gate_factor_up = spread(g[:, R:])
    moved = (
        adapter_scale
        * (
            flipped_product(gate_factor_gate, a_gate.astype(BF16))
            + flipped_product(gate_factor_up, a_up.astype(BF16))
        )
    ).astype(BF16)

    far_moved = along_tensor(moved[16:], CORE)
    far, far_moved, own_cols = in_order(far, far_moved, own_cols)
    sums = jnp.concatenate([keep_0, keep_1, keep_2], axis=1) + far.astype(F32)
    moved = jnp.concatenate([moved[:16], far_moved], axis=1)

    low = sums.astype(BF16)
    parts = [
        along_tensor(jnp.concatenate([low[8:16], moved[8:]], axis=1), X),
        across_groups(low[16:24]),
        across_groups(low[24:], X),
    ]
    gate_down_gradient = adapter_scale * rows_product(own_cols, gate_factor_gate)
    up_down_gradient = adapter_scale * rows_product(own_cols, gate_factor_up)
    gate_down_gradient, up_down_gradient, own, *parts = in_order(
        gate_down_gradient, up_down_gradient, own, *parts
    )
    near = sums[:8] + parts[0][:, :half].astype(F32)
    sums = jnp.concatenate([near, parts[1].astype(F32) + parts[2].astype(F32)], axis=1)
    moved = jnp.concatenate([moved[:8], parts[0][:, half:]], axis=1)

    low = jnp.concatenate([sums.astype(BF16), moved], axis=1)
    parts = from_far_z([low[2 * m : 2 * m + 2] for m in (1, 2, 3)])
    up_lift_gradient = adapter_scale * rows_product(up_factor_up, own[1])
    up_lift_gradient, *parts = in_order(up_lift_gradient, *parts)
    sums = sums[:2] + sum(p[:, :d].astype(F32) for p in parts)
    moved = jnp.stack([moved[:2]] + [p[:, d:] for p in parts])
    moved = moved.reshape(4, 2, 2, 2, feat_rows).transpose(0, 2, 3, 1, 4).reshape(N, 2 * feat_rows)
    source = jnp.arange(N, dtype=jnp.int32)
    sort = (source[:, None] == (t ^ source)[None, :]).astype(BF16)
    sorted_rows = jnp.dot(sort, moved, preferred_element_type=F32).reshape(N, 2, feat_rows)
    contribution = sorted_rows.transpose(1, 0, 2).reshape(2, d)
    near, far = sums[:, :half], sums[:, half:]
    sums = jnp.where(
        group == 0, jnp.concatenate([near, far], axis=1), jnp.concatenate([far, near], axis=1)
    )
    token_gradient = (sums + contribution).astype(BF16)
    return (
        token_gradient,
        gate_down_gradient,
        up_down_gradient,
        gate_lift_gradient,
        up_lift_gradient,
    )


def solution(mesh):
    sizes = dict(mesh.shape)

    def per_device(*args):
        tokens, b_gate = args[0], args[5]
        fits = (
            sizes["group"] == 2
            and sizes["tensor"] == N
            and tokens.shape[0] == 2
            and b_gate.shape[1] % 1792 == 0
            and tokens.shape[1] % 4096 == 0
        )
        return (shared_device if fits else plain_device)(*args)

    in_specs = (
        P(("group", "tensor"), None),
        P(None, "tensor"),
        P(None, "tensor"),
        P(("group", "tensor"), None),
        P(("group", "tensor"), None),
        P("group", "tensor"),
        P("group", "tensor"),
        P("group"),
        P("group", "tensor"),
    )
    out_specs = (
        P(("group", "tensor"), None),
        P(("group", "tensor"), None),
        P(("group", "tensor"), None),
        P("group", "tensor"),
        P("group", "tensor"),
    )
    return jax.shard_map(
        per_device, mesh=mesh, in_specs=in_specs, out_specs=out_specs, check_vma=False
    )
```

```python
import functools

import jax
import jax.numpy as jnp
from jax import lax
from jax.experimental import pallas as pl
from jax.experimental.pallas import tpu as pltpu
from jax.sharding import PartitionSpec as P

R = 64
AG = 16

adapter_scale = 2.0
BF16 = jnp.bfloat16
F32 = jnp.float32


def agent_mask(agent):
    return (agent[:, None] == jnp.arange(AG, dtype=jnp.int32)[None, :]).astype(jnp.float32)


def select_rank(values, onehot):
    shaped = values.reshape(values.shape[0], AG, R)
    return jnp.sum(shaped * onehot[:, :, None], axis=1)


def spread_rank(small, onehot):
    wide = onehot[:, :, None] * small.astype(jnp.float32)[:, None, :]
    return wide.reshape(small.shape[0], AG * R).astype(jnp.bfloat16)


def flipped_product(left, weight):
    return lax.dot_general(
        left, weight, (((1,), (1,)), ((), ())), preferred_element_type=jnp.float32
    )


def rows_product(left, right):
    return lax.dot_general(
        left, right, (((0,), (0,)), ((), ())), preferred_element_type=jnp.float32
    )


def plain_device(tokens, gate_weight, up_weight, a_gate, a_up, b_gate, b_up, agent, d_hidden):
    onehot = agent_mask(agent)
    feat_rows = a_gate.shape[0]
    feat_start = lax.axis_index("tensor") * feat_rows
    agent_gate_down = a_gate.astype(jnp.bfloat16)
    agent_up_down = a_up.astype(jnp.bfloat16)
    agent_gate_lift = b_gate.astype(jnp.bfloat16)
    agent_up_lift = b_up.astype(jnp.bfloat16)
    complete_result = lax.all_gather(tokens, "tensor", axis=0, tiled=True)
    own_cols = lax.dynamic_slice_in_dim(complete_result, feat_start, feat_rows, 1)
    part_gate = select_rank(
        jnp.dot(own_cols, agent_gate_down, preferred_element_type=jnp.float32), onehot
    )
    part_up = select_rank(
        jnp.dot(own_cols, agent_up_down, preferred_element_type=jnp.float32), onehot
    )
    u_gate, u_up = lax.psum((part_gate, part_up), "tensor")
    up_factor_gate = spread_rank(u_gate.astype(jnp.bfloat16), onehot)
    up_factor_up = spread_rank(u_up.astype(jnp.bfloat16), onehot)
    gate_values = jnp.dot(
        complete_result, gate_weight, preferred_element_type=jnp.float32
    ) + adapter_scale * jnp.dot(up_factor_gate, agent_gate_lift, preferred_element_type=jnp.float32)
    up_values = jnp.dot(
        complete_result, up_weight, preferred_element_type=jnp.float32
    ) + adapter_scale * jnp.dot(up_factor_up, agent_up_lift, preferred_element_type=jnp.float32)
    sig = jax.nn.sigmoid(gate_values)
    hidden_grad = d_hidden.astype(jnp.float32)
    gate_gradient = (hidden_grad * up_values * sig * (1.0 + gate_values * (1.0 - sig))).astype(
        jnp.bfloat16
    )
    up_gradient = (hidden_grad * gate_values * sig).astype(jnp.bfloat16)
    pg_gate = select_rank(flipped_product(gate_gradient, agent_gate_lift), onehot)
    pg_up = select_rank(flipped_product(up_gradient, agent_up_lift), onehot)
    g_gate, g_up = lax.psum((pg_gate, pg_up), "tensor")
    gate_factor_gate = spread_rank(g_gate.astype(jnp.bfloat16), onehot)
    gate_factor_up = spread_rank(g_up.astype(jnp.bfloat16), onehot)
    adapter_contribution = adapter_scale * (
        flipped_product(gate_factor_gate, agent_gate_down)
        + flipped_product(gate_factor_up, agent_up_down)
    )
    base_rows = flipped_product(gate_gradient, gate_weight) + flipped_product(
        up_gradient, up_weight
    )
    joined = lax.dynamic_slice_in_dim(base_rows, feat_start, feat_rows, 1) + adapter_contribution
    token_gradient = lax.psum_scatter(
        lax.dynamic_update_slice_in_dim(base_rows, joined, feat_start, 1),
        "tensor",
        scatter_dimension=0,
        tiled=True,
    ).astype(jnp.bfloat16)
    gate_down_gradient = adapter_scale * rows_product(own_cols, gate_factor_gate)
    up_down_gradient = adapter_scale * rows_product(own_cols, gate_factor_up)
    gate_lift_gradient = adapter_scale * rows_product(up_factor_gate, gate_gradient)
    up_lift_gradient = adapter_scale * rows_product(up_factor_up, up_gradient)
    return (
        token_gradient,
        gate_down_gradient,
        up_down_gradient,
        gate_lift_gradient,
        up_lift_gradient,
    )


def columns_copies(side_ref, first, w_refs, out_ref, sem):
    depth, count = out_ref.shape[1:]
    source = pl.ds(pl.multiple_of(side_ref[0] * depth, depth), depth)
    return [
        pltpu.make_async_copy(w_ref.at[source, pl.ds(first, count)], out_ref.at[i], sem.at[i])
        for i, w_ref in enumerate(w_refs)
    ]


def rows_copies(side_ref, first, w_refs, out_ref, sem):
    count = out_ref.shape[1]
    start = side_ref[0] * (w_refs[0].shape[0] // 2) + first
    source = pl.ds(pl.multiple_of(start, 16), count)
    return [
        pltpu.make_async_copy(w_ref.at[source], out_ref.at[i], sem.at[i])
        for i, w_ref in enumerate(w_refs)
    ]


VMEM = pl.BlockSpec(memory_space=pltpu.VMEM)
HBM = pl.BlockSpec(memory_space=pltpu.HBM)
SMEM = pl.BlockSpec(memory_space=pltpu.SMEM)
ANYWHERE = pl.BlockSpec(memory_space=pl.ANY)
PAIR = pltpu.SemaphoreType.DMA((2,))


def weights_in_hbm(side, gate_weight, up_weight):
    return (
        side,
        pltpu.with_memory_space_constraint(gate_weight, pltpu.HBM),
        pltpu.with_memory_space_constraint(up_weight, pltpu.HBM),
    )


def cost(products, bytes_moved):
    return pl.CostEstimate(flops=2 * products, bytes_accessed=bytes_moved, transcendentals=0)


def first_kernel(side_ref, wg_ref, wu_ref, next_ref, sem):
    copies = columns_copies(side_ref, 0, (wg_ref, wu_ref), next_ref, sem)
    for copy in copies:
        copy.start()
    for copy in copies:
        copy.wait()


def first_columns(weights, count):
    depth = weights[1].shape[0] // 2
    return pl.pallas_call(
        first_kernel,
        in_specs=[SMEM, HBM, HBM],
        out_specs=ANYWHERE,
        out_shape=pltpu.VMEM((2, depth, count), BF16),
        scratch_shapes=[PAIR],
        compiler_params=pltpu.CompilerParams(vmem_limit_bytes=2 << 20),
        cost_estimate=cost(0, 4 * depth * count),
        name="first_columns",
    )(*weights)


def forward_kernel(after, side_ref, x_ref, w_ref, wg_ref, wu_ref, keep_ref, send_ref, *rest):
    copies = columns_copies(side_ref, after, (wg_ref, wu_ref), *rest) if rest else []
    for copy in copies:
        copy.start()
    half = keep_ref.shape[1]
    for i in range(2):
        total = jnp.dot(x_ref[...], w_ref[i], preferred_element_type=F32)
        keep_ref[i] = total[:half]
        send_ref[i] = total[half:].astype(send_ref.dtype)
    for copy in copies:
        copy.wait()


def forward_products(weights, x, w, after, count_after):
    rows, depth = x.shape
    count = w.shape[2]
    side, gate_weight, up_weight = weights
    follow = count_after > 0
    return pl.pallas_call(
        functools.partial(forward_kernel, after),
        in_specs=[SMEM, VMEM, VMEM, HBM, HBM],
        out_specs=[VMEM] * 2 + [ANYWHERE] * follow,
        out_shape=[
            jax.ShapeDtypeStruct((2, rows // 2, count), F32),
            jax.ShapeDtypeStruct((2, rows // 2, count), BF16),
        ]
        + [pltpu.VMEM((2, depth, count_after), BF16)] * follow,
        scratch_shapes=[PAIR] * follow,
        compiler_params=pltpu.CompilerParams(vmem_limit_bytes=8 << 20),
        cost_estimate=cost(2 * rows * count * depth, 6 * count * depth),
        name="forward_products",
    )(side, x, w, gate_weight, up_weight)


def narrow_kernel(g_ref, u_ref, g16_ref, u16_ref):
    g16_ref[...] = g_ref[...].astype(BF16)
    u16_ref[...] = u_ref[...].astype(BF16)


def narrow(gate, up, depth):
    rows, width = gate.shape
    block = pl.BlockSpec((depth, width), lambda k: (k, 0))
    return pl.pallas_call(
        narrow_kernel,
        grid=(rows // depth,),
        in_specs=[block] * 2,
        out_specs=[block] * 2,
        out_shape=[jax.ShapeDtypeStruct(gate.shape, BF16)] * 2,
        compiler_params=pltpu.CompilerParams(vmem_limit_bytes=16 << 20),
        cost_estimate=cost(0, 12 * rows * width),
        name="narrow",
    )(
        pltpu.with_memory_space_constraint(gate, pltpu.HBM),
        pltpu.with_memory_space_constraint(up, pltpu.HBM),
    )


def hidden_kernel(
    side_ref, wg_ref, wu_ref, eug_ref, euu_ref, bg_ref, bu_ref, keep_ref, far_ref, dh_ref, d_ref,
    pg_ref, pu_ref, *rest
):
    def copies():
        return rows_copies(side_ref, 0, (wg_ref, wu_ref), *rest) if rest else []

    @pl.when(pl.program_id(0) == 0)
    def _():
        for copy in copies():
            copy.start()
        pg_ref[...] = jnp.zeros_like(pg_ref)
        pu_ref[...] = jnp.zeros_like(pu_ref)

    bg, bu = bg_ref[...], bu_ref[...]
    gate = (
        keep_ref[0]
        + far_ref[0].astype(F32)
        + adapter_scale * jnp.dot(eug_ref[...], bg, preferred_element_type=F32)
    )
    up = (
        keep_ref[1]
        + far_ref[1].astype(F32)
        + adapter_scale * jnp.dot(euu_ref[...], bu, preferred_element_type=F32)
    )
    sig = jax.nn.sigmoid(gate)
    hidden_grad = dh_ref[...]
    dg = (hidden_grad * up * sig * (1.0 + gate * (1.0 - sig))).astype(BF16)
    du = (hidden_grad * gate * sig).astype(BF16)
    d_ref[0] = dg
    d_ref[1] = du
    pg_ref[...] += flipped_product(dg, bg)
    pu_ref[...] += flipped_product(du, bu)

    @pl.when(pl.program_id(0) == pl.num_programs(0) - 1)
    def _():
        for copy in copies():
            copy.wait()


def hidden_gradients(weights, eug, euu, b_gate, b_up, keep, far, hidden_grad, first, width, count_after):
    rows, wide = eug.shape
    count = keep.shape[2]
    start = first // width
    follow = count_after > 0
    fixed = pl.BlockSpec((rows, wide), lambda k: (0, 0))
    b_block = pl.BlockSpec((wide, width), lambda k: (0, k + start))
    block = pl.BlockSpec((2, rows, width), lambda k: (0, 0, k))
    return pl.pallas_call(
        hidden_kernel,
        grid=(count // width,),
        in_specs=[
            SMEM,
            HBM,
            HBM,
            fixed,
            fixed,
            b_block,
            b_block,
            block,
            block,
            pl.BlockSpec((rows, width), lambda k: (0, k + start)),
        ],
        out_specs=[block, fixed, fixed] + [ANYWHERE] * follow,
        out_shape=[jax.ShapeDtypeStruct((2, rows, count), BF16)]
        + [jax.ShapeDtypeStruct((rows, wide), F32)] * 2
        + [pltpu.VMEM((2, count_after, weights[1].shape[1]), BF16)] * follow,
        scratch_shapes=[PAIR] * follow,
        compiler_params=pltpu.CompilerParams(vmem_limit_bytes=12 << 20),
        cost_estimate=cost(4 * rows * wide * count, 12 * wide * count),
        name="hidden_gradients",
    )(*weights, eug, euu, b_gate, b_up, keep, far, hidden_grad)


def backward_kernel(
    after, side_ref, dg_ref, du_ref, w_ref, wg_ref, wu_ref, keep_ref, send_ref, *rest
):
    copies = rows_copies(side_ref, after, (wg_ref, wu_ref), *rest) if rest else []
    for copy in copies:
        copy.start()
    q = dg_ref.shape[0] // 4
    step = 512
    for k in range(0, w_ref.shape[1], step):
        total = flipped_product(dg_ref[...], w_ref[0, k : k + step])
        total += flipped_product(du_ref[...], w_ref[1, k : k + step])
        out = pl.ds(k, step)
        keep_ref[:q, out] = total[:q]
        keep_ref[q:, out] = total[2 * q : 3 * q]
        send_ref[:q, out] = total[q : 2 * q].astype(send_ref.dtype)
        send_ref[q:, out] = total[3 * q :].astype(send_ref.dtype)
    for copy in copies:
        copy.wait()


def backward_products(weights, dg, du, w, after, count_after):
    rows, ff = dg.shape
    count = w.shape[1]
    side, gate_weight, up_weight = weights
    follow = count_after > 0
    return pl.pallas_call(
        functools.partial(backward_kernel, after),
        in_specs=[SMEM, VMEM, VMEM, VMEM, HBM, HBM],
        out_specs=[VMEM] * 2 + [ANYWHERE] * follow,
        out_shape=[
            jax.ShapeDtypeStruct((rows // 2, count), F32),
            jax.ShapeDtypeStruct((rows // 2, count), BF16),
        ]
        + [pltpu.VMEM((2, count_after, ff), BF16)] * follow,
        scratch_shapes=[PAIR] * follow,
        compiler_params=pltpu.CompilerParams(vmem_limit_bytes=8 << 20),
        cost_estimate=cost(2 * rows * count * ff, 6 * count * ff),
        name="backward_products",
    )(side, dg, du, w, gate_weight, up_weight)


N = 16
CORE, X = 1, 2


def along_tensor(value, mask):
    return lax.ppermute(value, "tensor", [(i, i ^ mask) for i in range(N)])


def across_groups(value, mask=0):
    both = ("group", "tensor")
    return lax.ppermute(value, both, [(i, i ^ (N | mask)) for i in range(2 * N)])


def from_far_z(values):
    return [along_tensor(v, 4 * m) for m, v in zip((1, 2, 3), values)]


def in_order(*values):
    return lax.optimization_barrier(values)


def add_core(value, recv):
    half = value.shape[0] // 2
    return value + jnp.concatenate([recv[half:], recv[:half]], axis=0)


def add_x(value, recv):
    q = value.shape[0] // 4
    order = (1, 0, 3, 2)
    return value + jnp.concatenate([recv[o * q : (o + 1) * q] for o in order], axis=0)


def add_z(value, recv, mask):
    shape = value.shape
    v, r = (w.reshape(4, 4, 2, shape[1]) for w in (value, recv))
    return (v + jnp.stack([r[:, q ^ mask] for q in range(4)], axis=1)).reshape(shape)


def shared_device(tokens, gate_weight, up_weight, a_gate, a_up, b_gate, b_up, agent, d_hidden):
    group = lax.axis_index("group")
    t = lax.axis_index("tensor")
    side = group.astype(jnp.int32).reshape(1)
    d = tokens.shape[1]
    half = d // 2
    feat_rows = a_gate.shape[0]
    per_half = half // feat_rows
    rows = 2 * N
    ff = b_gate.shape[1]

    weights = weights_in_hbm(side, gate_weight, up_weight)
    cuts = [ff * c // 7 for c in (0, 2, 4, 6, 7)]

    recv = along_tensor(tokens, 4)
    a_gate, a_up = narrow(a_gate, a_up, feat_rows // 2)
    recv, a_gate, a_up = in_order(recv, a_gate, a_up)
    line = jnp.concatenate([tokens, recv], axis=0)
    recv = along_tensor(line, 8)
    w = first_columns(weights, cuts[1])
    recv, w = in_order(recv, w)
    line = jnp.concatenate([line, recv], axis=0)
    mine = lax.dynamic_slice_in_dim(line, group * half, half, 1)
    other = lax.dynamic_slice_in_dim(line, half - group * half, half, 1)
    parts = [along_tensor(mine, X), across_groups(other), across_groups(other, X)]
    b_gate, b_up = narrow(b_gate, b_up, b_gate.shape[0] // 8)
    b_gate, b_up, *parts = in_order(b_gate, b_up, *parts)
    x = jnp.stack(
        [jnp.concatenate([mine, parts[0]], axis=0), jnp.concatenate([parts[1], parts[2]], axis=0)]
    )
    x = jnp.concatenate([x, along_tensor(x, CORE)], axis=1).reshape(2 * rows, half)

    place = jnp.arange(rows, dtype=jnp.int32)
    block = ((place >> 1) & 3) * 4 + ((place >> 3) & 1) * 2 + (place >> 4)
    token_of = ((t ^ block) << 1) + (place & 1)
    shuffle = token_of[:, None] == jnp.arange(rows, dtype=jnp.int32)[None, :]
    agent_here = jnp.sum(jnp.where(shuffle, agent[None, :], 0), axis=1)
    chosen = agent_here[:, None] == (jnp.arange(AG * R, dtype=jnp.int32) // R)[None, :]
    hidden_grad = jnp.dot(shuffle.astype(BF16), d_hidden, preferred_element_type=F32)

    def select(values):
        kept = jnp.where(chosen, values, 0.0)
        pair = sum(kept[:, c : c + 2 * R] for c in range(0, AG * R, 2 * R))
        return pair[:, :R] + pair[:, R:]

    def spread(small):
        wide = jnp.concatenate([small] * AG, axis=1)
        return jnp.where(chosen, wide, 0.0).astype(BF16)

    blocks = lax.dynamic_slice_in_dim(x, (t % per_half) * feat_rows, feat_rows, 1)
    swapped = across_groups(blocks[rows:])
    def forward(c, w):
        after = cuts[c + 1]
        return forward_products(weights, x, w, after, (cuts + cuts[-1:])[c + 2] - after)

    keep_0, send_0, w = forward(0, w)
    swapped, x, keep_0, send_0 = in_order(swapped, x, keep_0, send_0)
    own_cols = jnp.where(t // per_half == group, blocks[:rows], swapped)
    part = jnp.concatenate(
        [
            select(jnp.dot(own_cols, a_gate, preferred_element_type=F32)),
            select(jnp.dot(own_cols, a_up, preferred_element_type=F32)),
        ],
        axis=1,
    )

    part = add_core(part, along_tensor(part, CORE))
    part, x = in_order(part, x)
    recv = along_tensor(part, X)
    keep_1, send_1, w = forward(1, w)
    recv, x, keep_1, send_1 = in_order(recv, x, keep_1, send_1)
    part = add_x(part, recv)

    recv = along_tensor(part, 4)
    keep_2, send_2, w = forward(2, w)
    recv, x, keep_2, send_2 = in_order(recv, x, keep_2, send_2)
    part = add_z(part, recv, 1)

    recv = along_tensor(part, 8)
    far_a = across_groups(jnp.concatenate([send_0, send_1, send_2], axis=2))
    keep_3, send_3 = forward(3, w)
    far_a, recv, keep_3, send_3 = in_order(far_a, recv, keep_3, send_3)
    far_b = across_groups(send_3)
    part = add_z(part, recv, 2)
    u = part.astype(BF16).astype(F32)
    up_factor_gate = spread(u[:, :R])
    up_factor_up = spread(u[:, R:])

    steps = [half * c // 8 for c in (0, 2, 5, 8)]

    def hidden(keep, far, first, width, count_after):
        return hidden_gradients(
            weights,
            up_factor_gate,
            up_factor_up,
            b_gate,
            b_up,
            keep,
            far,
            hidden_grad,
            first,
            width,
            count_after,
        )

    keep = jnp.concatenate([keep_0, keep_1, keep_2], axis=2)
    own_a, pg_a, pu_a = hidden(keep, far_a, 0, 512, 0)
    far_b, own_a = in_order(far_b, own_a)
    own_b, pg_b, pu_b, w = hidden(keep_3, far_b, cuts[3], 256, steps[1])
    own = jnp.concatenate([own_a, own_b], axis=2)
    far = across_groups(own)
    part = jnp.concatenate([select(pg_a + pg_b), select(pu_a + pu_b)], axis=1)
    part, own = in_order(part, own)
    recv = along_tensor(part, CORE)
    gate_lift_gradient = adapter_scale * rows_product(up_factor_gate, own[0])
    far, recv, gate_lift_gradient = in_order(far, recv, gate_lift_gradient)
    part = add_core(part, recv)
    both = jnp.concatenate([own, far], axis=1)
    dg, du = both[0], both[1]

    def backward(c, w):
        after = steps[c + 1]
        return backward_products(weights, dg, du, w, after, (steps + steps[-1:])[c + 2] - after)

    recv = along_tensor(part, X)
    keep_0, send_0, w = backward(0, w)
    recv, dg, du, keep_0, send_0 = in_order(recv, dg, du, keep_0, send_0)
    part = add_x(part, recv)

    recv = along_tensor(part, 4)
    keep_1, send_1, w = backward(1, w)
    recv, dg, du, keep_1, send_1 = in_order(recv, dg, du, keep_1, send_1)
    part = add_z(part, recv, 1)

    recv = along_tensor(part, 8)
    keep_2, send_2 = backward(2, w)
    recv, keep_2, send_2, own, own_cols = in_order(recv, keep_2, send_2, own, own_cols)
    part = add_z(part, recv, 2)
    far = along_tensor(jnp.concatenate([send_0, send_1, send_2], axis=1), CORE)
    g = part.astype(BF16).astype(F32)
    gate_factor_gate = spread(g[:, :R])
    gate_factor_up = spread(g[:, R:])
    moved = (
        adapter_scale
        * (
            flipped_product(gate_factor_gate, a_gate)
            + flipped_product(gate_factor_up, a_up)
        )
    ).astype(BF16)

    far_moved = along_tensor(moved[16:], CORE)
    far, far_moved, own_cols = in_order(far, far_moved, own_cols)
    sums = jnp.concatenate([keep_0, keep_1, keep_2], axis=1) + far.astype(F32)
    moved = jnp.concatenate([moved[:16], far_moved], axis=1)

    low = sums.astype(BF16)
    parts = [
        along_tensor(jnp.concatenate([low[8:16], moved[8:]], axis=1), X),
        across_groups(low[16:24]),
        across_groups(low[24:], X),
    ]
    gate_down_gradient = adapter_scale * rows_product(own_cols, gate_factor_gate)
    up_down_gradient = adapter_scale * rows_product(own_cols, gate_factor_up)
    gate_down_gradient, up_down_gradient, own, *parts = in_order(
        gate_down_gradient, up_down_gradient, own, *parts
    )
    near = sums[:8] + parts[0][:, :half].astype(F32)
    sums = jnp.concatenate([near, parts[1].astype(F32) + parts[2].astype(F32)], axis=1)
    moved = jnp.concatenate([moved[:8], parts[0][:, half:]], axis=1)

    low = jnp.concatenate([sums.astype(BF16), moved], axis=1)
    parts = from_far_z([low[2 * m : 2 * m + 2] for m in (1, 2, 3)])
    up_lift_gradient = adapter_scale * rows_product(up_factor_up, own[1])
    up_lift_gradient, *parts = in_order(up_lift_gradient, *parts)
    sums = sums[:2] + sum(p[:, :d].astype(F32) for p in parts)
    moved = jnp.stack([moved[:2]] + [p[:, d:] for p in parts])
    moved = moved.reshape(4, 2, 2, 2, feat_rows).transpose(0, 2, 3, 1, 4).reshape(N, 2 * feat_rows)
    source = jnp.arange(N, dtype=jnp.int32)
    sort = (source[:, None] == (t ^ source)[None, :]).astype(BF16)
    sorted_rows = jnp.dot(sort, moved, preferred_element_type=F32).reshape(N, 2, feat_rows)
    contribution = sorted_rows.transpose(1, 0, 2).reshape(2, d)
    near, far = sums[:, :half], sums[:, half:]
    sums = jnp.where(
        group == 0, jnp.concatenate([near, far], axis=1), jnp.concatenate([far, near], axis=1)
    )
    token_gradient = (sums + contribution).astype(BF16)
    return (
        token_gradient,
        gate_down_gradient,
        up_down_gradient,
        gate_lift_gradient,
        up_lift_gradient,
    )


def solution(mesh):
    sizes = dict(mesh.shape)

    def per_device(*args):
        tokens, b_gate = args[0], args[5]
        fits = (
            sizes["group"] == 2
            and sizes["tensor"] == N
            and tokens.shape[0] == 2
            and b_gate.shape[1] % 1792 == 0
            and tokens.shape[1] % 4096 == 0
        )
        return (shared_device if fits else plain_device)(*args)

    in_specs = (
        P(("group", "tensor"), None),
        P(None, "tensor"),
        P(None, "tensor"),
        P(("group", "tensor"), None),
        P(("group", "tensor"), None),
        P("group", "tensor"),
        P("group", "tensor"),
        P("group"),
        P("group", "tensor"),
    )
    out_specs = (
        P(("group", "tensor"), None),
        P(("group", "tensor"), None),
        P(("group", "tensor"), None),
        P("group", "tensor"),
        P("group", "tensor"),
    )
    return jax.shard_map(
        per_device, mesh=mesh, in_specs=in_specs, out_specs=out_specs, check_vma=False
    )
```

```python
import functools

import jax
import jax.numpy as jnp
from jax import lax
from jax.experimental import pallas as pl
from jax.experimental.pallas import tpu as pltpu
from jax.sharding import PartitionSpec as P

R = 64
AG = 16

adapter_scale = 2.0
BF16 = jnp.bfloat16
F32 = jnp.float32


def agent_mask(agent):
    return (agent[:, None] == jnp.arange(AG, dtype=jnp.int32)[None, :]).astype(jnp.float32)


def select_rank(values, onehot):
    shaped = values.reshape(values.shape[0], AG, R)
    return jnp.sum(shaped * onehot[:, :, None], axis=1)


def spread_rank(small, onehot):
    wide = onehot[:, :, None] * small.astype(jnp.float32)[:, None, :]
    return wide.reshape(small.shape[0], AG * R).astype(jnp.bfloat16)


def flipped_product(left, weight):
    return lax.dot_general(
        left, weight, (((1,), (1,)), ((), ())), preferred_element_type=jnp.float32
    )


def rows_product(left, right):
    return lax.dot_general(
        left, right, (((0,), (0,)), ((), ())), preferred_element_type=jnp.float32
    )


def plain_device(tokens, gate_weight, up_weight, a_gate, a_up, b_gate, b_up, agent, d_hidden):
    onehot = agent_mask(agent)
    feat_rows = a_gate.shape[0]
    feat_start = lax.axis_index("tensor") * feat_rows
    agent_gate_down = a_gate.astype(jnp.bfloat16)
    agent_up_down = a_up.astype(jnp.bfloat16)
    agent_gate_lift = b_gate.astype(jnp.bfloat16)
    agent_up_lift = b_up.astype(jnp.bfloat16)
    complete_result = lax.all_gather(tokens, "tensor", axis=0, tiled=True)
    own_cols = lax.dynamic_slice_in_dim(complete_result, feat_start, feat_rows, 1)
    part_gate = select_rank(
        jnp.dot(own_cols, agent_gate_down, preferred_element_type=jnp.float32), onehot
    )
    part_up = select_rank(
        jnp.dot(own_cols, agent_up_down, preferred_element_type=jnp.float32), onehot
    )
    u_gate, u_up = lax.psum((part_gate, part_up), "tensor")
    up_factor_gate = spread_rank(u_gate.astype(jnp.bfloat16), onehot)
    up_factor_up = spread_rank(u_up.astype(jnp.bfloat16), onehot)
    gate_values = jnp.dot(
        complete_result, gate_weight, preferred_element_type=jnp.float32
    ) + adapter_scale * jnp.dot(up_factor_gate, agent_gate_lift, preferred_element_type=jnp.float32)
    up_values = jnp.dot(
        complete_result, up_weight, preferred_element_type=jnp.float32
    ) + adapter_scale * jnp.dot(up_factor_up, agent_up_lift, preferred_element_type=jnp.float32)
    sig = jax.nn.sigmoid(gate_values)
    hidden_grad = d_hidden.astype(jnp.float32)
    gate_gradient = (hidden_grad * up_values * sig * (1.0 + gate_values * (1.0 - sig))).astype(
        jnp.bfloat16
    )
    up_gradient = (hidden_grad * gate_values * sig).astype(jnp.bfloat16)
    pg_gate = select_rank(flipped_product(gate_gradient, agent_gate_lift), onehot)
    pg_up = select_rank(flipped_product(up_gradient, agent_up_lift), onehot)
    g_gate, g_up = lax.psum((pg_gate, pg_up), "tensor")
    gate_factor_gate = spread_rank(g_gate.astype(jnp.bfloat16), onehot)
    gate_factor_up = spread_rank(g_up.astype(jnp.bfloat16), onehot)
    adapter_contribution = adapter_scale * (
        flipped_product(gate_factor_gate, agent_gate_down)
        + flipped_product(gate_factor_up, agent_up_down)
    )
    base_rows = flipped_product(gate_gradient, gate_weight) + flipped_product(
        up_gradient, up_weight
    )
    joined = lax.dynamic_slice_in_dim(base_rows, feat_start, feat_rows, 1) + adapter_contribution
    token_gradient = lax.psum_scatter(
        lax.dynamic_update_slice_in_dim(base_rows, joined, feat_start, 1),
        "tensor",
        scatter_dimension=0,
        tiled=True,
    ).astype(jnp.bfloat16)
    gate_down_gradient = adapter_scale * rows_product(own_cols, gate_factor_gate)
    up_down_gradient = adapter_scale * rows_product(own_cols, gate_factor_up)
    gate_lift_gradient = adapter_scale * rows_product(up_factor_gate, gate_gradient)
    up_lift_gradient = adapter_scale * rows_product(up_factor_up, up_gradient)
    return (
        token_gradient,
        gate_down_gradient,
        up_down_gradient,
        gate_lift_gradient,
        up_lift_gradient,
    )


VMEM = pl.BlockSpec(memory_space=pltpu.VMEM)
HBM = pl.BlockSpec(memory_space=pltpu.HBM)
SMEM = pl.BlockSpec(memory_space=pltpu.SMEM)
ANYWHERE = pl.BlockSpec(memory_space=pl.ANY)
PIECES = 16


class Chunk:
    def __init__(self, arrays, first_row, rows, first_column, columns, per_side=0):
        self.arrays = [pltpu.with_memory_space_constraint(a, pltpu.HBM) for a in arrays]
        self.first_row, self.rows, self.per_side = first_row, rows, per_side
        self.first_column, self.columns = first_column, columns
        self.out = pltpu.VMEM((2, rows, columns), arrays[0].dtype)

    def copies(self, side_ref, refs, out_ref, sem):
        depth = self.rows // PIECES
        base = side_ref[0] * self.per_side + self.first_row
        columns = pl.ds(self.first_column, self.columns)
        return [
            pltpu.make_async_copy(
                ref.at[pl.ds(pl.multiple_of(base + k * depth, 16), depth), columns],
                out_ref.at[i, pl.ds(k * depth, depth)],
                sem.at[i, k],
            )
            for i, ref in enumerate(refs)
            for k in range(PIECES)
        ]


def run(name, kernel, side, operands, out_shape, chunk, products=0):
    n_in, n_out = len(operands), len(out_shape)
    follow = chunk is not None

    def body(side_ref, *refs):
        values, rest = refs[:n_in], refs[n_in:]
        if follow:
            outs = rest[2 : 2 + n_out]
            copies = chunk.copies(side_ref, rest[:2], *rest[2 + n_out :])
        else:
            outs, copies = rest, []
        for copy in copies:
            copy.start()
        kernel(*values, *outs)
        for copy in copies:
            copy.wait()

    moved = 4 * chunk.rows * chunk.columns if follow else 0
    return pl.pallas_call(
        body,
        in_specs=[SMEM] + [VMEM] * n_in + [HBM] * (2 * follow),
        out_specs=[VMEM] * n_out + [ANYWHERE] * follow,
        out_shape=out_shape + ([chunk.out] if follow else []),
        scratch_shapes=[pltpu.SemaphoreType.DMA((2, PIECES))] * follow,
        compiler_params=pltpu.CompilerParams(vmem_limit_bytes=8 << 20),
        cost_estimate=pl.CostEstimate(
            flops=2 * products, bytes_accessed=max(moved, products // 20), transcendentals=0
        ),
        name=name,
    )(side, *operands, *(chunk.arrays if follow else []))


def first_kernel():
    pass


def forward_kernel(x_ref, w_ref, keep_ref, send_ref):
    half = keep_ref.shape[1]
    for i in range(2):
        total = jnp.dot(x_ref[...], w_ref[i], preferred_element_type=F32)
        keep_ref[i] = total[:half]
        send_ref[i] = total[half:].astype(send_ref.dtype)


def forward_products(side, x, w, chunk):
    rows, depth = x.shape
    count = w.shape[2]
    out_shape = [jax.ShapeDtypeStruct((2, rows // 2, count), kind) for kind in (F32, BF16)]
    products = 2 * rows * depth * count
    return run("forward_products", forward_kernel, side, (x, w), out_shape, chunk, products)


def hidden_kernel(eug_ref, euu_ref, b_ref, keep_ref, far_ref, dh_ref, d_ref, pg_ref, pu_ref):
    count = keep_ref.shape[2]
    step = 512 if count % 512 == 0 else 256
    sums = None
    for start in range(0, count, step):
        at = pl.ds(start, step)
        bg = b_ref[0, :, at].astype(BF16)
        bu = b_ref[1, :, at].astype(BF16)
        gate = (
            keep_ref[0, :, at]
            + far_ref[0, :, at].astype(F32)
            + adapter_scale * jnp.dot(eug_ref[...], bg, preferred_element_type=F32)
        )
        up = (
            keep_ref[1, :, at]
            + far_ref[1, :, at].astype(F32)
            + adapter_scale * jnp.dot(euu_ref[...], bu, preferred_element_type=F32)
        )
        sig = jax.nn.sigmoid(gate)
        hidden_grad = dh_ref[:, at]
        dg = (hidden_grad * up * sig * (1.0 + gate * (1.0 - sig))).astype(BF16)
        du = (hidden_grad * gate * sig).astype(BF16)
        d_ref[0, :, at] = dg
        d_ref[1, :, at] = du
        terms = flipped_product(dg, bg), flipped_product(du, bu)
        sums = terms if sums is None else (sums[0] + terms[0], sums[1] + terms[1])
    pg_ref[...], pu_ref[...] = sums


def hidden_gradients(side, eug, euu, b, keep, far, hidden_grad, chunk):
    rows, wide = eug.shape
    count = keep.shape[2]
    out_shape = [jax.ShapeDtypeStruct((2, rows, count), BF16)]
    out_shape += [jax.ShapeDtypeStruct((rows, wide), F32)] * 2
    operands = (eug, euu, b, keep, far, hidden_grad)
    products = 4 * rows * wide * count
    return run("hidden_gradients", hidden_kernel, side, operands, out_shape, chunk, products)


def backward_kernel(dg_ref, du_ref, w_ref, keep_ref, send_ref):
    q = dg_ref.shape[0] // 4
    step = 512
    for k in range(0, w_ref.shape[1], step):
        total = flipped_product(dg_ref[...], w_ref[0, k : k + step])
        total += flipped_product(du_ref[...], w_ref[1, k : k + step])
        out = pl.ds(k, step)
        keep_ref[:q, out] = total[:q]
        keep_ref[q:, out] = total[2 * q : 3 * q]
        send_ref[:q, out] = total[q : 2 * q].astype(send_ref.dtype)
        send_ref[q:, out] = total[3 * q :].astype(send_ref.dtype)


def backward_products(side, dg, du, w, chunk):
    rows, ff = dg.shape
    count = w.shape[1]
    out_shape = [jax.ShapeDtypeStruct((rows // 2, count), kind) for kind in (F32, BF16)]
    products = 2 * rows * ff * count
    return run("backward_products", backward_kernel, side, (dg, du, w), out_shape, chunk, products)


def narrow_kernel(g_ref, u_ref, g16_ref, u16_ref):
    g16_ref[...] = g_ref[...].astype(BF16)
    u16_ref[...] = u_ref[...].astype(BF16)


def narrow(gate, up, depth):
    rows, width = gate.shape
    block = pl.BlockSpec((depth, width), lambda k: (k, 0))
    return pl.pallas_call(
        narrow_kernel,
        grid=(rows // depth,),
        in_specs=[block] * 2,
        out_specs=[block] * 2,
        out_shape=[jax.ShapeDtypeStruct(gate.shape, BF16)] * 2,
        compiler_params=pltpu.CompilerParams(vmem_limit_bytes=16 << 20),
        cost_estimate=pl.CostEstimate(flops=0, bytes_accessed=12 * rows * width, transcendentals=0),
        name="narrow",
    )(
        pltpu.with_memory_space_constraint(gate, pltpu.HBM),
        pltpu.with_memory_space_constraint(up, pltpu.HBM),
    )


N = 16
CORE, X = 1, 2


def along_tensor(value, mask):
    return lax.ppermute(value, "tensor", [(i, i ^ mask) for i in range(N)])


def across_groups(value, mask=0):
    both = ("group", "tensor")
    return lax.ppermute(value, both, [(i, i ^ (N | mask)) for i in range(2 * N)])


def from_far_z(values):
    return [along_tensor(v, 4 * m) for m, v in zip((1, 2, 3), values)]


def in_order(*values):
    return lax.optimization_barrier(values)


def add_core(value, recv):
    half = value.shape[0] // 2
    return value + jnp.concatenate([recv[half:], recv[:half]], axis=0)


def add_x(value, recv):
    q = value.shape[0] // 4
    order = (1, 0, 3, 2)
    return value + jnp.concatenate([recv[o * q : (o + 1) * q] for o in order], axis=0)


def add_z(value, recv, mask):
    shape = value.shape
    v, r = (w.reshape(4, 4, 2, shape[1]) for w in (value, recv))
    return (v + jnp.stack([r[:, q ^ mask] for q in range(4)], axis=1)).reshape(shape)


def shared_device(tokens, gate_weight, up_weight, a_gate, a_up, b_gate, b_up, agent, d_hidden):
    group = lax.axis_index("group")
    t = lax.axis_index("tensor")
    side = group.astype(jnp.int32).reshape(1)
    d = tokens.shape[1]
    half = d // 2
    feat_rows = a_gate.shape[0]
    per_half = half // feat_rows
    rows = 2 * N
    ff = b_gate.shape[1]

    weights = gate_weight, up_weight
    cuts = [ff * c // 7 for c in (0, 2, 4, 6, 7)]
    steps = [half * c // 8 for c in (0, 2, 5, 8)]
    columns = [Chunk(weights, 0, half, c, n - c, half) for c, n in zip(cuts, cuts[1:])]
    lifts = [
        Chunk((b_gate, b_up), 0, b_gate.shape[0], c, n - c)
        for c, n in ((0, cuts[3]), (cuts[3], ff))
    ]
    lines = [Chunk(weights, c, n - c, 0, ff, half) for c, n in zip(steps, steps[1:])]

    recv = along_tensor(tokens, 4)
    a_gate, a_up = narrow(a_gate, a_up, feat_rows // 2)
    recv, a_gate, a_up = in_order(recv, a_gate, a_up)
    line = jnp.concatenate([tokens, recv], axis=0)
    recv = along_tensor(line, 8)
    line = jnp.concatenate([line, recv], axis=0)
    mine = lax.dynamic_slice_in_dim(line, group * half, half, 1)
    other = lax.dynamic_slice_in_dim(line, half - group * half, half, 1)
    parts = [along_tensor(mine, X), across_groups(other), across_groups(other, X)]
    x = jnp.stack(
        [jnp.concatenate([mine, parts[0]], axis=0), jnp.concatenate([parts[1], parts[2]], axis=0)]
    )
    recv = along_tensor(x, CORE)
    side, x = in_order(side, x)
    (w,) = run("first_columns", first_kernel, side, (), [], columns[0])
    x = jnp.concatenate([x, recv], axis=1).reshape(2 * rows, half)

    place = jnp.arange(rows, dtype=jnp.int32)
    block = ((place >> 1) & 3) * 4 + ((place >> 3) & 1) * 2 + (place >> 4)
    token_of = ((t ^ block) << 1) + (place & 1)
    shuffle = token_of[:, None] == jnp.arange(rows, dtype=jnp.int32)[None, :]
    agent_here = jnp.sum(jnp.where(shuffle, agent[None, :], 0), axis=1)
    chosen = agent_here[:, None] == (jnp.arange(AG * R, dtype=jnp.int32) // R)[None, :]
    hidden_grad = jnp.dot(shuffle.astype(BF16), d_hidden, preferred_element_type=F32)

    def select(values):
        kept = jnp.where(chosen, values, 0.0)
        pair = sum(kept[:, c : c + 2 * R] for c in range(0, AG * R, 2 * R))
        return pair[:, :R] + pair[:, R:]

    def spread(small):
        wide = jnp.concatenate([small] * AG, axis=1)
        return jnp.where(chosen, wide, 0.0).astype(BF16)

    blocks = lax.dynamic_slice_in_dim(x, (t % per_half) * feat_rows, feat_rows, 1)
    swapped = across_groups(blocks[rows:])
    def forward(c, w):
        return forward_products(side, x, w, (columns + lifts)[c + 1])

    keep_0, send_0, w = forward(0, w)
    swapped, x, keep_0, send_0 = in_order(swapped, x, keep_0, send_0)
    own_cols = jnp.where(t // per_half == group, blocks[:rows], swapped)
    part = jnp.concatenate(
        [
            select(jnp.dot(own_cols, a_gate, preferred_element_type=F32)),
            select(jnp.dot(own_cols, a_up, preferred_element_type=F32)),
        ],
        axis=1,
    )

    part = add_core(part, along_tensor(part, CORE))
    part, x = in_order(part, x)
    recv = along_tensor(part, X)
    keep_1, send_1, w = forward(1, w)
    recv, x, keep_1, send_1 = in_order(recv, x, keep_1, send_1)
    part = add_x(part, recv)

    recv = along_tensor(part, 4)
    keep_2, send_2, w = forward(2, w)
    recv, x, keep_2, send_2 = in_order(recv, x, keep_2, send_2)
    part = add_z(part, recv, 1)

    recv = along_tensor(part, 8)
    far_a = across_groups(jnp.concatenate([send_0, send_1, send_2], axis=2))
    keep_3, send_3, b = forward(3, w)
    far_a, recv, keep_3, send_3 = in_order(far_a, recv, keep_3, send_3)
    far_b = across_groups(send_3)
    part = add_z(part, recv, 2)
    u = part.astype(BF16).astype(F32)
    up_factor_gate = spread(u[:, :R])
    up_factor_up = spread(u[:, R:])

    def hidden(b, keep, far, dh, chunk):
        return hidden_gradients(side, up_factor_gate, up_factor_up, b, keep, far, dh, chunk)

    keep = jnp.concatenate([keep_0, keep_1, keep_2], axis=2)
    own_a, pg_a, pu_a, b = hidden(b, keep, far_a, hidden_grad[:, : cuts[3]], lifts[1])
    far_b, own_a = in_order(far_b, own_a)
    own_b, pg_b, pu_b, w = hidden(b, keep_3, far_b, hidden_grad[:, cuts[3] :], lines[0])
    own = jnp.concatenate([own_a, own_b], axis=2)
    far = across_groups(own)
    part = jnp.concatenate([select(pg_a + pg_b), select(pu_a + pu_b)], axis=1)
    part, own = in_order(part, own)
    recv = along_tensor(part, CORE)
    gate_lift_gradient = adapter_scale * rows_product(up_factor_gate, own[0])
    far, recv, gate_lift_gradient = in_order(far, recv, gate_lift_gradient)
    part = add_core(part, recv)
    both = jnp.concatenate([own, far], axis=1)
    dg, du = both[0], both[1]

    def backward(c, w):
        return backward_products(side, dg, du, w, (lines + [None])[c + 1])

    recv = along_tensor(part, X)
    keep_0, send_0, w = backward(0, w)
    recv, dg, du, keep_0, send_0 = in_order(recv, dg, du, keep_0, send_0)
    part = add_x(part, recv)

    recv = along_tensor(part, 4)
    keep_1, send_1, w = backward(1, w)
    recv, dg, du, keep_1, send_1 = in_order(recv, dg, du, keep_1, send_1)
    part = add_z(part, recv, 1)

    recv = along_tensor(part, 8)
    keep_2, send_2 = backward(2, w)
    recv, keep_2, send_2, own, own_cols = in_order(recv, keep_2, send_2, own, own_cols)
    part = add_z(part, recv, 2)
    far = along_tensor(jnp.concatenate([send_0, send_1, send_2], axis=1), CORE)
    g = part.astype(BF16).astype(F32)
    gate_factor_gate = spread(g[:, :R])
    gate_factor_up = spread(g[:, R:])
    moved = (
        adapter_scale
        * (
            flipped_product(gate_factor_gate, a_gate)
            + flipped_product(gate_factor_up, a_up)
        )
    ).astype(BF16)

    far_moved = along_tensor(moved[16:], CORE)
    far, far_moved, own_cols = in_order(far, far_moved, own_cols)
    sums = jnp.concatenate([keep_0, keep_1, keep_2], axis=1) + far.astype(F32)
    moved = jnp.concatenate([moved[:16], far_moved], axis=1)

    low = sums.astype(BF16)
    parts = [
        along_tensor(jnp.concatenate([low[8:16], moved[8:]], axis=1), X),
        across_groups(low[16:24]),
        across_groups(low[24:], X),
    ]
    gate_down_gradient = adapter_scale * rows_product(own_cols, gate_factor_gate)
    up_down_gradient = adapter_scale * rows_product(own_cols, gate_factor_up)
    gate_down_gradient, up_down_gradient, own, *parts = in_order(
        gate_down_gradient, up_down_gradient, own, *parts
    )
    near = sums[:8] + parts[0][:, :half].astype(F32)
    sums = jnp.concatenate([near, parts[1].astype(F32) + parts[2].astype(F32)], axis=1)
    moved = jnp.concatenate([moved[:8], parts[0][:, half:]], axis=1)

    low = jnp.concatenate([sums.astype(BF16), moved], axis=1)
    parts = from_far_z([low[2 * m : 2 * m + 2] for m in (1, 2, 3)])
    up_lift_gradient = adapter_scale * rows_product(up_factor_up, own[1])
    up_lift_gradient, *parts = in_order(up_lift_gradient, *parts)
    sums = sums[:2] + sum(p[:, :d].astype(F32) for p in parts)
    moved = jnp.stack([moved[:2]] + [p[:, d:] for p in parts])
    moved = moved.reshape(4, 2, 2, 2, feat_rows).transpose(0, 2, 3, 1, 4).reshape(N, 2 * feat_rows)
    source = jnp.arange(N, dtype=jnp.int32)
    sort = (source[:, None] == (t ^ source)[None, :]).astype(BF16)
    sorted_rows = jnp.dot(sort, moved, preferred_element_type=F32).reshape(N, 2, feat_rows)
    contribution = sorted_rows.transpose(1, 0, 2).reshape(2, d)
    near, far = sums[:, :half], sums[:, half:]
    sums = jnp.where(
        group == 0, jnp.concatenate([near, far], axis=1), jnp.concatenate([far, near], axis=1)
    )
    token_gradient = (sums + contribution).astype(BF16)
    return (
        token_gradient,
        gate_down_gradient,
        up_down_gradient,
        gate_lift_gradient,
        up_lift_gradient,
    )


def solution(mesh):
    sizes = dict(mesh.shape)

    def per_device(*args):
        tokens, b_gate = args[0], args[5]
        fits = (
            sizes["group"] == 2
            and sizes["tensor"] == N
            and tokens.shape[0] == 2
            and b_gate.shape[1] % 1792 == 0
            and tokens.shape[1] % 4096 == 0
        )
        return (shared_device if fits else plain_device)(*args)

    in_specs = (
        P(("group", "tensor"), None),
        P(None, "tensor"),
        P(None, "tensor"),
        P(("group", "tensor"), None),
        P(("group", "tensor"), None),
        P("group", "tensor"),
        P("group", "tensor"),
        P("group"),
        P("group", "tensor"),
    )
    out_specs = (
        P(("group", "tensor"), None),
        P(("group", "tensor"), None),
        P(("group", "tensor"), None),
        P("group", "tensor"),
        P("group", "tensor"),
    )
    return jax.shard_map(
        per_device, mesh=mesh, in_specs=in_specs, out_specs=out_specs, check_vma=False
    )
```

```python
import functools

import jax
import jax.numpy as jnp
from jax import lax
from jax.experimental import pallas as pl
from jax.experimental.pallas import tpu as pltpu
from jax.sharding import PartitionSpec as P

R = 64
AG = 16

adapter_scale = 2.0
BF16 = jnp.bfloat16
F32 = jnp.float32


def agent_mask(agent):
    return (agent[:, None] == jnp.arange(AG, dtype=jnp.int32)[None, :]).astype(jnp.float32)


def select_rank(values, onehot):
    shaped = values.reshape(values.shape[0], AG, R)
    return jnp.sum(shaped * onehot[:, :, None], axis=1)


def spread_rank(small, onehot):
    wide = onehot[:, :, None] * small.astype(jnp.float32)[:, None, :]
    return wide.reshape(small.shape[0], AG * R).astype(jnp.bfloat16)


def flipped_product(left, weight):
    return lax.dot_general(
        left, weight, (((1,), (1,)), ((), ())), preferred_element_type=jnp.float32
    )


def rows_product(left, right):
    return lax.dot_general(
        left, right, (((0,), (0,)), ((), ())), preferred_element_type=jnp.float32
    )


def plain_device(tokens, gate_weight, up_weight, a_gate, a_up, b_gate, b_up, agent, d_hidden):
    onehot = agent_mask(agent)
    feat_rows = a_gate.shape[0]
    feat_start = lax.axis_index("tensor") * feat_rows
    agent_gate_down = a_gate.astype(jnp.bfloat16)
    agent_up_down = a_up.astype(jnp.bfloat16)
    agent_gate_lift = b_gate.astype(jnp.bfloat16)
    agent_up_lift = b_up.astype(jnp.bfloat16)
    complete_result = lax.all_gather(tokens, "tensor", axis=0, tiled=True)
    own_cols = lax.dynamic_slice_in_dim(complete_result, feat_start, feat_rows, 1)
    part_gate = select_rank(
        jnp.dot(own_cols, agent_gate_down, preferred_element_type=jnp.float32), onehot
    )
    part_up = select_rank(
        jnp.dot(own_cols, agent_up_down, preferred_element_type=jnp.float32), onehot
    )
    u_gate, u_up = lax.psum((part_gate, part_up), "tensor")
    up_factor_gate = spread_rank(u_gate.astype(jnp.bfloat16), onehot)
    up_factor_up = spread_rank(u_up.astype(jnp.bfloat16), onehot)
    gate_values = jnp.dot(
        complete_result, gate_weight, preferred_element_type=jnp.float32
    ) + adapter_scale * jnp.dot(up_factor_gate, agent_gate_lift, preferred_element_type=jnp.float32)
    up_values = jnp.dot(
        complete_result, up_weight, preferred_element_type=jnp.float32
    ) + adapter_scale * jnp.dot(up_factor_up, agent_up_lift, preferred_element_type=jnp.float32)
    sig = jax.nn.sigmoid(gate_values)
    hidden_grad = d_hidden.astype(jnp.float32)
    gate_gradient = (hidden_grad * up_values * sig * (1.0 + gate_values * (1.0 - sig))).astype(
        jnp.bfloat16
    )
    up_gradient = (hidden_grad * gate_values * sig).astype(jnp.bfloat16)
    pg_gate = select_rank(flipped_product(gate_gradient, agent_gate_lift), onehot)
    pg_up = select_rank(flipped_product(up_gradient, agent_up_lift), onehot)
    g_gate, g_up = lax.psum((pg_gate, pg_up), "tensor")
    gate_factor_gate = spread_rank(g_gate.astype(jnp.bfloat16), onehot)
    gate_factor_up = spread_rank(g_up.astype(jnp.bfloat16), onehot)
    adapter_contribution = adapter_scale * (
        flipped_product(gate_factor_gate, agent_gate_down)
        + flipped_product(gate_factor_up, agent_up_down)
    )
    base_rows = flipped_product(gate_gradient, gate_weight) + flipped_product(
        up_gradient, up_weight
    )
    joined = lax.dynamic_slice_in_dim(base_rows, feat_start, feat_rows, 1) + adapter_contribution
    token_gradient = lax.psum_scatter(
        lax.dynamic_update_slice_in_dim(base_rows, joined, feat_start, 1),
        "tensor",
        scatter_dimension=0,
        tiled=True,
    ).astype(jnp.bfloat16)
    gate_down_gradient = adapter_scale * rows_product(own_cols, gate_factor_gate)
    up_down_gradient = adapter_scale * rows_product(own_cols, gate_factor_up)
    gate_lift_gradient = adapter_scale * rows_product(up_factor_gate, gate_gradient)
    up_lift_gradient = adapter_scale * rows_product(up_factor_up, up_gradient)
    return (
        token_gradient,
        gate_down_gradient,
        up_down_gradient,
        gate_lift_gradient,
        up_lift_gradient,
    )


def forward_kernel(first, side_ref, x_ref, wg_ref, wu_ref, keep_ref, send_ref, piece, sem):
    pieces, depth, count = piece.shape[1:]
    half = keep_ref.shape[1]
    base = side_ref[0] * (pieces * depth)
    copies = []
    for i, w_ref in enumerate((wg_ref, wu_ref)):
        for k in range(pieces):
            source = pl.ds(pl.multiple_of(base + k * depth, depth), depth)
            copy = pltpu.make_async_copy(
                w_ref.at[source, pl.ds(first, count)], piece.at[i, k], sem.at[i, k]
            )
            copy.start()
            copies.append(copy)
    for i in range(2):
        total = None
        for k in range(pieces):
            copies[i * pieces + k].wait()
            term = jnp.dot(
                x_ref[:, k * depth : (k + 1) * depth], piece[i, k], preferred_element_type=F32
            )
            total = term if total is None else total + term
        keep_ref[i] = total[:half]
        send_ref[i] = total[half:].astype(send_ref.dtype)


def forward_products(side, x, gate_weight, up_weight, first, count, pieces=4):
    rows, depth = x.shape
    vmem = pl.BlockSpec(memory_space=pltpu.VMEM)
    hbm = pl.BlockSpec(memory_space=pltpu.HBM)
    return pl.pallas_call(
        functools.partial(forward_kernel, first),
        in_specs=[pl.BlockSpec(memory_space=pltpu.SMEM), vmem, hbm, hbm],
        out_specs=[vmem] * 2,
        out_shape=[
            jax.ShapeDtypeStruct((2, rows // 2, count), F32),
            jax.ShapeDtypeStruct((2, rows // 2, count), BF16),
        ],
        scratch_shapes=[
            pltpu.VMEM((2, pieces, depth // pieces, count), BF16),
            pltpu.SemaphoreType.DMA((2, pieces)),
        ],
        compiler_params=pltpu.CompilerParams(vmem_limit_bytes=20 << 20),
        cost_estimate=pl.CostEstimate(
            flops=4 * rows * count * depth, bytes_accessed=6 * count * depth, transcendentals=0
        ),
        name="forward_products",
    )(
        side,
        x,
        pltpu.with_memory_space_constraint(gate_weight, pltpu.HBM),
        pltpu.with_memory_space_constraint(up_weight, pltpu.HBM),
    )


def narrow_kernel(g_ref, u_ref, g16_ref, u16_ref):
    g16_ref[...] = g_ref[...].astype(BF16)
    u16_ref[...] = u_ref[...].astype(BF16)


def narrow(gate, up, depth):
    rows, width = gate.shape
    block = pl.BlockSpec((depth, width), lambda k: (k, 0))
    return pl.pallas_call(
        narrow_kernel,
        grid=(rows // depth,),
        in_specs=[block] * 2,
        out_specs=[block] * 2,
        out_shape=[jax.ShapeDtypeStruct(gate.shape, BF16)] * 2,
        compiler_params=pltpu.CompilerParams(vmem_limit_bytes=16 << 20),
        cost_estimate=pl.CostEstimate(flops=0, bytes_accessed=12 * rows * width, transcendentals=0),
        name="narrow",
    )(
        pltpu.with_memory_space_constraint(gate, pltpu.HBM),
        pltpu.with_memory_space_constraint(up, pltpu.HBM),
    )


def hidden_kernel(
    first, step, eug_ref, euu_ref, keep_ref, far_ref, dh_ref, bg_ref, bu_ref, d_ref, pg_ref, pu_ref,
    b_ref, sem
):
    blocks, _, pieces = sem.shape
    depth = b_ref.shape[2] // pieces

    def copies(block):
        return [
            pltpu.make_async_copy(
                ref.at[pl.ds(k * depth, depth), pl.ds(first + block * step, step)],
                b_ref.at[block, i, pl.ds(k * depth, depth)],
                sem.at[block, i, k],
            )
            for i, ref in enumerate((bg_ref, bu_ref))
            for k in range(pieces)
        ]

    running = [copies(block) for block in range(blocks)]
    for block in range(min(2, blocks)):
        for copy in running[block]:
            copy.start()
    for block in range(blocks):
        for copy in running[block]:
            copy.wait()
        if block + 2 < blocks:
            for copy in running[block + 2]:
                copy.start()
        at = pl.ds(block * step, step)
        bg = b_ref[block, 0].astype(BF16)
        bu = b_ref[block, 1].astype(BF16)
        gate = (
            keep_ref[0, :, at]
            + far_ref[0, :, at].astype(F32)
            + adapter_scale * jnp.dot(eug_ref[...], bg, preferred_element_type=F32)
        )
        up = (
            keep_ref[1, :, at]
            + far_ref[1, :, at].astype(F32)
            + adapter_scale * jnp.dot(euu_ref[...], bu, preferred_element_type=F32)
        )
        sig = jax.nn.sigmoid(gate)
        hidden_grad = dh_ref[:, at]
        dg = (hidden_grad * up * sig * (1.0 + gate * (1.0 - sig))).astype(BF16)
        du = (hidden_grad * gate * sig).astype(BF16)
        d_ref[0, :, at] = dg
        d_ref[1, :, at] = du
        if block == 0:
            pg_ref[...] = flipped_product(dg, bg)
            pu_ref[...] = flipped_product(du, bu)
        else:
            pg_ref[...] += flipped_product(dg, bg)
            pu_ref[...] += flipped_product(du, bu)


def hidden_gradients(eug, euu, b_gate, b_up, keep, far, hidden_grad, first, step, pieces=4):
    rows, wide = eug.shape
    count = keep.shape[2]
    vmem = pl.BlockSpec(memory_space=pltpu.VMEM)
    hbm = pl.BlockSpec(memory_space=pltpu.HBM)
    return pl.pallas_call(
        functools.partial(hidden_kernel, first, step),
        in_specs=[vmem] * 5 + [hbm] * 2,
        out_specs=[vmem] * 3,
        out_shape=[jax.ShapeDtypeStruct((2, rows, count), BF16)]
        + [jax.ShapeDtypeStruct((rows, wide), F32)] * 2,
        scratch_shapes=[
            pltpu.VMEM((count // step, 2, wide, step), F32),
            pltpu.SemaphoreType.DMA((count // step, 2, pieces)),
        ],
        compiler_params=pltpu.CompilerParams(vmem_limit_bytes=28 << 20),
        cost_estimate=pl.CostEstimate(
            flops=8 * rows * wide * count, bytes_accessed=12 * wide * count, transcendentals=0
        ),
        name="hidden_gradients",
    )(
        eug,
        euu,
        keep,
        far,
        hidden_grad[:, first : first + count],
        pltpu.with_memory_space_constraint(b_gate, pltpu.HBM),
        pltpu.with_memory_space_constraint(b_up, pltpu.HBM),
    )


def backward_kernel(first, side_ref, dg_ref, du_ref, wg_ref, wu_ref, keep_ref, send_ref, rows_ref, sem):
    pieces = sem.shape[1]
    total_rows = rows_ref.shape[1]
    depth = total_rows // pieces
    base = side_ref[0] * (wg_ref.shape[0] // 2) + first
    copies = {}
    for j in range(pieces):
        for i, w_ref in enumerate((wg_ref, wu_ref)):
            source = pl.ds(pl.multiple_of(base + j * depth, depth), depth)
            copies[i, j] = pltpu.make_async_copy(
                w_ref.at[source], rows_ref.at[i, pl.ds(j * depth, depth)], sem.at[i, j]
            )

    def start(j):
        if j < pieces:
            for at in ((0, j), (0, j + 1), (1, j), (1, j + 1)):
                copies[at].start()

    start(0)
    start(2)
    q = dg_ref.shape[0] // 4
    step = 2 * depth
    for k in range(0, total_rows, step):
        j = k // depth
        copies[0, j].wait()
        copies[0, j + 1].wait()
        copies[1, j].wait()
        copies[1, j + 1].wait()
        start(j + 4)
        total = flipped_product(dg_ref[...], rows_ref[0, k : k + step])
        total += flipped_product(du_ref[...], rows_ref[1, k : k + step])
        out = pl.ds(k, step)
        keep_ref[:q, out] = total[:q]
        keep_ref[q:, out] = total[2 * q : 3 * q]
        send_ref[:q, out] = total[q : 2 * q].astype(send_ref.dtype)
        send_ref[q:, out] = total[3 * q :].astype(send_ref.dtype)


def backward_products(side, dg, du, gate_weight, up_weight, first, count, depth=256):
    rows, ff = dg.shape
    vmem = pl.BlockSpec(memory_space=pltpu.VMEM)
    hbm = pl.BlockSpec(memory_space=pltpu.HBM)
    return pl.pallas_call(
        functools.partial(backward_kernel, first),
        in_specs=[pl.BlockSpec(memory_space=pltpu.SMEM), vmem, vmem, hbm, hbm],
        out_specs=[vmem] * 2,
        out_shape=[
            jax.ShapeDtypeStruct((rows // 2, count), F32),
            jax.ShapeDtypeStruct((rows // 2, count), BF16),
        ],
        scratch_shapes=[
            pltpu.VMEM((2, count, ff), BF16),
            pltpu.SemaphoreType.DMA((2, count // depth)),
        ],
        compiler_params=pltpu.CompilerParams(vmem_limit_bytes=36 << 20),
        cost_estimate=pl.CostEstimate(
            flops=4 * rows * count * ff, bytes_accessed=6 * count * ff, transcendentals=0
        ),
        name="backward_products",
    )(
        side,
        dg,
        du,
        pltpu.with_memory_space_constraint(gate_weight, pltpu.HBM),
        pltpu.with_memory_space_constraint(up_weight, pltpu.HBM),
    )


N = 16
CORE, X = 1, 2


def along_tensor(value, mask):
    return lax.ppermute(value, "tensor", [(i, i ^ mask) for i in range(N)])


def across_groups(value, mask=0):
    both = ("group", "tensor")
    return lax.ppermute(value, both, [(i, i ^ (N | mask)) for i in range(2 * N)])


def from_far_z(values):
    return [along_tensor(v, 4 * m) for m, v in zip((1, 2, 3), values)]


def in_order(*values):
    return lax.optimization_barrier(values)


def add_core(value, recv):
    half = value.shape[0] // 2
    return value + jnp.concatenate([recv[half:], recv[:half]], axis=0)


def add_x(value, recv):
    q = value.shape[0] // 4
    order = (1, 0, 3, 2)
    return value + jnp.concatenate([recv[o * q : (o + 1) * q] for o in order], axis=0)


def add_z(value, recv, mask):
    shape = value.shape
    v, r = (w.reshape(4, 4, 2, shape[1]) for w in (value, recv))
    return (v + jnp.stack([r[:, q ^ mask] for q in range(4)], axis=1)).reshape(shape)


def shared_device(tokens, gate_weight, up_weight, a_gate, a_up, b_gate, b_up, agent, d_hidden):
    group = lax.axis_index("group")
    t = lax.axis_index("tensor")
    side = group.astype(jnp.int32).reshape(1)
    d = tokens.shape[1]
    half = d // 2
    feat_rows = a_gate.shape[0]
    per_half = half // feat_rows
    rows = 2 * N
    ff = b_gate.shape[1]

    recv = along_tensor(tokens, 4)
    a_gate, a_up = narrow(a_gate, a_up, feat_rows // 2)
    recv, a_gate, a_up = in_order(recv, a_gate, a_up)
    line = jnp.concatenate([tokens, recv], axis=0)
    line = jnp.concatenate([line, along_tensor(line, 8)], axis=0)
    mine = lax.dynamic_slice_in_dim(line, group * half, half, 1)
    other = lax.dynamic_slice_in_dim(line, half - group * half, half, 1)
    parts = [along_tensor(mine, X), across_groups(other), across_groups(other, X)]
    x = jnp.stack(
        [jnp.concatenate([mine, parts[0]], axis=0), jnp.concatenate([parts[1], parts[2]], axis=0)]
    )
    x = jnp.concatenate([x, along_tensor(x, CORE)], axis=1).reshape(2 * rows, half)

    place = jnp.arange(rows, dtype=jnp.int32)
    block = ((place >> 1) & 3) * 4 + ((place >> 3) & 1) * 2 + (place >> 4)
    token_of = ((t ^ block) << 1) + (place & 1)
    shuffle = token_of[:, None] == jnp.arange(rows, dtype=jnp.int32)[None, :]
    agent_here = jnp.sum(jnp.where(shuffle, agent[None, :], 0), axis=1)
    chosen = agent_here[:, None] == (jnp.arange(AG * R, dtype=jnp.int32) // R)[None, :]
    hidden_grad = jnp.dot(shuffle.astype(BF16), d_hidden, preferred_element_type=F32)

    def select(values):
        kept = jnp.where(chosen, values, 0.0)
        pair = sum(kept[:, c : c + 2 * R] for c in range(0, AG * R, 2 * R))
        return pair[:, :R] + pair[:, R:]

    def spread(small):
        wide = jnp.concatenate([small] * AG, axis=1)
        return jnp.where(chosen, wide, 0.0).astype(BF16)

    blocks = lax.dynamic_slice_in_dim(x, (t % per_half) * feat_rows, feat_rows, 1)
    swapped = across_groups(blocks[rows:])
    cuts = [ff * c // 7 for c in (0, 2, 4, 6, 7)]

    def forward(c):
        return forward_products(
            side, x, gate_weight, up_weight, cuts[c], cuts[c + 1] - cuts[c]
        )

    keep_0, send_0 = forward(0)
    swapped, x, keep_0, send_0 = in_order(swapped, x, keep_0, send_0)
    own_cols = jnp.where(t // per_half == group, blocks[:rows], swapped)
    part = jnp.concatenate(
        [
            select(jnp.dot(own_cols, a_gate, preferred_element_type=F32)),
            select(jnp.dot(own_cols, a_up, preferred_element_type=F32)),
        ],
        axis=1,
    )

    part = add_core(part, along_tensor(part, CORE))
    part, x = in_order(part, x)
    recv = along_tensor(part, X)
    keep_1, send_1 = forward(1)
    recv, x, keep_1, send_1 = in_order(recv, x, keep_1, send_1)
    part = add_x(part, recv)

    recv = along_tensor(part, 4)
    keep_2, send_2 = forward(2)
    recv, x, keep_2, send_2 = in_order(recv, x, keep_2, send_2)
    part = add_z(part, recv, 1)

    recv = along_tensor(part, 8)
    far_a = across_groups(jnp.concatenate([send_0, send_1, send_2], axis=2))
    keep_3, send_3 = forward(3)
    far_a, recv, keep_3, send_3 = in_order(far_a, recv, keep_3, send_3)
    far_b = across_groups(send_3)
    part = add_z(part, recv, 2)
    u = part.astype(BF16).astype(F32)
    up_factor_gate = spread(u[:, :R])
    up_factor_up = spread(u[:, R:])

    def hidden(keep, far, first, width):
        return hidden_gradients(
            up_factor_gate, up_factor_up, b_gate, b_up, keep, far, hidden_grad, first, width
        )

    keep = jnp.concatenate([keep_0, keep_1, keep_2], axis=2)
    own_a, pg_a, pu_a = hidden(keep, far_a, 0, 512)
    far_b, own_a = in_order(far_b, own_a)
    own_b, pg_b, pu_b = hidden(keep_3, far_b, cuts[3], 256)
    own = jnp.concatenate([own_a, own_b], axis=2)
    far = across_groups(own)
    part = jnp.concatenate([select(pg_a + pg_b), select(pu_a + pu_b)], axis=1)
    part, own = in_order(part, own)
    recv = along_tensor(part, CORE)
    gate_lift_gradient = adapter_scale * rows_product(up_factor_gate, own[0])
    far, recv, gate_lift_gradient = in_order(far, recv, gate_lift_gradient)
    part = add_core(part, recv)
    both = jnp.concatenate([own, far], axis=1)
    dg, du = both[0], both[1]

    count = half // 8

    def backward(c, n):
        return backward_products(side, dg, du, gate_weight, up_weight, c * count, n * count)

    recv = along_tensor(part, X)
    keep_0, send_0 = backward(0, 1)
    recv, dg, du, keep_0, send_0 = in_order(recv, dg, du, keep_0, send_0)
    part = add_x(part, recv)

    recv = along_tensor(part, 4)
    keep_1, send_1 = backward(1, 1)
    recv, dg, du, keep_1, send_1 = in_order(recv, dg, du, keep_1, send_1)
    part = add_z(part, recv, 1)

    recv = along_tensor(part, 8)
    keep_2, send_2 = backward(2, 6)
    recv, keep_2, send_2, own, own_cols = in_order(recv, keep_2, send_2, own, own_cols)
    part = add_z(part, recv, 2)
    far = along_tensor(jnp.concatenate([send_0, send_1, send_2], axis=1), CORE)
    g = part.astype(BF16).astype(F32)
    gate_factor_gate = spread(g[:, :R])
    gate_factor_up = spread(g[:, R:])
    moved = (
        adapter_scale
        * (
            flipped_product(gate_factor_gate, a_gate)
            + flipped_product(gate_factor_up, a_up)
        )
    ).astype(BF16)

    far_moved = along_tensor(moved[16:], CORE)
    far, far_moved, own_cols = in_order(far, far_moved, own_cols)
    sums = jnp.concatenate([keep_0, keep_1, keep_2], axis=1) + far.astype(F32)
    moved = jnp.concatenate([moved[:16], far_moved], axis=1)

    low = sums.astype(BF16)
    parts = [
        along_tensor(jnp.concatenate([low[8:16], moved[8:]], axis=1), X),
        across_groups(low[16:24]),
        across_groups(low[24:], X),
    ]
    gate_down_gradient = adapter_scale * rows_product(own_cols, gate_factor_gate)
    up_down_gradient = adapter_scale * rows_product(own_cols, gate_factor_up)
    gate_down_gradient, up_down_gradient, own, *parts = in_order(
        gate_down_gradient, up_down_gradient, own, *parts
    )
    near = sums[:8] + parts[0][:, :half].astype(F32)
    sums = jnp.concatenate([near, parts[1].astype(F32) + parts[2].astype(F32)], axis=1)
    moved = jnp.concatenate([moved[:8], parts[0][:, half:]], axis=1)

    low = jnp.concatenate([sums.astype(BF16), moved], axis=1)
    parts = from_far_z([low[2 * m : 2 * m + 2] for m in (1, 2, 3)])
    up_lift_gradient = adapter_scale * rows_product(up_factor_up, own[1])
    up_lift_gradient, *parts = in_order(up_lift_gradient, *parts)
    sums = sums[:2] + sum(p[:, :d].astype(F32) for p in parts)
    moved = jnp.stack([moved[:2]] + [p[:, d:] for p in parts])
    moved = moved.reshape(4, 2, 2, 2, feat_rows).transpose(0, 2, 3, 1, 4).reshape(N, 2 * feat_rows)
    source = jnp.arange(N, dtype=jnp.int32)
    sort = (source[:, None] == (t ^ source)[None, :]).astype(BF16)
    sorted_rows = jnp.dot(sort, moved, preferred_element_type=F32).reshape(N, 2, feat_rows)
    contribution = sorted_rows.transpose(1, 0, 2).reshape(2, d)
    near, far = sums[:, :half], sums[:, half:]
    sums = jnp.where(
        group == 0, jnp.concatenate([near, far], axis=1), jnp.concatenate([far, near], axis=1)
    )
    token_gradient = (sums + contribution).astype(BF16)
    return (
        token_gradient,
        gate_down_gradient,
        up_down_gradient,
        gate_lift_gradient,
        up_lift_gradient,
    )


def solution(mesh):
    sizes = dict(mesh.shape)

    def per_device(*args):
        tokens, b_gate = args[0], args[5]
        fits = (
            sizes["group"] == 2
            and sizes["tensor"] == N
            and tokens.shape[0] == 2
            and b_gate.shape[1] % 1792 == 0
            and tokens.shape[1] % 4096 == 0
        )
        return (shared_device if fits else plain_device)(*args)

    in_specs = (
        P(("group", "tensor"), None),
        P(None, "tensor"),
        P(None, "tensor"),
        P(("group", "tensor"), None),
        P(("group", "tensor"), None),
        P("group", "tensor"),
        P("group", "tensor"),
        P("group"),
        P("group", "tensor"),
    )
    out_specs = (
        P(("group", "tensor"), None),
        P(("group", "tensor"), None),
        P(("group", "tensor"), None),
        P("group", "tensor"),
        P("group", "tensor"),
    )
    return jax.shard_map(
        per_device, mesh=mesh, in_specs=in_specs, out_specs=out_specs, check_vma=False
    )
```

```python
import functools

import jax
import jax.numpy as jnp
from jax import lax
from jax.experimental import pallas as pl
from jax.experimental.pallas import tpu as pltpu
from jax.sharding import PartitionSpec as P

R = 64
AG = 16

adapter_scale = 2.0
BF16 = jnp.bfloat16
F32 = jnp.float32


def agent_mask(agent):
    return (agent[:, None] == jnp.arange(AG, dtype=jnp.int32)[None, :]).astype(jnp.float32)


def select_rank(values, onehot):
    shaped = values.reshape(values.shape[0], AG, R)
    return jnp.sum(shaped * onehot[:, :, None], axis=1)


def spread_rank(small, onehot):
    wide = onehot[:, :, None] * small.astype(jnp.float32)[:, None, :]
    return wide.reshape(small.shape[0], AG * R).astype(jnp.bfloat16)


def flipped_product(left, weight):
    return lax.dot_general(
        left, weight, (((1,), (1,)), ((), ())), preferred_element_type=jnp.float32
    )


def rows_product(left, right):
    return lax.dot_general(
        left, right, (((0,), (0,)), ((), ())), preferred_element_type=jnp.float32
    )


def plain_device(tokens, gate_weight, up_weight, a_gate, a_up, b_gate, b_up, agent, d_hidden):
    onehot = agent_mask(agent)
    feat_rows = a_gate.shape[0]
    feat_start = lax.axis_index("tensor") * feat_rows
    agent_gate_down = a_gate.astype(jnp.bfloat16)
    agent_up_down = a_up.astype(jnp.bfloat16)
    agent_gate_lift = b_gate.astype(jnp.bfloat16)
    agent_up_lift = b_up.astype(jnp.bfloat16)
    complete_result = lax.all_gather(tokens, "tensor", axis=0, tiled=True)
    own_cols = lax.dynamic_slice_in_dim(complete_result, feat_start, feat_rows, 1)
    part_gate = select_rank(
        jnp.dot(own_cols, agent_gate_down, preferred_element_type=jnp.float32), onehot
    )
    part_up = select_rank(
        jnp.dot(own_cols, agent_up_down, preferred_element_type=jnp.float32), onehot
    )
    u_gate, u_up = lax.psum((part_gate, part_up), "tensor")
    up_factor_gate = spread_rank(u_gate.astype(jnp.bfloat16), onehot)
    up_factor_up = spread_rank(u_up.astype(jnp.bfloat16), onehot)
    gate_values = jnp.dot(
        complete_result, gate_weight, preferred_element_type=jnp.float32
    ) + adapter_scale * jnp.dot(up_factor_gate, agent_gate_lift, preferred_element_type=jnp.float32)
    up_values = jnp.dot(
        complete_result, up_weight, preferred_element_type=jnp.float32
    ) + adapter_scale * jnp.dot(up_factor_up, agent_up_lift, preferred_element_type=jnp.float32)
    sig = jax.nn.sigmoid(gate_values)
    hidden_grad = d_hidden.astype(jnp.float32)
    gate_gradient = (hidden_grad * up_values * sig * (1.0 + gate_values * (1.0 - sig))).astype(
        jnp.bfloat16
    )
    up_gradient = (hidden_grad * gate_values * sig).astype(jnp.bfloat16)
    pg_gate = select_rank(flipped_product(gate_gradient, agent_gate_lift), onehot)
    pg_up = select_rank(flipped_product(up_gradient, agent_up_lift), onehot)
    g_gate, g_up = lax.psum((pg_gate, pg_up), "tensor")
    gate_factor_gate = spread_rank(g_gate.astype(jnp.bfloat16), onehot)
    gate_factor_up = spread_rank(g_up.astype(jnp.bfloat16), onehot)
    adapter_contribution = adapter_scale * (
        flipped_product(gate_factor_gate, agent_gate_down)
        + flipped_product(gate_factor_up, agent_up_down)
    )
    base_rows = flipped_product(gate_gradient, gate_weight) + flipped_product(
        up_gradient, up_weight
    )
    joined = lax.dynamic_slice_in_dim(base_rows, feat_start, feat_rows, 1) + adapter_contribution
    token_gradient = lax.psum_scatter(
        lax.dynamic_update_slice_in_dim(base_rows, joined, feat_start, 1),
        "tensor",
        scatter_dimension=0,
        tiled=True,
    ).astype(jnp.bfloat16)
    gate_down_gradient = adapter_scale * rows_product(own_cols, gate_factor_gate)
    up_down_gradient = adapter_scale * rows_product(own_cols, gate_factor_up)
    gate_lift_gradient = adapter_scale * rows_product(up_factor_gate, gate_gradient)
    up_lift_gradient = adapter_scale * rows_product(up_factor_up, up_gradient)
    return (
        token_gradient,
        gate_down_gradient,
        up_down_gradient,
        gate_lift_gradient,
        up_lift_gradient,
    )


def forward_kernel(first, side_ref, x_ref, w_ref, keep_ref, send_ref, piece, sem):
    pieces, depth, count = piece.shape
    half = keep_ref.shape[0]
    base = side_ref[0] * (pieces * depth)
    copies = []
    for k in range(pieces):
        source = pl.ds(pl.multiple_of(base + k * depth, depth), depth)
        copy = pltpu.make_async_copy(w_ref.at[source, pl.ds(first, count)], piece.at[k], sem.at[k])
        copy.start()
        copies.append(copy)
    total = None
    step = 2
    for k in range(0, pieces, step):
        for copy in copies[k : k + step]:
            copy.wait()
        term = jnp.dot(
            x_ref[:, k * depth : (k + step) * depth],
            piece[k : k + step].reshape(step * depth, count),
            preferred_element_type=F32,
        )
        total = term if total is None else total + term
    keep_ref[...] = total[:half]
    send_ref[...] = total[half:].astype(send_ref.dtype)


def forward_products(side, x, weight, first, count, pieces=8):
    rows, depth = x.shape
    vmem = pl.BlockSpec(memory_space=pltpu.VMEM)
    return pl.pallas_call(
        functools.partial(forward_kernel, first),
        in_specs=[
            pl.BlockSpec(memory_space=pltpu.SMEM),
            vmem,
            pl.BlockSpec(memory_space=pltpu.HBM),
        ],
        out_specs=[vmem] * 2,
        out_shape=[jax.ShapeDtypeStruct((rows // 2, count), kind) for kind in (F32, BF16)],
        scratch_shapes=[
            pltpu.VMEM((pieces, depth // pieces, count), BF16),
            pltpu.SemaphoreType.DMA((pieces,)),
        ],
        compiler_params=pltpu.CompilerParams(vmem_limit_bytes=20 << 20),
        cost_estimate=pl.CostEstimate(
            flops=2 * rows * count * depth, bytes_accessed=3 * count * depth, transcendentals=0
        ),
        name="forward_products",
    )(side, x, pltpu.with_memory_space_constraint(weight, pltpu.HBM))


def narrow_kernel(g_ref, u_ref, g16_ref, u16_ref):
    g16_ref[...] = g_ref[...].astype(BF16)
    u16_ref[...] = u_ref[...].astype(BF16)


def narrow(gate, up, depth):
    rows, width = gate.shape
    block = pl.BlockSpec((depth, width), lambda k: (k, 0))
    return pl.pallas_call(
        narrow_kernel,
        grid=(rows // depth,),
        in_specs=[block] * 2,
        out_specs=[block] * 2,
        out_shape=[jax.ShapeDtypeStruct(gate.shape, BF16)] * 2,
        compiler_params=pltpu.CompilerParams(vmem_limit_bytes=16 << 20),
        cost_estimate=pl.CostEstimate(flops=0, bytes_accessed=12 * rows * width, transcendentals=0),
        name="narrow",
    )(
        pltpu.with_memory_space_constraint(gate, pltpu.HBM),
        pltpu.with_memory_space_constraint(up, pltpu.HBM),
    )


def hidden_kernel(
    first, step, eug_ref, euu_ref, keep_ref, far_ref, dh_ref, bg_ref, bu_ref, d_ref, pg_ref, pu_ref,
    b_ref, sem
):
    blocks, _, pieces = sem.shape
    depth = b_ref.shape[2] // pieces

    def copies(block):
        return [
            pltpu.make_async_copy(
                ref.at[pl.ds(k * depth, depth), pl.ds(first + block * step, step)],
                b_ref.at[block, i, pl.ds(k * depth, depth)],
                sem.at[block, i, k],
            )
            for i, ref in enumerate((bg_ref, bu_ref))
            for k in range(pieces)
        ]

    running = [copies(block) for block in range(blocks)]
    for block in range(min(2, blocks)):
        for copy in running[block]:
            copy.start()
    for block in range(blocks):
        for copy in running[block]:
            copy.wait()
        if block + 2 < blocks:
            for copy in running[block + 2]:
                copy.start()
        at = pl.ds(block * step, step)
        bg = b_ref[block, 0].astype(BF16)
        bu = b_ref[block, 1].astype(BF16)
        gate = (
            keep_ref[0, :, at]
            + far_ref[0, :, at].astype(F32)
            + adapter_scale * jnp.dot(eug_ref[...], bg, preferred_element_type=F32)
        )
        up = (
            keep_ref[1, :, at]
            + far_ref[1, :, at].astype(F32)
            + adapter_scale * jnp.dot(euu_ref[...], bu, preferred_element_type=F32)
        )
        sig = jax.nn.sigmoid(gate)
        hidden_grad = dh_ref[:, at]
        dg = (hidden_grad * up * sig * (1.0 + gate * (1.0 - sig))).astype(BF16)
        du = (hidden_grad * gate * sig).astype(BF16)
        d_ref[0, :, at] = dg
        d_ref[1, :, at] = du
        if block == 0:
            pg_ref[...] = flipped_product(dg, bg)
            pu_ref[...] = flipped_product(du, bu)
        else:
            pg_ref[...] += flipped_product(dg, bg)
            pu_ref[...] += flipped_product(du, bu)


def hidden_gradients(eug, euu, b_gate, b_up, keep, far, hidden_grad, first, step, pieces=4):
    rows, wide = eug.shape
    count = keep.shape[2]
    vmem = pl.BlockSpec(memory_space=pltpu.VMEM)
    hbm = pl.BlockSpec(memory_space=pltpu.HBM)
    return pl.pallas_call(
        functools.partial(hidden_kernel, first, step),
        in_specs=[vmem] * 5 + [hbm] * 2,
        out_specs=[vmem] * 3,
        out_shape=[jax.ShapeDtypeStruct((2, rows, count), BF16)]
        + [jax.ShapeDtypeStruct((rows, wide), F32)] * 2,
        scratch_shapes=[
            pltpu.VMEM((count // step, 2, wide, step), F32),
            pltpu.SemaphoreType.DMA((count // step, 2, pieces)),
        ],
        compiler_params=pltpu.CompilerParams(vmem_limit_bytes=28 << 20),
        cost_estimate=pl.CostEstimate(
            flops=8 * rows * wide * count, bytes_accessed=12 * wide * count, transcendentals=0
        ),
        name="hidden_gradients",
    )(
        eug,
        euu,
        keep,
        far,
        hidden_grad[:, first : first + count],
        pltpu.with_memory_space_constraint(b_gate, pltpu.HBM),
        pltpu.with_memory_space_constraint(b_up, pltpu.HBM),
    )


def backward_kernel(first, side_ref, dg_ref, du_ref, wg_ref, wu_ref, keep_ref, send_ref, rows_ref, sem):
    pieces = sem.shape[1]
    total_rows = rows_ref.shape[1]
    depth = total_rows // pieces
    base = side_ref[0] * (wg_ref.shape[0] // 2) + first
    copies = {}
    for j in range(pieces):
        for i, w_ref in enumerate((wg_ref, wu_ref)):
            source = pl.ds(pl.multiple_of(base + j * depth, depth), depth)
            copies[i, j] = pltpu.make_async_copy(
                w_ref.at[source], rows_ref.at[i, pl.ds(j * depth, depth)], sem.at[i, j]
            )

    def start(j):
        if j < pieces:
            for at in ((0, j), (0, j + 1), (1, j), (1, j + 1)):
                copies[at].start()

    start(0)
    start(2)
    q = dg_ref.shape[0] // 4
    step = 2 * depth
    for k in range(0, total_rows, step):
        j = k // depth
        copies[0, j].wait()
        copies[0, j + 1].wait()
        copies[1, j].wait()
        copies[1, j + 1].wait()
        start(j + 4)
        total = flipped_product(dg_ref[...], rows_ref[0, k : k + step])
        total += flipped_product(du_ref[...], rows_ref[1, k : k + step])
        out = pl.ds(k, step)
        keep_ref[:q, out] = total[:q]
        keep_ref[q:, out] = total[2 * q : 3 * q]
        send_ref[:q, out] = total[q : 2 * q].astype(send_ref.dtype)
        send_ref[q:, out] = total[3 * q :].astype(send_ref.dtype)


def backward_products(side, dg, du, gate_weight, up_weight, first, count, depth=256):
    rows, ff = dg.shape
    vmem = pl.BlockSpec(memory_space=pltpu.VMEM)
    hbm = pl.BlockSpec(memory_space=pltpu.HBM)
    return pl.pallas_call(
        functools.partial(backward_kernel, first),
        in_specs=[pl.BlockSpec(memory_space=pltpu.SMEM), vmem, vmem, hbm, hbm],
        out_specs=[vmem] * 2,
        out_shape=[
            jax.ShapeDtypeStruct((rows // 2, count), F32),
            jax.ShapeDtypeStruct((rows // 2, count), BF16),
        ],
        scratch_shapes=[
            pltpu.VMEM((2, count, ff), BF16),
            pltpu.SemaphoreType.DMA((2, count // depth)),
        ],
        compiler_params=pltpu.CompilerParams(vmem_limit_bytes=36 << 20),
        cost_estimate=pl.CostEstimate(
            flops=4 * rows * count * ff, bytes_accessed=6 * count * ff, transcendentals=0
        ),
        name="backward_products",
    )(
        side,
        dg,
        du,
        pltpu.with_memory_space_constraint(gate_weight, pltpu.HBM),
        pltpu.with_memory_space_constraint(up_weight, pltpu.HBM),
    )


N = 16
CORE, X = 1, 2


def along_tensor(value, mask):
    return lax.ppermute(value, "tensor", [(i, i ^ mask) for i in range(N)])


def across_groups(value, mask=0):
    both = ("group", "tensor")
    return lax.ppermute(value, both, [(i, i ^ (N | mask)) for i in range(2 * N)])


def from_far_z(values):
    return [along_tensor(v, 4 * m) for m, v in zip((1, 2, 3), values)]


def in_order(*values):
    return lax.optimization_barrier(values)


def add_core(value, recv):
    half = value.shape[0] // 2
    return value + jnp.concatenate([recv[half:], recv[:half]], axis=0)


def add_x(value, recv):
    q = value.shape[0] // 4
    order = (1, 0, 3, 2)
    return value + jnp.concatenate([recv[o * q : (o + 1) * q] for o in order], axis=0)


def add_z(value, recv, mask):
    shape = value.shape
    v, r = (w.reshape(4, 4, 2, shape[1]) for w in (value, recv))
    return (v + jnp.stack([r[:, q ^ mask] for q in range(4)], axis=1)).reshape(shape)


def shared_device(tokens, gate_weight, up_weight, a_gate, a_up, b_gate, b_up, agent, d_hidden):
    group = lax.axis_index("group")
    t = lax.axis_index("tensor")
    side = group.astype(jnp.int32).reshape(1)
    d = tokens.shape[1]
    half = d // 2
    feat_rows = a_gate.shape[0]
    per_half = half // feat_rows
    rows = 2 * N
    ff = b_gate.shape[1]

    recv = along_tensor(tokens, 4)
    a_gate, a_up = narrow(a_gate, a_up, feat_rows // 2)
    recv, a_gate, a_up = in_order(recv, a_gate, a_up)
    line = jnp.concatenate([tokens, recv], axis=0)
    line = jnp.concatenate([line, along_tensor(line, 8)], axis=0)
    mine = lax.dynamic_slice_in_dim(line, group * half, half, 1)
    other = lax.dynamic_slice_in_dim(line, half - group * half, half, 1)
    parts = [along_tensor(mine, X), across_groups(other), across_groups(other, X)]
    x = jnp.stack(
        [jnp.concatenate([mine, parts[0]], axis=0), jnp.concatenate([parts[1], parts[2]], axis=0)]
    )
    x = jnp.concatenate([x, along_tensor(x, CORE)], axis=1).reshape(2 * rows, half)

    place = jnp.arange(rows, dtype=jnp.int32)
    block = ((place >> 1) & 3) * 4 + ((place >> 3) & 1) * 2 + (place >> 4)
    token_of = ((t ^ block) << 1) + (place & 1)
    shuffle = token_of[:, None] == jnp.arange(rows, dtype=jnp.int32)[None, :]
    agent_here = jnp.sum(jnp.where(shuffle, agent[None, :], 0), axis=1)
    chosen = agent_here[:, None] == (jnp.arange(AG * R, dtype=jnp.int32) // R)[None, :]
    hidden_grad = jnp.dot(shuffle.astype(BF16), d_hidden, preferred_element_type=F32)

    def select(values):
        kept = jnp.where(chosen, values, 0.0)
        pair = sum(kept[:, c : c + 2 * R] for c in range(0, AG * R, 2 * R))
        return pair[:, :R] + pair[:, R:]

    def spread(small):
        wide = jnp.concatenate([small] * AG, axis=1)
        return jnp.where(chosen, wide, 0.0).astype(BF16)

    blocks = lax.dynamic_slice_in_dim(x, (t % per_half) * feat_rows, feat_rows, 1)
    swapped = across_groups(blocks[rows:])
    cut = ff * 4 // 7

    def forward(weight, late):
        first, count = (cut, ff - cut) if late else (0, cut)
        return forward_products(side, x, weight, first, count)

    keep_0, send_0 = forward(gate_weight, False)
    swapped, x, keep_0, send_0 = in_order(swapped, x, keep_0, send_0)
    own_cols = jnp.where(t // per_half == group, blocks[:rows], swapped)
    part = jnp.concatenate(
        [
            select(jnp.dot(own_cols, a_gate, preferred_element_type=F32)),
            select(jnp.dot(own_cols, a_up, preferred_element_type=F32)),
        ],
        axis=1,
    )

    part = add_core(part, along_tensor(part, CORE))
    part, x = in_order(part, x)
    recv = along_tensor(part, X)
    keep_1, send_1 = forward(up_weight, False)
    recv, x, keep_1, send_1 = in_order(recv, x, keep_1, send_1)
    part = add_x(part, recv)

    recv = along_tensor(part, 4)
    far_a = across_groups(jnp.stack([send_0, send_1]))
    keep_2, send_2 = forward(gate_weight, True)
    recv, far_a, x, keep_2, send_2 = in_order(recv, far_a, x, keep_2, send_2)
    part = add_z(part, recv, 1)

    recv = along_tensor(part, 8)
    keep_3, send_3 = forward(up_weight, True)
    recv, keep_3, send_3 = in_order(recv, keep_3, send_3)
    far_b = across_groups(jnp.stack([send_2, send_3]))
    part = add_z(part, recv, 2)
    u = part.astype(BF16).astype(F32)
    up_factor_gate = spread(u[:, :R])
    up_factor_up = spread(u[:, R:])

    def hidden(keep, far, first, width):
        return hidden_gradients(
            up_factor_gate, up_factor_up, b_gate, b_up, keep, far, hidden_grad, first, width
        )

    own_a, pg_a, pu_a = hidden(jnp.stack([keep_0, keep_1]), far_a, 0, 512)
    far_b, own_a = in_order(far_b, own_a)
    own_b, pg_b, pu_b = hidden(jnp.stack([keep_2, keep_3]), far_b, cut, 256)
    own = jnp.concatenate([own_a, own_b], axis=2)
    far = across_groups(own)
    part = jnp.concatenate([select(pg_a + pg_b), select(pu_a + pu_b)], axis=1)
    part, own = in_order(part, own)
    recv = along_tensor(part, CORE)
    gate_lift_gradient = adapter_scale * rows_product(up_factor_gate, own[0])
    far, recv, gate_lift_gradient = in_order(far, recv, gate_lift_gradient)
    part = add_core(part, recv)
    both = jnp.concatenate([own, far], axis=1)
    dg, du = both[0], both[1]

    count = half // 8

    def backward(c, n):
        return backward_products(side, dg, du, gate_weight, up_weight, c * count, n * count)

    recv = along_tensor(part, X)
    keep_0, send_0 = backward(0, 1)
    recv, dg, du, keep_0, send_0 = in_order(recv, dg, du, keep_0, send_0)
    part = add_x(part, recv)

    recv = along_tensor(part, 4)
    keep_1, send_1 = backward(1, 1)
    recv, dg, du, keep_1, send_1 = in_order(recv, dg, du, keep_1, send_1)
    part = add_z(part, recv, 1)

    recv = along_tensor(part, 8)
    keep_2, send_2 = backward(2, 6)
    recv, keep_2, send_2, own, own_cols = in_order(recv, keep_2, send_2, own, own_cols)
    part = add_z(part, recv, 2)
    far = along_tensor(jnp.concatenate([send_0, send_1, send_2], axis=1), CORE)
    g = part.astype(BF16).astype(F32)
    gate_factor_gate = spread(g[:, :R])
    gate_factor_up = spread(g[:, R:])
    moved = (
        adapter_scale
        * (
            flipped_product(gate_factor_gate, a_gate)
            + flipped_product(gate_factor_up, a_up)
        )
    ).astype(BF16)

    far_moved = along_tensor(moved[16:], CORE)
    far, far_moved, own_cols = in_order(far, far_moved, own_cols)
    sums = jnp.concatenate([keep_0, keep_1, keep_2], axis=1) + far.astype(F32)
    moved = jnp.concatenate([moved[:16], far_moved], axis=1)

    low = sums.astype(BF16)
    parts = [
        along_tensor(jnp.concatenate([low[8:16], moved[8:]], axis=1), X),
        across_groups(low[16:24]),
        across_groups(low[24:], X),
    ]
    gate_down_gradient = adapter_scale * rows_product(own_cols, gate_factor_gate)
    up_down_gradient = adapter_scale * rows_product(own_cols, gate_factor_up)
    gate_down_gradient, up_down_gradient, own, *parts = in_order(
        gate_down_gradient, up_down_gradient, own, *parts
    )
    near = sums[:8] + parts[0][:, :half].astype(F32)
    sums = jnp.concatenate([near, parts[1].astype(F32) + parts[2].astype(F32)], axis=1)
    moved = jnp.concatenate([moved[:8], parts[0][:, half:]], axis=1)

    low = jnp.concatenate([sums.astype(BF16), moved], axis=1)
    parts = from_far_z([low[2 * m : 2 * m + 2] for m in (1, 2, 3)])
    up_lift_gradient = adapter_scale * rows_product(up_factor_up, own[1])
    up_lift_gradient, *parts = in_order(up_lift_gradient, *parts)
    sums = sums[:2] + sum(p[:, :d].astype(F32) for p in parts)
    moved = jnp.stack([moved[:2]] + [p[:, d:] for p in parts])
    moved = moved.reshape(4, 2, 2, 2, feat_rows).transpose(0, 2, 3, 1, 4).reshape(N, 2 * feat_rows)
    source = jnp.arange(N, dtype=jnp.int32)
    sort = (source[:, None] == (t ^ source)[None, :]).astype(BF16)
    sorted_rows = jnp.dot(sort, moved, preferred_element_type=F32).reshape(N, 2, feat_rows)
    contribution = sorted_rows.transpose(1, 0, 2).reshape(2, d)
    near, far = sums[:, :half], sums[:, half:]
    sums = jnp.where(
        group == 0, jnp.concatenate([near, far], axis=1), jnp.concatenate([far, near], axis=1)
    )
    token_gradient = (sums + contribution).astype(BF16)
    return (
        token_gradient,
        gate_down_gradient,
        up_down_gradient,
        gate_lift_gradient,
        up_lift_gradient,
    )


def solution(mesh):
    sizes = dict(mesh.shape)

    def per_device(*args):
        tokens, b_gate = args[0], args[5]
        fits = (
            sizes["group"] == 2
            and sizes["tensor"] == N
            and tokens.shape[0] == 2
            and b_gate.shape[1] % 1792 == 0
            and tokens.shape[1] % 4096 == 0
        )
        return (shared_device if fits else plain_device)(*args)

    in_specs = (
        P(("group", "tensor"), None),
        P(None, "tensor"),
        P(None, "tensor"),
        P(("group", "tensor"), None),
        P(("group", "tensor"), None),
        P("group", "tensor"),
        P("group", "tensor"),
        P("group"),
        P("group", "tensor"),
    )
    out_specs = (
        P(("group", "tensor"), None),
        P(("group", "tensor"), None),
        P(("group", "tensor"), None),
        P("group", "tensor"),
        P("group", "tensor"),
    )
    return jax.shard_map(
        per_device, mesh=mesh, in_specs=in_specs, out_specs=out_specs, check_vma=False
    )
```

```python
import functools

import jax
import jax.numpy as jnp
from jax import lax
from jax.experimental import pallas as pl
from jax.experimental.pallas import tpu as pltpu
from jax.sharding import PartitionSpec as P

R = 64
AG = 16

adapter_scale = 2.0
BF16 = jnp.bfloat16
F32 = jnp.float32


def agent_mask(agent):
    return (agent[:, None] == jnp.arange(AG, dtype=jnp.int32)[None, :]).astype(jnp.float32)


def select_rank(values, onehot):
    shaped = values.reshape(values.shape[0], AG, R)
    return jnp.sum(shaped * onehot[:, :, None], axis=1)


def spread_rank(small, onehot):
    wide = onehot[:, :, None] * small.astype(jnp.float32)[:, None, :]
    return wide.reshape(small.shape[0], AG * R).astype(jnp.bfloat16)


def flipped_product(left, weight):
    return lax.dot_general(
        left, weight, (((1,), (1,)), ((), ())), preferred_element_type=jnp.float32
    )


def rows_product(left, right):
    return lax.dot_general(
        left, right, (((0,), (0,)), ((), ())), preferred_element_type=jnp.float32
    )


def plain_device(tokens, gate_weight, up_weight, a_gate, a_up, b_gate, b_up, agent, d_hidden):
    onehot = agent_mask(agent)
    feat_rows = a_gate.shape[0]
    feat_start = lax.axis_index("tensor") * feat_rows
    agent_gate_down = a_gate.astype(jnp.bfloat16)
    agent_up_down = a_up.astype(jnp.bfloat16)
    agent_gate_lift = b_gate.astype(jnp.bfloat16)
    agent_up_lift = b_up.astype(jnp.bfloat16)
    complete_result = lax.all_gather(tokens, "tensor", axis=0, tiled=True)
    own_cols = lax.dynamic_slice_in_dim(complete_result, feat_start, feat_rows, 1)
    part_gate = select_rank(
        jnp.dot(own_cols, agent_gate_down, preferred_element_type=jnp.float32), onehot
    )
    part_up = select_rank(
        jnp.dot(own_cols, agent_up_down, preferred_element_type=jnp.float32), onehot
    )
    u_gate, u_up = lax.psum((part_gate, part_up), "tensor")
    up_factor_gate = spread_rank(u_gate.astype(jnp.bfloat16), onehot)
    up_factor_up = spread_rank(u_up.astype(jnp.bfloat16), onehot)
    gate_values = jnp.dot(
        complete_result, gate_weight, preferred_element_type=jnp.float32
    ) + adapter_scale * jnp.dot(up_factor_gate, agent_gate_lift, preferred_element_type=jnp.float32)
    up_values = jnp.dot(
        complete_result, up_weight, preferred_element_type=jnp.float32
    ) + adapter_scale * jnp.dot(up_factor_up, agent_up_lift, preferred_element_type=jnp.float32)
    sig = jax.nn.sigmoid(gate_values)
    hidden_grad = d_hidden.astype(jnp.float32)
    gate_gradient = (hidden_grad * up_values * sig * (1.0 + gate_values * (1.0 - sig))).astype(
        jnp.bfloat16
    )
    up_gradient = (hidden_grad * gate_values * sig).astype(jnp.bfloat16)
    pg_gate = select_rank(flipped_product(gate_gradient, agent_gate_lift), onehot)
    pg_up = select_rank(flipped_product(up_gradient, agent_up_lift), onehot)
    g_gate, g_up = lax.psum((pg_gate, pg_up), "tensor")
    gate_factor_gate = spread_rank(g_gate.astype(jnp.bfloat16), onehot)
    gate_factor_up = spread_rank(g_up.astype(jnp.bfloat16), onehot)
    adapter_contribution = adapter_scale * (
        flipped_product(gate_factor_gate, agent_gate_down)
        + flipped_product(gate_factor_up, agent_up_down)
    )
    base_rows = flipped_product(gate_gradient, gate_weight) + flipped_product(
        up_gradient, up_weight
    )
    joined = lax.dynamic_slice_in_dim(base_rows, feat_start, feat_rows, 1) + adapter_contribution
    token_gradient = lax.psum_scatter(
        lax.dynamic_update_slice_in_dim(base_rows, joined, feat_start, 1),
        "tensor",
        scatter_dimension=0,
        tiled=True,
    ).astype(jnp.bfloat16)
    gate_down_gradient = adapter_scale * rows_product(own_cols, gate_factor_gate)
    up_down_gradient = adapter_scale * rows_product(own_cols, gate_factor_up)
    gate_lift_gradient = adapter_scale * rows_product(up_factor_gate, gate_gradient)
    up_lift_gradient = adapter_scale * rows_product(up_factor_up, up_gradient)
    return (
        token_gradient,
        gate_down_gradient,
        up_down_gradient,
        gate_lift_gradient,
        up_lift_gradient,
    )


def forward_kernel(first, side_ref, x_ref, w_ref, keep_ref, send_ref, piece, sem):
    pieces, depth, count = piece.shape
    half = keep_ref.shape[0]
    base = side_ref[0] * (pieces * depth)
    copies = []
    for k in range(pieces):
        source = pl.ds(pl.multiple_of(base + k * depth, depth), depth)
        copy = pltpu.make_async_copy(w_ref.at[source, pl.ds(first, count)], piece.at[k], sem.at[k])
        copy.start()
        copies.append(copy)
    total = None
    step = 2
    for k in range(0, pieces, step):
        for copy in copies[k : k + step]:
            copy.wait()
        term = jnp.dot(
            x_ref[:, k * depth : (k + step) * depth],
            piece[k : k + step].reshape(step * depth, count),
            preferred_element_type=F32,
        )
        total = term if total is None else total + term
    keep_ref[...] = total[:half]
    send_ref[...] = total[half:].astype(send_ref.dtype)


def forward_products(side, x, weight, first, count, pieces=8):
    rows, depth = x.shape
    vmem = pl.BlockSpec(memory_space=pltpu.VMEM)
    return pl.pallas_call(
        functools.partial(forward_kernel, first),
        in_specs=[
            pl.BlockSpec(memory_space=pltpu.SMEM),
            vmem,
            pl.BlockSpec(memory_space=pltpu.HBM),
        ],
        out_specs=[vmem] * 2,
        out_shape=[jax.ShapeDtypeStruct((rows // 2, count), kind) for kind in (F32, BF16)],
        scratch_shapes=[
            pltpu.VMEM((pieces, depth // pieces, count), BF16),
            pltpu.SemaphoreType.DMA((pieces,)),
        ],
        compiler_params=pltpu.CompilerParams(vmem_limit_bytes=20 << 20),
        cost_estimate=pl.CostEstimate(
            flops=2 * rows * count * depth, bytes_accessed=3 * count * depth, transcendentals=0
        ),
        name="forward_products",
    )(side, x, pltpu.with_memory_space_constraint(weight, pltpu.HBM))


def narrow_kernel(g_ref, u_ref, g16_ref, u16_ref):
    g16_ref[...] = g_ref[...].astype(BF16)
    u16_ref[...] = u_ref[...].astype(BF16)


def narrow(gate, up, depth):
    rows, width = gate.shape
    block = pl.BlockSpec((depth, width), lambda k: (k, 0))
    return pl.pallas_call(
        narrow_kernel,
        grid=(rows // depth,),
        in_specs=[block] * 2,
        out_specs=[block] * 2,
        out_shape=[jax.ShapeDtypeStruct(gate.shape, BF16)] * 2,
        compiler_params=pltpu.CompilerParams(vmem_limit_bytes=16 << 20),
        cost_estimate=pl.CostEstimate(flops=0, bytes_accessed=12 * rows * width, transcendentals=0),
        name="narrow",
    )(
        pltpu.with_memory_space_constraint(gate, pltpu.HBM),
        pltpu.with_memory_space_constraint(up, pltpu.HBM),
    )


def hidden_kernel(
    first, step, eug_ref, euu_ref, keep_ref, far_ref, dh_ref, bg_ref, bu_ref, d_ref, pg_ref, pu_ref,
    b_ref, sem
):
    blocks, _, pieces = sem.shape
    depth = b_ref.shape[2] // pieces

    def copies(block):
        return [
            pltpu.make_async_copy(
                ref.at[pl.ds(k * depth, depth), pl.ds(first + block * step, step)],
                b_ref.at[block, i, pl.ds(k * depth, depth)],
                sem.at[block, i, k],
            )
            for i, ref in enumerate((bg_ref, bu_ref))
            for k in range(pieces)
        ]

    running = [copies(block) for block in range(blocks)]
    for block in range(min(2, blocks)):
        for copy in running[block]:
            copy.start()
    for block in range(blocks):
        for copy in running[block]:
            copy.wait()
        if block + 2 < blocks:
            for copy in running[block + 2]:
                copy.start()
        at = pl.ds(block * step, step)
        bg = b_ref[block, 0].astype(BF16)
        bu = b_ref[block, 1].astype(BF16)
        gate = (
            keep_ref[0, :, at]
            + far_ref[0, :, at].astype(F32)
            + adapter_scale * jnp.dot(eug_ref[...], bg, preferred_element_type=F32)
        )
        up = (
            keep_ref[1, :, at]
            + far_ref[1, :, at].astype(F32)
            + adapter_scale * jnp.dot(euu_ref[...], bu, preferred_element_type=F32)
        )
        sig = jax.nn.sigmoid(gate)
        hidden_grad = dh_ref[:, at]
        dg = (hidden_grad * up * sig * (1.0 + gate * (1.0 - sig))).astype(BF16)
        du = (hidden_grad * gate * sig).astype(BF16)
        d_ref[0, :, at] = dg
        d_ref[1, :, at] = du
        if block == 0:
            pg_ref[...] = flipped_product(dg, bg)
            pu_ref[...] = flipped_product(du, bu)
        else:
            pg_ref[...] += flipped_product(dg, bg)
            pu_ref[...] += flipped_product(du, bu)


def hidden_gradients(eug, euu, b_gate, b_up, keep, far, hidden_grad, first, step, pieces=4):
    rows, wide = eug.shape
    count = keep.shape[2]
    vmem = pl.BlockSpec(memory_space=pltpu.VMEM)
    hbm = pl.BlockSpec(memory_space=pltpu.HBM)
    return pl.pallas_call(
        functools.partial(hidden_kernel, first, step),
        in_specs=[vmem] * 5 + [hbm] * 2,
        out_specs=[vmem] * 3,
        out_shape=[jax.ShapeDtypeStruct((2, rows, count), BF16)]
        + [jax.ShapeDtypeStruct((rows, wide), F32)] * 2,
        scratch_shapes=[
            pltpu.VMEM((count // step, 2, wide, step), F32),
            pltpu.SemaphoreType.DMA((count // step, 2, pieces)),
        ],
        compiler_params=pltpu.CompilerParams(vmem_limit_bytes=28 << 20),
        cost_estimate=pl.CostEstimate(
            flops=8 * rows * wide * count, bytes_accessed=12 * wide * count, transcendentals=0
        ),
        name="hidden_gradients",
    )(
        eug,
        euu,
        keep,
        far,
        hidden_grad[:, first : first + count],
        pltpu.with_memory_space_constraint(b_gate, pltpu.HBM),
        pltpu.with_memory_space_constraint(b_up, pltpu.HBM),
    )


def backward_kernel(first, side_ref, dg_ref, du_ref, wg_ref, wu_ref, keep_ref, send_ref, rows_ref, sem):
    pieces = sem.shape[1]
    total_rows = rows_ref.shape[1]
    depth = total_rows // pieces
    base = side_ref[0] * (wg_ref.shape[0] // 2) + first
    copies = {}
    for j in range(pieces):
        for i, w_ref in enumerate((wg_ref, wu_ref)):
            source = pl.ds(pl.multiple_of(base + j * depth, depth), depth)
            copies[i, j] = pltpu.make_async_copy(
                w_ref.at[source], rows_ref.at[i, pl.ds(j * depth, depth)], sem.at[i, j]
            )

    def start(j):
        if j < pieces:
            for at in ((0, j), (0, j + 1), (1, j), (1, j + 1)):
                copies[at].start()

    start(0)
    start(2)
    q = dg_ref.shape[0] // 4
    step = 2 * depth
    for k in range(0, total_rows, step):
        j = k // depth
        copies[0, j].wait()
        copies[0, j + 1].wait()
        copies[1, j].wait()
        copies[1, j + 1].wait()
        start(j + 4)
        total = flipped_product(dg_ref[...], rows_ref[0, k : k + step])
        total += flipped_product(du_ref[...], rows_ref[1, k : k + step])
        out = pl.ds(k, step)
        keep_ref[:q, out] = total[:q]
        keep_ref[q:, out] = total[2 * q : 3 * q]
        send_ref[:q, out] = total[q : 2 * q].astype(send_ref.dtype)
        send_ref[q:, out] = total[3 * q :].astype(send_ref.dtype)


def backward_products(side, dg, du, gate_weight, up_weight, first, count, depth=256):
    rows, ff = dg.shape
    vmem = pl.BlockSpec(memory_space=pltpu.VMEM)
    hbm = pl.BlockSpec(memory_space=pltpu.HBM)
    return pl.pallas_call(
        functools.partial(backward_kernel, first),
        in_specs=[pl.BlockSpec(memory_space=pltpu.SMEM), vmem, vmem, hbm, hbm],
        out_specs=[vmem] * 2,
        out_shape=[
            jax.ShapeDtypeStruct((rows // 2, count), F32),
            jax.ShapeDtypeStruct((rows // 2, count), BF16),
        ],
        scratch_shapes=[
            pltpu.VMEM((2, count, ff), BF16),
            pltpu.SemaphoreType.DMA((2, count // depth)),
        ],
        compiler_params=pltpu.CompilerParams(vmem_limit_bytes=36 << 20),
        cost_estimate=pl.CostEstimate(
            flops=4 * rows * count * ff, bytes_accessed=6 * count * ff, transcendentals=0
        ),
        name="backward_products",
    )(
        side,
        dg,
        du,
        pltpu.with_memory_space_constraint(gate_weight, pltpu.HBM),
        pltpu.with_memory_space_constraint(up_weight, pltpu.HBM),
    )


def outer_kernel(pairs, *refs):
    ins, outs, parts, sem = refs[: 2 * pairs], refs[2 * pairs : 3 * pairs], refs[-2], refs[-1]
    depth = parts.shape[1]
    copies = []
    for i in range(pairs):
        left_ref, right_ref, out_ref = ins[2 * i], ins[2 * i + 1], outs[i]
        for k in range(0, out_ref.shape[0], depth):
            at = len(copies)
            parts[at] = adapter_scale * rows_product(left_ref[:, k : k + depth], right_ref[...])
            copy = pltpu.make_async_copy(parts.at[at], out_ref.at[pl.ds(k, depth)], sem.at[at])
            copy.start()
            copies.append(copy)
    for copy in copies:
        copy.wait()


def outer_products(*pairs, depth=128):
    shapes = [(left.shape[1], right.shape[1]) for left, right in pairs]
    count = sum(rows // depth for rows, _ in shapes)
    width = shapes[0][1]
    rows = pairs[0][0].shape[0]
    return pl.pallas_call(
        functools.partial(outer_kernel, len(pairs)),
        in_specs=[pl.BlockSpec(memory_space=pltpu.VMEM)] * (2 * len(pairs)),
        out_specs=[pl.BlockSpec(memory_space=pltpu.HBM)] * len(pairs),
        out_shape=[jax.ShapeDtypeStruct(shape, F32) for shape in shapes],
        scratch_shapes=[
            pltpu.VMEM((count, depth, width), F32),
            pltpu.SemaphoreType.DMA((count,)),
        ],
        compiler_params=pltpu.CompilerParams(vmem_limit_bytes=16 << 20),
        cost_estimate=pl.CostEstimate(
            flops=2 * count * depth * width * rows,
            bytes_accessed=4 * count * depth * width,
            transcendentals=0,
        ),
        name="outer_products",
    )(*[operand for pair in pairs for operand in pair])


N = 16
CORE, X = 1, 2


def along_tensor(value, mask):
    return lax.ppermute(value, "tensor", [(i, i ^ mask) for i in range(N)])


def across_groups(value, mask=0):
    both = ("group", "tensor")
    return lax.ppermute(value, both, [(i, i ^ (N | mask)) for i in range(2 * N)])


def from_far_z(values):
    return [along_tensor(v, 4 * m) for m, v in zip((1, 2, 3), values)]


def in_order(*values):
    return lax.optimization_barrier(values)


def add_core(value, recv):
    half = value.shape[0] // 2
    return value + jnp.concatenate([recv[half:], recv[:half]], axis=0)


def add_x(value, recv):
    q = value.shape[0] // 4
    order = (1, 0, 3, 2)
    return value + jnp.concatenate([recv[o * q : (o + 1) * q] for o in order], axis=0)


def add_z(value, recv, mask):
    shape = value.shape
    v, r = (w.reshape(4, 4, 2, shape[1]) for w in (value, recv))
    return (v + jnp.stack([r[:, q ^ mask] for q in range(4)], axis=1)).reshape(shape)


def shared_device(tokens, gate_weight, up_weight, a_gate, a_up, b_gate, b_up, agent, d_hidden):
    group = lax.axis_index("group")
    t = lax.axis_index("tensor")
    side = group.astype(jnp.int32).reshape(1)
    d = tokens.shape[1]
    half = d // 2
    feat_rows = a_gate.shape[0]
    per_half = half // feat_rows
    rows = 2 * N
    ff = b_gate.shape[1]

    recv = along_tensor(tokens, 4)
    a_gate, a_up = narrow(a_gate, a_up, feat_rows // 2)
    recv, a_gate, a_up = in_order(recv, a_gate, a_up)
    line = jnp.concatenate([tokens, recv], axis=0)
    line = jnp.concatenate([line, along_tensor(line, 8)], axis=0)
    mine = lax.dynamic_slice_in_dim(line, group * half, half, 1)
    other = lax.dynamic_slice_in_dim(line, half - group * half, half, 1)
    parts = [along_tensor(mine, X), across_groups(other), across_groups(other, X)]
    x = jnp.stack(
        [jnp.concatenate([mine, parts[0]], axis=0), jnp.concatenate([parts[1], parts[2]], axis=0)]
    )
    x = jnp.concatenate([x, along_tensor(x, CORE)], axis=1).reshape(2 * rows, half)

    place = jnp.arange(rows, dtype=jnp.int32)
    block = ((place >> 1) & 3) * 4 + ((place >> 3) & 1) * 2 + (place >> 4)
    token_of = ((t ^ block) << 1) + (place & 1)
    shuffle = token_of[:, None] == jnp.arange(rows, dtype=jnp.int32)[None, :]
    agent_here = jnp.sum(jnp.where(shuffle, agent[None, :], 0), axis=1)
    chosen = agent_here[:, None] == (jnp.arange(AG * R, dtype=jnp.int32) // R)[None, :]
    hidden_grad = jnp.dot(shuffle.astype(BF16), d_hidden, preferred_element_type=F32)

    def select(values):
        kept = jnp.where(chosen, values, 0.0)
        pair = sum(kept[:, c : c + 2 * R] for c in range(0, AG * R, 2 * R))
        return pair[:, :R] + pair[:, R:]

    def spread(small):
        wide = jnp.concatenate([small] * AG, axis=1)
        return jnp.where(chosen, wide, 0.0).astype(BF16)

    blocks = lax.dynamic_slice_in_dim(x, (t % per_half) * feat_rows, feat_rows, 1)
    swapped = across_groups(blocks[rows:])
    cut = ff * 4 // 7

    def forward(weight, late):
        first, count = (cut, ff - cut) if late else (0, cut)
        return forward_products(side, x, weight, first, count)

    keep_0, send_0 = forward(gate_weight, False)
    swapped, x, keep_0, send_0 = in_order(swapped, x, keep_0, send_0)
    own_cols = jnp.where(t // per_half == group, blocks[:rows], swapped)
    part = jnp.concatenate(
        [
            select(jnp.dot(own_cols, a_gate, preferred_element_type=F32)),
            select(jnp.dot(own_cols, a_up, preferred_element_type=F32)),
        ],
        axis=1,
    )

    part = add_core(part, along_tensor(part, CORE))
    part, x = in_order(part, x)
    recv = along_tensor(part, X)
    keep_1, send_1 = forward(up_weight, False)
    recv, x, keep_1, send_1 = in_order(recv, x, keep_1, send_1)
    part = add_x(part, recv)

    recv = along_tensor(part, 4)
    far_a = across_groups(jnp.stack([send_0, send_1]))
    keep_2, send_2 = forward(gate_weight, True)
    recv, far_a, x, keep_2, send_2 = in_order(recv, far_a, x, keep_2, send_2)
    part = add_z(part, recv, 1)

    recv = along_tensor(part, 8)
    keep_3, send_3 = forward(up_weight, True)
    recv, keep_3, send_3 = in_order(recv, keep_3, send_3)
    far_b = across_groups(jnp.stack([send_2, send_3]))
    part = add_z(part, recv, 2)
    u = part.astype(BF16).astype(F32)
    up_factor_gate = spread(u[:, :R])
    up_factor_up = spread(u[:, R:])

    def hidden(keep, far, first, width):
        return hidden_gradients(
            up_factor_gate, up_factor_up, b_gate, b_up, keep, far, hidden_grad, first, width
        )

    own_a, pg_a, pu_a = hidden(jnp.stack([keep_0, keep_1]), far_a, 0, 512)
    far_b, own_a = in_order(far_b, own_a)
    own_b, pg_b, pu_b = hidden(jnp.stack([keep_2, keep_3]), far_b, cut, 256)
    own = jnp.concatenate([own_a, own_b], axis=2)
    far = across_groups(own)
    part = jnp.concatenate([select(pg_a + pg_b), select(pu_a + pu_b)], axis=1)
    part, own = in_order(part, own)
    recv = along_tensor(part, CORE)
    (gate_lift_gradient,) = outer_products((up_factor_gate, own[0]))
    far, recv, gate_lift_gradient = in_order(far, recv, gate_lift_gradient)
    part = add_core(part, recv)
    both = jnp.concatenate([own, far], axis=1)
    dg, du = both[0], both[1]

    count = half // 8

    def backward(c, n):
        return backward_products(side, dg, du, gate_weight, up_weight, c * count, n * count)

    recv = along_tensor(part, X)
    keep_0, send_0 = backward(0, 1)
    recv, dg, du, keep_0, send_0 = in_order(recv, dg, du, keep_0, send_0)
    part = add_x(part, recv)

    recv = along_tensor(part, 4)
    keep_1, send_1 = backward(1, 1)
    recv, dg, du, keep_1, send_1 = in_order(recv, dg, du, keep_1, send_1)
    part = add_z(part, recv, 1)

    recv = along_tensor(part, 8)
    keep_2, send_2 = backward(2, 6)
    recv, keep_2, send_2, own, own_cols = in_order(recv, keep_2, send_2, own, own_cols)
    part = add_z(part, recv, 2)
    far = along_tensor(jnp.concatenate([send_0, send_1, send_2], axis=1), CORE)
    g = part.astype(BF16).astype(F32)
    gate_factor_gate = spread(g[:, :R])
    gate_factor_up = spread(g[:, R:])
    moved = (
        adapter_scale
        * (
            flipped_product(gate_factor_gate, a_gate)
            + flipped_product(gate_factor_up, a_up)
        )
    ).astype(BF16)

    far_moved = along_tensor(moved[16:], CORE)
    far, far_moved, own = in_order(far, far_moved, own)
    sums = jnp.concatenate([keep_0, keep_1, keep_2], axis=1) + far.astype(F32)
    moved = jnp.concatenate([moved[:16], far_moved], axis=1)

    low = sums.astype(BF16)
    parts = [
        along_tensor(jnp.concatenate([low[8:16], moved[8:]], axis=1), X),
        across_groups(low[16:24]),
        across_groups(low[24:], X),
    ]
    (up_lift_gradient,) = outer_products((up_factor_up, own[1]))
    up_lift_gradient, own_cols, *parts = in_order(up_lift_gradient, own_cols, *parts)
    near = sums[:8] + parts[0][:, :half].astype(F32)
    sums = jnp.concatenate([near, parts[1].astype(F32) + parts[2].astype(F32)], axis=1)
    moved = jnp.concatenate([moved[:8], parts[0][:, half:]], axis=1)

    low = jnp.concatenate([sums.astype(BF16), moved], axis=1)
    parts = from_far_z([low[2 * m : 2 * m + 2] for m in (1, 2, 3)])
    gate_down_gradient, up_down_gradient = outer_products(
        (own_cols, gate_factor_gate), (own_cols, gate_factor_up)
    )
    gate_down_gradient, up_down_gradient, *parts = in_order(
        gate_down_gradient, up_down_gradient, *parts
    )
    sums = sums[:2] + sum(p[:, :d].astype(F32) for p in parts)
    moved = jnp.stack([moved[:2]] + [p[:, d:] for p in parts])
    moved = moved.reshape(4, 2, 2, 2, feat_rows).transpose(0, 2, 3, 1, 4).reshape(N, 2 * feat_rows)
    source = jnp.arange(N, dtype=jnp.int32)
    sort = (source[:, None] == (t ^ source)[None, :]).astype(BF16)
    sorted_rows = jnp.dot(sort, moved, preferred_element_type=F32).reshape(N, 2, feat_rows)
    contribution = sorted_rows.transpose(1, 0, 2).reshape(2, d)
    near, far = sums[:, :half], sums[:, half:]
    sums = jnp.where(
        group == 0, jnp.concatenate([near, far], axis=1), jnp.concatenate([far, near], axis=1)
    )
    token_gradient = (sums + contribution).astype(BF16)
    return (
        token_gradient,
        gate_down_gradient,
        up_down_gradient,
        gate_lift_gradient,
        up_lift_gradient,
    )


def solution(mesh):
    sizes = dict(mesh.shape)

    def per_device(*args):
        tokens, b_gate = args[0], args[5]
        fits = (
            sizes["group"] == 2
            and sizes["tensor"] == N
            and tokens.shape[0] == 2
            and b_gate.shape[1] % 1792 == 0
            and tokens.shape[1] % 4096 == 0
        )
        return (shared_device if fits else plain_device)(*args)

    in_specs = (
        P(("group", "tensor"), None),
        P(None, "tensor"),
        P(None, "tensor"),
        P(("group", "tensor"), None),
        P(("group", "tensor"), None),
        P("group", "tensor"),
        P("group", "tensor"),
        P("group"),
        P("group", "tensor"),
    )
    out_specs = (
        P(("group", "tensor"), None),
        P(("group", "tensor"), None),
        P(("group", "tensor"), None),
        P("group", "tensor"),
        P("group", "tensor"),
    )
    return jax.shard_map(
        per_device, mesh=mesh, in_specs=in_specs, out_specs=out_specs, check_vma=False
    )
```

```python
import functools

import jax
import jax.numpy as jnp
from jax import lax
from jax.experimental import pallas as pl
from jax.experimental.pallas import tpu as pltpu
from jax.sharding import PartitionSpec as P

R = 64
AG = 16

adapter_scale = 2.0
BF16 = jnp.bfloat16
F32 = jnp.float32


def agent_mask(agent):
    return (agent[:, None] == jnp.arange(AG, dtype=jnp.int32)[None, :]).astype(jnp.float32)


def select_rank(values, onehot):
    shaped = values.reshape(values.shape[0], AG, R)
    return jnp.sum(shaped * onehot[:, :, None], axis=1)


def spread_rank(small, onehot):
    wide = onehot[:, :, None] * small.astype(jnp.float32)[:, None, :]
    return wide.reshape(small.shape[0], AG * R).astype(jnp.bfloat16)


def flipped_product(left, weight):
    return lax.dot_general(
        left, weight, (((1,), (1,)), ((), ())), preferred_element_type=jnp.float32
    )


def rows_product(left, right):
    return lax.dot_general(
        left, right, (((0,), (0,)), ((), ())), preferred_element_type=jnp.float32
    )


def plain_device(tokens, gate_weight, up_weight, a_gate, a_up, b_gate, b_up, agent, d_hidden):
    onehot = agent_mask(agent)
    feat_rows = a_gate.shape[0]
    feat_start = lax.axis_index("tensor") * feat_rows
    agent_gate_down = a_gate.astype(jnp.bfloat16)
    agent_up_down = a_up.astype(jnp.bfloat16)
    agent_gate_lift = b_gate.astype(jnp.bfloat16)
    agent_up_lift = b_up.astype(jnp.bfloat16)
    complete_result = lax.all_gather(tokens, "tensor", axis=0, tiled=True)
    own_cols = lax.dynamic_slice_in_dim(complete_result, feat_start, feat_rows, 1)
    part_gate = select_rank(
        jnp.dot(own_cols, agent_gate_down, preferred_element_type=jnp.float32), onehot
    )
    part_up = select_rank(
        jnp.dot(own_cols, agent_up_down, preferred_element_type=jnp.float32), onehot
    )
    u_gate, u_up = lax.psum((part_gate, part_up), "tensor")
    up_factor_gate = spread_rank(u_gate.astype(jnp.bfloat16), onehot)
    up_factor_up = spread_rank(u_up.astype(jnp.bfloat16), onehot)
    gate_values = jnp.dot(
        complete_result, gate_weight, preferred_element_type=jnp.float32
    ) + adapter_scale * jnp.dot(up_factor_gate, agent_gate_lift, preferred_element_type=jnp.float32)
    up_values = jnp.dot(
        complete_result, up_weight, preferred_element_type=jnp.float32
    ) + adapter_scale * jnp.dot(up_factor_up, agent_up_lift, preferred_element_type=jnp.float32)
    sig = jax.nn.sigmoid(gate_values)
    hidden_grad = d_hidden.astype(jnp.float32)
    gate_gradient = (hidden_grad * up_values * sig * (1.0 + gate_values * (1.0 - sig))).astype(
        jnp.bfloat16
    )
    up_gradient = (hidden_grad * gate_values * sig).astype(jnp.bfloat16)
    pg_gate = select_rank(flipped_product(gate_gradient, agent_gate_lift), onehot)
    pg_up = select_rank(flipped_product(up_gradient, agent_up_lift), onehot)
    g_gate, g_up = lax.psum((pg_gate, pg_up), "tensor")
    gate_factor_gate = spread_rank(g_gate.astype(jnp.bfloat16), onehot)
    gate_factor_up = spread_rank(g_up.astype(jnp.bfloat16), onehot)
    adapter_contribution = adapter_scale * (
        flipped_product(gate_factor_gate, agent_gate_down)
        + flipped_product(gate_factor_up, agent_up_down)
    )
    base_rows = flipped_product(gate_gradient, gate_weight) + flipped_product(
        up_gradient, up_weight
    )
    joined = lax.dynamic_slice_in_dim(base_rows, feat_start, feat_rows, 1) + adapter_contribution
    token_gradient = lax.psum_scatter(
        lax.dynamic_update_slice_in_dim(base_rows, joined, feat_start, 1),
        "tensor",
        scatter_dimension=0,
        tiled=True,
    ).astype(jnp.bfloat16)
    gate_down_gradient = adapter_scale * rows_product(own_cols, gate_factor_gate)
    up_down_gradient = adapter_scale * rows_product(own_cols, gate_factor_up)
    gate_lift_gradient = adapter_scale * rows_product(up_factor_gate, gate_gradient)
    up_lift_gradient = adapter_scale * rows_product(up_factor_up, up_gradient)
    return (
        token_gradient,
        gate_down_gradient,
        up_down_gradient,
        gate_lift_gradient,
        up_lift_gradient,
    )


def forward_kernel(first, side_ref, x_ref, w_ref, keep_ref, send_ref, piece, sem):
    pieces, depth, count = piece.shape
    half = keep_ref.shape[0]
    base = side_ref[0] * (pieces * depth)
    copies = []
    for k in range(pieces):
        source = pl.ds(pl.multiple_of(base + k * depth, depth), depth)
        copy = pltpu.make_async_copy(w_ref.at[source, pl.ds(first, count)], piece.at[k], sem.at[k])
        copy.start()
        copies.append(copy)
    total = None
    step = 2
    for k in range(0, pieces, step):
        for copy in copies[k : k + step]:
            copy.wait()
        term = jnp.dot(
            x_ref[:, k * depth : (k + step) * depth],
            piece[k : k + step].reshape(step * depth, count),
            preferred_element_type=F32,
        )
        total = term if total is None else total + term
    keep_ref[...] = total[:half]
    send_ref[...] = total[half:].astype(send_ref.dtype)


def forward_products(side, x, weight, first, count, pieces=8):
    rows, depth = x.shape
    vmem = pl.BlockSpec(memory_space=pltpu.VMEM)
    return pl.pallas_call(
        functools.partial(forward_kernel, first),
        in_specs=[
            pl.BlockSpec(memory_space=pltpu.SMEM),
            vmem,
            pl.BlockSpec(memory_space=pltpu.HBM),
        ],
        out_specs=[vmem] * 2,
        out_shape=[jax.ShapeDtypeStruct((rows // 2, count), kind) for kind in (F32, BF16)],
        scratch_shapes=[
            pltpu.VMEM((pieces, depth // pieces, count), BF16),
            pltpu.SemaphoreType.DMA((pieces,)),
        ],
        compiler_params=pltpu.CompilerParams(vmem_limit_bytes=20 << 20),
        cost_estimate=pl.CostEstimate(
            flops=2 * rows * count * depth, bytes_accessed=3 * count * depth, transcendentals=0
        ),
        name="forward_products",
    )(side, x, pltpu.with_memory_space_constraint(weight, pltpu.HBM))


def ahead_kernel(side_ref, w_ref, out_ref, again_ref, sem):
    pieces = sem.shape[0]
    depth = out_ref.shape[0] // pieces
    base = side_ref[0] * out_ref.shape[0]
    again_ref[0] = side_ref[0]
    copies = [
        pltpu.make_async_copy(
            w_ref.at[
                pl.ds(pl.multiple_of(base + k * depth, depth), depth), pl.ds(0, out_ref.shape[1])
            ],
            out_ref.at[pl.ds(k * depth, depth)],
            sem.at[k],
        )
        for k in range(pieces)
    ]
    for copy in copies:
        copy.start()
    for copy in copies:
        copy.wait()


def columns_ahead(side, weight, count, pieces=8):
    depth = weight.shape[0] // 2
    smem = pl.BlockSpec(memory_space=pltpu.SMEM)
    return pl.pallas_call(
        ahead_kernel,
        in_specs=[smem, pl.BlockSpec(memory_space=pltpu.HBM)],
        out_specs=[pl.BlockSpec(memory_space=pl.ANY), smem],
        out_shape=[
            pltpu.VMEM((depth, count), weight.dtype),
            jax.ShapeDtypeStruct((1,), jnp.int32),
        ],
        scratch_shapes=[pltpu.SemaphoreType.DMA((pieces,))],
        compiler_params=pltpu.CompilerParams(vmem_limit_bytes=2 << 20),
        cost_estimate=pl.CostEstimate(
            flops=0, bytes_accessed=3 * depth * count, transcendentals=0
        ),
        name="columns_ahead",
    )(side, pltpu.with_memory_space_constraint(weight, pltpu.HBM))


def product_kernel(x_ref, w_ref, keep_ref, send_ref):
    half = keep_ref.shape[0]
    total = jnp.dot(x_ref[...], w_ref[...], preferred_element_type=F32)
    keep_ref[...] = total[:half]
    send_ref[...] = total[half:].astype(send_ref.dtype)


def product_ahead(x, w):
    rows, depth = x.shape
    count = w.shape[1]
    vmem = pl.BlockSpec(memory_space=pltpu.VMEM)
    return pl.pallas_call(
        product_kernel,
        in_specs=[vmem] * 2,
        out_specs=[vmem] * 2,
        out_shape=[jax.ShapeDtypeStruct((rows // 2, count), kind) for kind in (F32, BF16)],
        compiler_params=pltpu.CompilerParams(vmem_limit_bytes=8 << 20),
        cost_estimate=pl.CostEstimate(
            flops=2 * rows * count * depth, bytes_accessed=depth * count, transcendentals=0
        ),
        name="product_ahead",
    )(x, w)


def narrow_kernel(g_ref, u_ref, g16_ref, u16_ref):
    g16_ref[...] = g_ref[...].astype(BF16)
    u16_ref[...] = u_ref[...].astype(BF16)


def narrow(gate, up, depth):
    rows, width = gate.shape
    block = pl.BlockSpec((depth, width), lambda k: (k, 0))
    return pl.pallas_call(
        narrow_kernel,
        grid=(rows // depth,),
        in_specs=[block] * 2,
        out_specs=[block] * 2,
        out_shape=[jax.ShapeDtypeStruct(gate.shape, BF16)] * 2,
        compiler_params=pltpu.CompilerParams(vmem_limit_bytes=16 << 20),
        cost_estimate=pl.CostEstimate(flops=0, bytes_accessed=12 * rows * width, transcendentals=0),
        name="narrow",
    )(
        pltpu.with_memory_space_constraint(gate, pltpu.HBM),
        pltpu.with_memory_space_constraint(up, pltpu.HBM),
    )


def hidden_kernel(
    first, step, eug_ref, euu_ref, keep_ref, far_ref, dh_ref, bg_ref, bu_ref, d_ref, pg_ref, pu_ref,
    b_ref, sem
):
    blocks, _, pieces = sem.shape
    depth = b_ref.shape[2] // pieces

    def copies(block):
        return [
            pltpu.make_async_copy(
                ref.at[pl.ds(k * depth, depth), pl.ds(first + block * step, step)],
                b_ref.at[block, i, pl.ds(k * depth, depth)],
                sem.at[block, i, k],
            )
            for i, ref in enumerate((bg_ref, bu_ref))
            for k in range(pieces)
        ]

    running = [copies(block) for block in range(blocks)]
    for block in range(min(2, blocks)):
        for copy in running[block]:
            copy.start()
    for block in range(blocks):
        for copy in running[block]:
            copy.wait()
        if block + 2 < blocks:
            for copy in running[block + 2]:
                copy.start()
        at = pl.ds(block * step, step)
        bg = b_ref[block, 0].astype(BF16)
        bu = b_ref[block, 1].astype(BF16)
        gate = (
            keep_ref[0, :, at]
            + far_ref[0, :, at].astype(F32)
            + adapter_scale * jnp.dot(eug_ref[...], bg, preferred_element_type=F32)
        )
        up = (
            keep_ref[1, :, at]
            + far_ref[1, :, at].astype(F32)
            + adapter_scale * jnp.dot(euu_ref[...], bu, preferred_element_type=F32)
        )
        sig = jax.nn.sigmoid(gate)
        hidden_grad = dh_ref[:, at]
        dg = (hidden_grad * up * sig * (1.0 + gate * (1.0 - sig))).astype(BF16)
        du = (hidden_grad * gate * sig).astype(BF16)
        d_ref[0, :, at] = dg
        d_ref[1, :, at] = du
        if block == 0:
            pg_ref[...] = flipped_product(dg, bg)
            pu_ref[...] = flipped_product(du, bu)
        else:
            pg_ref[...] += flipped_product(dg, bg)
            pu_ref[...] += flipped_product(du, bu)


def hidden_gradients(eug, euu, b_gate, b_up, keep, far, hidden_grad, first, step, pieces=4):
    rows, wide = eug.shape
    count = keep.shape[2]
    vmem = pl.BlockSpec(memory_space=pltpu.VMEM)
    hbm = pl.BlockSpec(memory_space=pltpu.HBM)
    return pl.pallas_call(
        functools.partial(hidden_kernel, first, step),
        in_specs=[vmem] * 5 + [hbm] * 2,
        out_specs=[vmem] * 3,
        out_shape=[jax.ShapeDtypeStruct((2, rows, count), BF16)]
        + [jax.ShapeDtypeStruct((rows, wide), F32)] * 2,
        scratch_shapes=[
            pltpu.VMEM((count // step, 2, wide, step), F32),
            pltpu.SemaphoreType.DMA((count // step, 2, pieces)),
        ],
        compiler_params=pltpu.CompilerParams(vmem_limit_bytes=28 << 20),
        cost_estimate=pl.CostEstimate(
            flops=8 * rows * wide * count, bytes_accessed=12 * wide * count, transcendentals=0
        ),
        name="hidden_gradients",
    )(
        eug,
        euu,
        keep,
        far,
        hidden_grad[:, first : first + count],
        pltpu.with_memory_space_constraint(b_gate, pltpu.HBM),
        pltpu.with_memory_space_constraint(b_up, pltpu.HBM),
    )


def backward_kernel(first, side_ref, dg_ref, du_ref, wg_ref, wu_ref, keep_ref, send_ref, rows_ref, sem):
    pieces = sem.shape[1]
    total_rows = rows_ref.shape[1]
    depth = total_rows // pieces
    base = side_ref[0] * (wg_ref.shape[0] // 2) + first
    copies = {}
    for j in range(pieces):
        for i, w_ref in enumerate((wg_ref, wu_ref)):
            source = pl.ds(pl.multiple_of(base + j * depth, depth), depth)
            copies[i, j] = pltpu.make_async_copy(
                w_ref.at[source], rows_ref.at[i, pl.ds(j * depth, depth)], sem.at[i, j]
            )

    def start(j):
        if j < pieces:
            for at in ((0, j), (0, j + 1), (1, j), (1, j + 1)):
                copies[at].start()

    start(0)
    start(2)
    q = dg_ref.shape[0] // 4
    step = 2 * depth
    for k in range(0, total_rows, step):
        j = k // depth
        copies[0, j].wait()
        copies[0, j + 1].wait()
        copies[1, j].wait()
        copies[1, j + 1].wait()
        start(j + 4)
        total = flipped_product(dg_ref[...], rows_ref[0, k : k + step])
        total += flipped_product(du_ref[...], rows_ref[1, k : k + step])
        out = pl.ds(k, step)
        keep_ref[:q, out] = total[:q]
        keep_ref[q:, out] = total[2 * q : 3 * q]
        send_ref[:q, out] = total[q : 2 * q].astype(send_ref.dtype)
        send_ref[q:, out] = total[3 * q :].astype(send_ref.dtype)


def backward_products(side, dg, du, gate_weight, up_weight, first, count, depth=256):
    rows, ff = dg.shape
    vmem = pl.BlockSpec(memory_space=pltpu.VMEM)
    hbm = pl.BlockSpec(memory_space=pltpu.HBM)
    return pl.pallas_call(
        functools.partial(backward_kernel, first),
        in_specs=[pl.BlockSpec(memory_space=pltpu.SMEM), vmem, vmem, hbm, hbm],
        out_specs=[vmem] * 2,
        out_shape=[
            jax.ShapeDtypeStruct((rows // 2, count), F32),
            jax.ShapeDtypeStruct((rows // 2, count), BF16),
        ],
        scratch_shapes=[
            pltpu.VMEM((2, count, ff), BF16),
            pltpu.SemaphoreType.DMA((2, count // depth)),
        ],
        compiler_params=pltpu.CompilerParams(vmem_limit_bytes=36 << 20),
        cost_estimate=pl.CostEstimate(
            flops=4 * rows * count * ff, bytes_accessed=6 * count * ff, transcendentals=0
        ),
        name="backward_products",
    )(
        side,
        dg,
        du,
        pltpu.with_memory_space_constraint(gate_weight, pltpu.HBM),
        pltpu.with_memory_space_constraint(up_weight, pltpu.HBM),
    )


def outer_kernel(pairs, *refs):
    ins, outs, parts, sem = refs[: 2 * pairs], refs[2 * pairs : 3 * pairs], refs[-2], refs[-1]
    depth = parts.shape[1]
    copies = []
    for i in range(pairs):
        left_ref, right_ref, out_ref = ins[2 * i], ins[2 * i + 1], outs[i]
        for k in range(0, out_ref.shape[0], depth):
            at = len(copies)
            parts[at] = adapter_scale * rows_product(left_ref[:, k : k + depth], right_ref[...])
            copy = pltpu.make_async_copy(parts.at[at], out_ref.at[pl.ds(k, depth)], sem.at[at])
            copy.start()
            copies.append(copy)
    for copy in copies:
        copy.wait()


def outer_products(*pairs, depth=128):
    shapes = [(left.shape[1], right.shape[1]) for left, right in pairs]
    count = sum(rows // depth for rows, _ in shapes)
    width = shapes[0][1]
    rows = pairs[0][0].shape[0]
    return pl.pallas_call(
        functools.partial(outer_kernel, len(pairs)),
        in_specs=[pl.BlockSpec(memory_space=pltpu.VMEM)] * (2 * len(pairs)),
        out_specs=[pl.BlockSpec(memory_space=pltpu.HBM)] * len(pairs),
        out_shape=[jax.ShapeDtypeStruct(shape, F32) for shape in shapes],
        scratch_shapes=[
            pltpu.VMEM((count, depth, width), F32),
            pltpu.SemaphoreType.DMA((count,)),
        ],
        compiler_params=pltpu.CompilerParams(vmem_limit_bytes=16 << 20),
        cost_estimate=pl.CostEstimate(
            flops=2 * count * depth * width * rows,
            bytes_accessed=4 * count * depth * width,
            transcendentals=0,
        ),
        name="outer_products",
    )(*[operand for pair in pairs for operand in pair])


N = 16
CORE, X = 1, 2


def along_tensor(value, mask):
    return lax.ppermute(value, "tensor", [(i, i ^ mask) for i in range(N)])


def across_groups(value, mask=0):
    both = ("group", "tensor")
    return lax.ppermute(value, both, [(i, i ^ (N | mask)) for i in range(2 * N)])


def from_far_z(values):
    return [along_tensor(v, 4 * m) for m, v in zip((1, 2, 3), values)]


def in_order(*values):
    return lax.optimization_barrier(values)


def add_core(value, recv):
    half = value.shape[0] // 2
    return value + jnp.concatenate([recv[half:], recv[:half]], axis=0)


def add_x(value, recv):
    q = value.shape[0] // 4
    order = (1, 0, 3, 2)
    return value + jnp.concatenate([recv[o * q : (o + 1) * q] for o in order], axis=0)


def add_z(value, recv, mask):
    shape = value.shape
    v, r = (w.reshape(4, 4, 2, shape[1]) for w in (value, recv))
    return (v + jnp.stack([r[:, q ^ mask] for q in range(4)], axis=1)).reshape(shape)


def shared_device(tokens, gate_weight, up_weight, a_gate, a_up, b_gate, b_up, agent, d_hidden):
    group = lax.axis_index("group")
    t = lax.axis_index("tensor")
    side = group.astype(jnp.int32).reshape(1)
    d = tokens.shape[1]
    half = d // 2
    feat_rows = a_gate.shape[0]
    per_half = half // feat_rows
    rows = 2 * N
    ff = b_gate.shape[1]

    recv = along_tensor(tokens, 4)
    a_gate, a_up = narrow(a_gate, a_up, feat_rows // 2)
    recv, a_gate, a_up = in_order(recv, a_gate, a_up)
    line = jnp.concatenate([tokens, recv], axis=0)
    line = jnp.concatenate([line, along_tensor(line, 8)], axis=0)
    mine = lax.dynamic_slice_in_dim(line, group * half, half, 1)
    other = lax.dynamic_slice_in_dim(line, half - group * half, half, 1)
    side, mine, other = in_order(side, mine, other)
    parts = [along_tensor(mine, X), across_groups(other), across_groups(other, X)]
    cut = ff * 4 // 7
    w, side = columns_ahead(side, gate_weight, cut)
    side, *parts = in_order(side, *parts)
    x = jnp.stack(
        [jnp.concatenate([mine, parts[0]], axis=0), jnp.concatenate([parts[1], parts[2]], axis=0)]
    )
    x = jnp.concatenate([x, along_tensor(x, CORE)], axis=1).reshape(2 * rows, half)

    place = jnp.arange(rows, dtype=jnp.int32)
    block = ((place >> 1) & 3) * 4 + ((place >> 3) & 1) * 2 + (place >> 4)
    token_of = ((t ^ block) << 1) + (place & 1)
    shuffle = token_of[:, None] == jnp.arange(rows, dtype=jnp.int32)[None, :]
    agent_here = jnp.sum(jnp.where(shuffle, agent[None, :], 0), axis=1)
    chosen = agent_here[:, None] == (jnp.arange(AG * R, dtype=jnp.int32) // R)[None, :]
    hidden_grad = jnp.dot(shuffle.astype(BF16), d_hidden, preferred_element_type=F32)

    def select(values):
        kept = jnp.where(chosen, values, 0.0)
        pair = sum(kept[:, c : c + 2 * R] for c in range(0, AG * R, 2 * R))
        return pair[:, :R] + pair[:, R:]

    def spread(small):
        wide = jnp.concatenate([small] * AG, axis=1)
        return jnp.where(chosen, wide, 0.0).astype(BF16)

    blocks = lax.dynamic_slice_in_dim(x, (t % per_half) * feat_rows, feat_rows, 1)
    swapped = across_groups(blocks[rows:])
    def forward(weight, late):
        first, count = (cut, ff - cut) if late else (0, cut)
        return forward_products(side, x, weight, first, count)

    keep_0, send_0 = product_ahead(x, w)
    swapped, x, keep_0, send_0 = in_order(swapped, x, keep_0, send_0)
    own_cols = jnp.where(t // per_half == group, blocks[:rows], swapped)
    part = jnp.concatenate(
        [
            select(jnp.dot(own_cols, a_gate, preferred_element_type=F32)),
            select(jnp.dot(own_cols, a_up, preferred_element_type=F32)),
        ],
        axis=1,
    )

    part = add_core(part, along_tensor(part, CORE))
    part, x = in_order(part, x)
    recv = along_tensor(part, X)
    keep_1, send_1 = forward(up_weight, False)
    recv, x, keep_1, send_1 = in_order(recv, x, keep_1, send_1)
    part = add_x(part, recv)

    recv = along_tensor(part, 4)
    far_a = across_groups(jnp.stack([send_0, send_1]))
    keep_2, send_2 = forward(gate_weight, True)
    recv, far_a, x, keep_2, send_2 = in_order(recv, far_a, x, keep_2, send_2)
    part = add_z(part, recv, 1)

    recv = along_tensor(part, 8)
    keep_3, send_3 = forward(up_weight, True)
    recv, keep_3, send_3 = in_order(recv, keep_3, send_3)
    far_b = across_groups(jnp.stack([send_2, send_3]))
    part = add_z(part, recv, 2)
    u = part.astype(BF16).astype(F32)
    up_factor_gate = spread(u[:, :R])
    up_factor_up = spread(u[:, R:])

    def hidden(keep, far, first, width):
        return hidden_gradients(
            up_factor_gate, up_factor_up, b_gate, b_up, keep, far, hidden_grad, first, width
        )

    own_a, pg_a, pu_a = hidden(jnp.stack([keep_0, keep_1]), far_a, 0, 512)
    far_b, own_a = in_order(far_b, own_a)
    own_b, pg_b, pu_b = hidden(jnp.stack([keep_2, keep_3]), far_b, cut, 256)
    own = jnp.concatenate([own_a, own_b], axis=2)
    far = across_groups(own)
    part = jnp.concatenate([select(pg_a + pg_b), select(pu_a + pu_b)], axis=1)
    part, own = in_order(part, own)
    recv = along_tensor(part, CORE)
    (gate_lift_gradient,) = outer_products((up_factor_gate, own[0]))
    far, recv, gate_lift_gradient = in_order(far, recv, gate_lift_gradient)
    part = add_core(part, recv)
    both = jnp.concatenate([own, far], axis=1)
    dg, du = both[0], both[1]

    count = half // 8

    def backward(c, n):
        return backward_products(side, dg, du, gate_weight, up_weight, c * count, n * count)

    recv = along_tensor(part, X)
    keep_0, send_0 = backward(0, 1)
    recv, dg, du, keep_0, send_0 = in_order(recv, dg, du, keep_0, send_0)
    part = add_x(part, recv)

    recv = along_tensor(part, 4)
    keep_1, send_1 = backward(1, 1)
    recv, dg, du, keep_1, send_1 = in_order(recv, dg, du, keep_1, send_1)
    part = add_z(part, recv, 1)

    recv = along_tensor(part, 8)
    keep_2, send_2 = backward(2, 6)
    recv, keep_2, send_2, own, own_cols = in_order(recv, keep_2, send_2, own, own_cols)
    part = add_z(part, recv, 2)
    far = along_tensor(jnp.concatenate([send_0, send_1, send_2], axis=1), CORE)
    g = part.astype(BF16).astype(F32)
    gate_factor_gate = spread(g[:, :R])
    gate_factor_up = spread(g[:, R:])
    moved = (
        adapter_scale
        * (
            flipped_product(gate_factor_gate, a_gate)
            + flipped_product(gate_factor_up, a_up)
        )
    ).astype(BF16)

    far_moved = along_tensor(moved[16:], CORE)
    far, far_moved, own = in_order(far, far_moved, own)
    sums = jnp.concatenate([keep_0, keep_1, keep_2], axis=1) + far.astype(F32)
    moved = jnp.concatenate([moved[:16], far_moved], axis=1)

    low = sums.astype(BF16)
    parts = [
        along_tensor(jnp.concatenate([low[8:16], moved[8:]], axis=1), X),
        across_groups(low[16:24]),
        across_groups(low[24:], X),
    ]
    (up_lift_gradient,) = outer_products((up_factor_up, own[1]))
    up_lift_gradient, own_cols, *parts = in_order(up_lift_gradient, own_cols, *parts)
    near = sums[:8] + parts[0][:, :half].astype(F32)
    sums = jnp.concatenate([near, parts[1].astype(F32) + parts[2].astype(F32)], axis=1)
    moved = jnp.concatenate([moved[:8], parts[0][:, half:]], axis=1)

    low = jnp.concatenate([sums.astype(BF16), moved], axis=1)
    parts = from_far_z([low[2 * m : 2 * m + 2] for m in (1, 2, 3)])
    gate_down_gradient, up_down_gradient = outer_products(
        (own_cols, gate_factor_gate), (own_cols, gate_factor_up)
    )
    gate_down_gradient, up_down_gradient, *parts = in_order(
        gate_down_gradient, up_down_gradient, *parts
    )
    sums = sums[:2] + sum(p[:, :d].astype(F32) for p in parts)
    moved = jnp.stack([moved[:2]] + [p[:, d:] for p in parts])
    moved = moved.reshape(4, 2, 2, 2, feat_rows).transpose(0, 2, 3, 1, 4).reshape(N, 2 * feat_rows)
    source = jnp.arange(N, dtype=jnp.int32)
    sort = (source[:, None] == (t ^ source)[None, :]).astype(BF16)
    sorted_rows = jnp.dot(sort, moved, preferred_element_type=F32).reshape(N, 2, feat_rows)
    contribution = sorted_rows.transpose(1, 0, 2).reshape(2, d)
    near, far = sums[:, :half], sums[:, half:]
    sums = jnp.where(
        group == 0, jnp.concatenate([near, far], axis=1), jnp.concatenate([far, near], axis=1)
    )
    token_gradient = (sums + contribution).astype(BF16)
    return (
        token_gradient,
        gate_down_gradient,
        up_down_gradient,
        gate_lift_gradient,
        up_lift_gradient,
    )


def solution(mesh):
    sizes = dict(mesh.shape)

    def per_device(*args):
        tokens, b_gate = args[0], args[5]
        fits = (
            sizes["group"] == 2
            and sizes["tensor"] == N
            and tokens.shape[0] == 2
            and b_gate.shape[1] % 1792 == 0
            and tokens.shape[1] % 4096 == 0
        )
        return (shared_device if fits else plain_device)(*args)

    in_specs = (
        P(("group", "tensor"), None),
        P(None, "tensor"),
        P(None, "tensor"),
        P(("group", "tensor"), None),
        P(("group", "tensor"), None),
        P("group", "tensor"),
        P("group", "tensor"),
        P("group"),
        P("group", "tensor"),
    )
    out_specs = (
        P(("group", "tensor"), None),
        P(("group", "tensor"), None),
        P(("group", "tensor"), None),
        P("group", "tensor"),
        P("group", "tensor"),
    )
    return jax.shard_map(
        per_device, mesh=mesh, in_specs=in_specs, out_specs=out_specs, check_vma=False
    )
```
